32 devices in a mesh: dp: 8 (over z, x), tensor: 4 (over y, core).
Axes of the slice: x: 2, y: 2, z: 4, core: 2. Of those that a mesh axis runs over, the one named last changes fastest.
Arguments:
- tokens: bfloat16 [16384, 1024], P(('dp', 'tensor')), may hold values from -6 to 6
- lengths: int32 [16], P('dp'), may hold values from 256 to 1024, as said below
- routes: int32 [16384, 8], P('dp'), may hold values from 0 to 31, all different within a row; in each aligned block of 512 rows (0 to 511, 512 to 1023, ...) at most 136 rows name the same one
- gain_attn: float32 [1024], replicated, may hold values from 0.5 to 1.5
- w_query: bfloat16 [1024, 1024], P('dp', 'tensor'), may hold values from -0.1875 to 0.1875
- w_keyvalue: bfloat16 [1024, 2, 512], P('dp', None, 'tensor'), may hold values from -0.1875 to 0.1875
- w_out: bfloat16 [1024, 1024], P('dp', 'tensor'), may hold values from -3 to 3
- gain_mixer: float32 [1024], replicated, may hold values from 0.5 to 1.5
- w_router: bfloat16 [1024, 32], replicated, may hold values from -0.09375 to 0.09375
- w_gate: bfloat16 [1024, 32, 512], P('dp', None, 'tensor'), may hold values from -0.1875 to 0.1875
- w_up: bfloat16 [1024, 32, 512], P('dp', None, 'tensor'), may hold values from -0.1875 to 0.1875
- w_down: bfloat16 [1024, 32, 512], P('dp', None, 'tensor'), may hold values from -1 to 1
- out_grad: bfloat16 [16384, 1024], P(('dp', 'tensor')), may hold values from -6 to 6
Outputs:
- mixed: bfloat16 [16384, 1024], P(('dp', 'tensor'))
- grad_tokens: bfloat16 [16384, 1024], P(('dp', 'tensor'))
- grad_gain_attn: float32 [1024], replicated
- grad_w_query: float32 [1024, 1024], P('dp', 'tensor')
- grad_w_keyvalue: float32 [1024, 2, 512], P('dp', None, 'tensor')
- grad_w_out: float32 [1024, 1024], P('dp', 'tensor')
- grad_gain_mixer: float32 [1024], replicated
- grad_w_router: float32 [1024, 32], replicated
- grad_w_gate: float32 [1024, 32, 512], P('dp', None, 'tensor')
- grad_w_up: float32 [1024, 32, 512], P('dp', None, 'tensor')
- grad_w_down: float32 [1024, 32, 512], P('dp', None, 'tensor')
The draws below stay inside these ranges and needn't reach their ends.
Inputs may be any that keep to these rules, and one draw needn't show every extreme that they name: `lengths`: every sequence has at least 256 live tokens; in every draw some sequence is full and some has exactly 256. `routes`: each row names 8 different experts; within each aligned block of 512 rows (the token slots of one device) no expert is named by more than 136 rows, and in every draw some expert reaches 136 in some block.
All inputs are finite; a program needn't handle non-finite values.
Results may differ from the reference program's by a relative error of at most 0.023.
Values may be sent and summed in bfloat16 or wider, within the bound.
A program may use at most 576 MiB of HBM per device.

```python
import math
import jax
import jax.numpy as jnp
import numpy as np
from jax import lax

D = 1024
QH = 16
KVH = 8
HD = 64
FF = 512
EXPERTS = 32
TOPK = 8
SEQ_LEN = 1024
MIN_LEN = 256
SEQS = 2
SEQUENCES = 16
TOKENS = 16384
TOK_DEV = 512
CAP = 136


def draw_lengths(key, part):
    key_values, key_full, key_short = jax.random.split(key, 3)
    values = jax.random.randint(key_values, (SEQUENCES,), MIN_LEN, SEQ_LEN + 1)
    full_at = jax.random.randint(key_full, (), 0, SEQUENCES)
    short_at = (full_at + 1 + jax.random.randint(key_short, (), 0, SEQUENCES - 1)) % SEQUENCES
    values = values.at[full_at].set(SEQ_LEN)
    values = values.at[short_at].set(MIN_LEN)
    return values.astype(jnp.int32)


def block_scale(rng, shape, cuts, low, top_value):
    level = 1.0
    for position, shards_of in cuts:
        steps = jax.random.uniform(jax.random.fold_in(jax.random.fold_in(rng, 6), position), (shards_of,), jnp.float32, low / len(cuts), top_value / len(cuts))
        level = level * jnp.repeat(jnp.exp(steps), shape[position] // shards_of).reshape((-1,) + (1,) * (len(shape) - 1 - position))
    return level


def assign_block(key, own, number, rows, number_of, top, limit, skew):
    sequence = jax.random.permutation(key, number_of)
    packed, ordinary = shares(number_of, rows * top, limit, skew, True), shares(number_of, rows * top, limit, skew, False)
    places = jnp.arange(number_of)

    def named(sizes, turn):
        used = int((sizes > 0).sum())
        fixed = max(1, used // 4)
        shifted = fixed + (places - fixed + turn * (used - fixed)) % max(1, number_of - fixed)
        return jnp.zeros((number_of,), jnp.int32).at[sequence[jnp.where(places < fixed, places, shifted)]].set(jnp.asarray(sizes, jnp.int32))

    sizes = jnp.where(number % 4 == 0, named(packed, number // 4), named(ordinary, number - number // 4 - 1))
    mixed = jax.random.permutation(jax.random.fold_in(own, 3), number_of)
    donor, receiver = mixed[0:number_of // 2 * 2:2], mixed[1:number_of // 2 * 2:2]
    slack = jnp.minimum(sizes[donor] - 1, limit - sizes[receiver]) // 2
    slack = jnp.where((donor == sequence[0]) | (receiver == sequence[0]) | (sizes[receiver] == 0), 0, jnp.maximum(slack, 0))
    shifted = jax.random.randint(jax.random.fold_in(own, 4), (number_of // 2,), 0, 1 << 20) % (slack + 1)
    sizes = sizes.at[donor].add(-shifted).at[receiver].add(shifted)
    members = jnp.searchsorted(jnp.cumsum(sizes), jnp.arange(rows * top), side="right").astype(jnp.int32)
    listing = members.reshape(top, rows).T
    listing = listing[jax.random.permutation(jax.random.fold_in(own, 1), rows)]
    turn = jax.random.randint(jax.random.fold_in(own, 2), (rows, 1), 0, top)
    return jnp.take_along_axis(listing, (jnp.arange(top)[None, :] + turn) % top, axis=1)


def shares(count, total, limit, lean, full):
    portions = [(1 << 20) // math.isqrt(rank ** lean) + 1 for rank in range(1, count + 1)]
    largest = limit if full else min(limit, max(-(-total // count), total * portions[0] // sum(portions)))
    least = 1 if total - largest >= count - 1 else 0
    holding, surplus = [largest] + [least] * (count - 1), total - largest - least * (count - 1)
    while surplus > 0:
        candidates = [i for i in range(1, count) if holding[i] < largest] or [i for i in range(1, count) if holding[i] < limit]
        whole, budget = sum([portions[i] for i in candidates]), surplus
        for i in candidates:
            extra = min(limit - holding[i], max(1, budget * portions[i] // whole), surplus)
            holding[i] = holding[i] + extra
            surplus = surplus - extra
    return np.array(holding)


def scatter_about(key, dims, spread, most, pieces=(), held_as=jnp.bfloat16):
    array = jax.random.normal(key, dims, jnp.float32) * spread
    if len(pieces) > 0:
        array = block_scale(key, dims, pieces, -0.22, 0.18) * array
    return jnp.clip(array, min=-most, max=most).astype(held_as)


def setup_inputs(seed: int = 0) -> dict:
    splits = jax.random.split(jax.random.key(seed), 14)
    tokens = scatter_about(splits[0], (TOKENS, D), 1.0, 6.0, ((0, 32),))
    lengths = draw_lengths(jax.random.fold_in(splits[13], 71), 0)
    routes_keys = jax.random.split(jax.random.fold_in(splits[2], 1), TOKENS // TOK_DEV)
    routes_turns = jax.random.permutation(jax.random.fold_in(splits[2], 3), TOKENS // TOK_DEV)
    routes = jax.vmap(lambda own, number: assign_block(jax.random.fold_in(splits[2], 2), own, number, TOK_DEV, EXPERTS, TOPK, CAP, 1))(routes_keys, routes_turns).reshape((TOKENS, TOPK))
    gain_attn = jnp.clip(1.0 + 0.1 * jax.random.normal(splits[3], (D,), jnp.float32), 0.5, 1.5)
    w_query = scatter_about(splits[4], (D, QH * HD), D ** -0.5, 0.1875, ((0, 8), (1, 4)))
    w_keyvalue = scatter_about(splits[5], (D, 2, KVH * HD), D ** -0.5, 0.1875, ((0, 8), (2, 4)))
    w_out = scatter_about(splits[6], (D, QH * HD), (max(QH * HD * 4 // SEQ_LEN, 1)) ** -0.5, 3.0, ((0, 8), (1, 4)))
    gain_mixer = jnp.clip(1.0 + 0.1 * jax.random.normal(splits[7], (D,), jnp.float32), 0.5, 1.5)
    w_router = scatter_about(splits[8], (D, EXPERTS), (4 * D) ** -0.5, 0.09375)
    w_gate = scatter_about(splits[9], (D, EXPERTS, FF), D ** -0.5, 0.1875, ((0, 8), (2, 4)))
    w_up = scatter_about(splits[10], (D, EXPERTS, FF), D ** -0.5, 0.1875, ((0, 8), (2, 4)))
    w_down = scatter_about(splits[11], (D, EXPERTS, FF), (FF // 16) ** -0.5, 1.0, ((0, 8), (2, 4)))
    out_grad = scatter_about(splits[12], (TOKENS, D), 1.0, 6.0, ((0, 32),))
    return dict(tokens=tokens, lengths=lengths, routes=routes, gain_attn=gain_attn, w_query=w_query, w_keyvalue=w_keyvalue, w_out=w_out, gain_mixer=gain_mixer, w_router=w_router, w_gate=w_gate, w_up=w_up, w_down=w_down, out_grad=out_grad)


epsilon = 1e-06
rope_base = 10000.0
highest = lax.Precision.HIGHEST

@jax.custom_vjp
def low(v):
    return lax.optimization_barrier(v.astype(jnp.bfloat16)).astype(jnp.float32)

@jax.custom_vjp
def low_back(v):
    return v

def low_keep(v):
    return (low(v), None)

def low_pass(kept, grad):
    return (grad,)

def back_keep(v):
    return (v, None)

def back_low(kept, grad):
    return (low(grad),)
low.defvjp(low_keep, low_pass)
low_back.defvjp(back_keep, back_low)

def rotary_tables(positions, head_size):
    half_size = head_size // 2
    exponent = 2.0 * jnp.arange(half_size, dtype=jnp.float32) / head_size
    frequency = jnp.exp(-math.log(rope_base) * exponent)
    angles = positions.astype(jnp.float32)[:, None] * frequency[None, :]
    return (jnp.cos(angles), jnp.sin(angles))

def rotate(vectors, cosine_table, sine_table):
    half_size = vectors.shape[-1] // 2
    first_half = vectors[..., :half_size]
    second_half = vectors[..., half_size:]
    cos_rows = cosine_table[:, None, :]
    sin_rows = sine_table[:, None, :]
    return jnp.concatenate([first_half * cos_rows - second_half * sin_rows, second_half * cos_rows + first_half * sin_rows], axis=-1)

def sequence_attention(operands):
    query_seq, keys_seq, values_seq, seq_length = operands
    seq_len = query_seq.shape[0]
    block_len = min(512, seq_len)
    key_pos = jnp.arange(seq_len, dtype=jnp.int32)
    outputs = []
    for block_id in range(seq_len // block_len):
        block_start = block_id * block_len
        query_blk = query_seq[block_start:block_start + block_len]
        raw_scores = jnp.einsum('qgrd,kgd->grqk', query_blk, keys_seq, precision=highest)
        query_pos = block_start + jnp.arange(block_len, dtype=jnp.int32)
        allowed = (key_pos[None, :] <= query_pos[:, None]) & (key_pos[None, :] < seq_length)
        scores = jnp.where(allowed[None, None], low_back(raw_scores) * (1.0 / math.sqrt(HD)), -1e+30)
        attn_weights = low(jax.nn.softmax(scores, axis=-1))
        outputs.append(jnp.einsum('grqk,kgd->qgrd', attn_weights, values_seq, precision=highest))
    return jnp.concatenate(outputs, axis=0)

def layer_forward(tokens_f, gain_attn, w_query, w_keyvalue, w_out, gain_mixer, w_router, w_gate, w_up, w_down, routes_grp, lengths_grp):
    group_rows = tokens_f.shape[0]
    seq_count = lengths_grp.shape[0]
    seq_len = group_rows // seq_count
    rows_all = jnp.arange(group_rows, dtype=jnp.int32)
    positions = rows_all % seq_len
    seq_ids = rows_all // seq_len
    row_length = lax.optimization_barrier(jnp.sum(jnp.where(seq_ids[:, None] == jnp.arange(seq_count, dtype=jnp.int32)[None, :], lengths_grp[None, :], 0), axis=1))
    live = (positions < row_length).astype(jnp.float32)
    inverse_attn = lax.rsqrt(lax.optimization_barrier(jnp.mean(tokens_f * tokens_f, axis=1, keepdims=True)) + epsilon)
    normed_attn = low(tokens_f * inverse_attn * gain_attn[None, :])
    query_pre = low_back(jnp.dot(normed_attn, w_query, precision=highest))
    keyval_pre = low_back(jnp.einsum('rd,dsk->rsk', normed_attn, w_keyvalue, precision=highest))
    cosine_table, sine_table = rotary_tables(positions, HD)
    query_rot = low(rotate(query_pre.reshape(group_rows, QH, HD), cosine_table, sine_table))
    keys_rot = low(rotate(keyval_pre[:, 0].reshape(group_rows, KVH, HD), cosine_table, sine_table))
    values_rows = low(keyval_pre[:, 1].reshape(group_rows, KVH, HD))
    repeat_count = QH // KVH
    query_seqs = query_rot.reshape(seq_count, seq_len, KVH, repeat_count, HD)
    keys_seqs = keys_rot.reshape(seq_count, seq_len, KVH, HD)
    values_seqs = values_rows.reshape(seq_count, seq_len, KVH, HD)
    context_seqs = lax.map(jax.checkpoint(sequence_attention), (query_seqs, keys_seqs, values_seqs, lengths_grp))
    context_rows = low(low_back(context_seqs.reshape(group_rows, QH * HD)))
    attn_branch = low_back(live[:, None] * jnp.einsum('rh,dh->rd', context_rows, w_out, precision=highest))
    hidden = tokens_f + attn_branch
    inverse_mix = lax.rsqrt(lax.optimization_barrier(jnp.mean(hidden * hidden, axis=1, keepdims=True)) + epsilon)
    normed_mix = low(hidden * inverse_mix * gain_mixer[None, :])
    logits = jnp.dot(normed_mix, w_router, precision=highest)
    picks = (routes_grp[:, :, None] == jnp.arange(EXPERTS, dtype=jnp.int32)[None, None, :]).astype(jnp.float32)
    chosen = lax.optimization_barrier(jnp.sum(picks * logits[:, None, :], axis=2))
    gates = jax.nn.softmax(chosen, axis=1) * live[:, None]
    mixing = lax.optimization_barrier(jnp.sum(picks * gates[:, :, None], axis=1))

    def expert_term(total, operands):
        gate_one, up_one, down_one, mix_one = operands
        gate_lin = low_back(jnp.dot(normed_mix, gate_one, precision=highest))
        up_lin = low_back(jnp.dot(normed_mix, up_one, precision=highest))
        scaled_hidden = low(mix_one[:, None] * jax.nn.silu(gate_lin) * up_lin)
        return (total + jnp.einsum('rf,df->rd', scaled_hidden, down_one, precision=highest), None)
    expert_inputs = (jnp.moveaxis(w_gate, 1, 0), jnp.moveaxis(w_up, 1, 0), jnp.moveaxis(w_down, 1, 0), jnp.transpose(mixing))
    moe_total = lax.scan(jax.checkpoint(expert_term), jnp.zeros(hidden.shape, jnp.float32), expert_inputs)[0]
    return hidden + moe_total

def reference(tokens, lengths, routes, gain_attn, w_query, w_keyvalue, w_out, gain_mixer, w_router, w_gate, w_up, w_down, out_grad):
    group_rows = SEQS * SEQ_LEN
    groups = TOKENS // group_rows
    weights = tuple((item.astype(jnp.float32) for item in (gain_attn, w_query, w_keyvalue, w_out, gain_mixer, w_router, w_gate, w_up, w_down)))

    def per_group(totals, operands):
        tok_grp, len_grp, route_grp, grad_grp = operands

        def forward(tok_f, *params):
            return layer_forward(tok_f, *params, route_grp, len_grp)
        mixed_grp, pullback = jax.vjp(forward, tok_grp.astype(jnp.float32), *weights)
        grads_all = pullback(grad_grp.astype(jnp.float32))
        totals = tuple((left + right for left, right in zip(totals, grads_all[1:])))
        return (totals, (mixed_grp.astype(jnp.bfloat16), grads_all[0].astype(jnp.bfloat16)))
    start_totals = tuple((jnp.zeros(item.shape, jnp.float32) for item in weights))
    scan_inputs = (tokens.reshape(groups, group_rows, D), lengths.reshape(groups, SEQS), routes.reshape(groups, group_rows, TOPK), out_grad.reshape(groups, group_rows, D))
    totals, (mixed, grad_tokens) = lax.scan(per_group, start_totals, scan_inputs)
    return (mixed.reshape(TOKENS, D), grad_tokens.reshape(TOKENS, D), totals[0], totals[1], totals[2], totals[3], totals[4], totals[5], totals[6], totals[7], totals[8])
```

```python
import functools
import math

import jax
import jax.numpy as jnp
from jax import lax
from jax.experimental import pallas as pl
from jax.experimental.pallas import tpu as pltpu
from jax.sharding import PartitionSpec as P

HD = 64
LANES = 128
epsilon = 1e-06
rope_base = 10000.0
bf16 = jnp.bfloat16
f32 = jnp.float32
BOTH = ("dp", "tensor")
VMEM_LIMIT = 60 * 1024 * 1024
QBLK = 256


def dot(a, b, ca, cb):
    return lax.dot_general(a, b, (((ca,), (cb,)), ((), ())), preferred_element_type=f32)


def call(kernel, out_shape, flops, nbytes, **kw):
    return pl.pallas_call(
        kernel,
        out_shape=out_shape,
        compiler_params=pltpu.CompilerParams(vmem_limit_bytes=VMEM_LIMIT),
        cost_estimate=pl.CostEstimate(flops=flops, bytes_accessed=nbytes, transcendentals=0),
        **kw,
    )


def sds(shape, dtype):
    return jax.ShapeDtypeStruct(shape, dtype)


VM = pl.BlockSpec(memory_space=pltpu.VMEM)
SM = pl.BlockSpec(memory_space=pltpu.SMEM)


def hop(x, dp_bit, t_bits):
    nd, nt = lax.axis_size("dp"), lax.axis_size("tensor")
    pairs = [
        (d * nt + t, (d ^ dp_bit) * nt + (t ^ t_bits)) for d in range(nd) for t in range(nt)
    ]
    return lax.ppermute(x, BOTH, pairs)


def hop_c(x):
    return hop(x, 0, 1)


def hop_y(x):
    return hop(x, 0, 2)


def hop_x(x):
    return hop(x, 1, 0)


def gather_plane(x):
    half = x.shape[0] // 2
    from_y, from_x = hop_y(x), hop_x(x)
    diag_a, diag_b = hop_x(from_y[:half]), hop_y(from_x[half:])
    near = (x, from_y, from_x, diag_a, diag_b)
    far = tuple(hop_c(item) for item in near)
    return near + far


def add16(a, b):
    return (a.astype(f32) + b.astype(f32)).astype(bf16)


def scatter_plane(send, keep):
    total = add16(keep, hop_c(send))
    half = total.shape[1] // 2
    x_a, y_b = total[2, :half], total[1, half:]
    got_xa, got_yb = hop_x(x_a), hop_y(y_b)
    got_da, got_db = hop_x(total[3, :half]), hop_y(total[3, half:])
    got_ya = hop_y(add16(total[1, :half], got_da))
    got_xb = hop_x(add16(total[2, half:], got_db))
    return total[0], jnp.concatenate([got_xa, got_xb]), jnp.concatenate([got_ya, got_yb])


def swap_halves(v):
    lane = lax.broadcasted_iota(jnp.int32, v.shape, 1)
    left = pltpu.roll(v, LANES - HD // 2, 1)
    right = pltpu.roll(v, HD // 2, 1)
    return jnp.where(lane % HD < HD // 2, left, right)


def in_head(tile, h):
    lane = lax.broadcasted_iota(jnp.int32, tile.shape, 1)
    return (lane < HD) if h == 0 else (lane >= HD)


def only_head(tile, h):
    return jnp.where(in_head(tile, h), tile, jnp.zeros_like(tile))


def spread_head(tile, h):
    wide = tile.astype(f32)
    return jnp.where(in_head(wide, h), wide, pltpu.roll(wide, HD, 1)).astype(tile.dtype)


def stacked(tile):
    return jnp.concatenate([only_head(tile, 0), only_head(tile, 1)], axis=0)


def key_limit(start, rows, length):
    column = lax.broadcasted_iota(jnp.int32, (1, 2 * rows), 1)
    position = start + jnp.where(column >= rows, column - rows, column)
    return jnp.minimum(position, length - 1)


def scores_t(kd, qm, limit):
    raw = dot(kd, qm, 1, 1) * (1.0 / math.sqrt(HD))
    key = lax.broadcasted_iota(jnp.int32, raw.shape, 0)
    return jnp.where(key <= limit, raw, -1e30)


def attend_kernel(
    where_ref, own, peer, w, wo, cos, sin,
    q_ref, k_ref, v_ref, ctx_ref, lse_ref, keep_ref, send_ref,
    rows_ref,
):
    core, length = where_ref[0], where_ref[1]
    half = own.shape[0]
    seq = 2 * half
    qw, kw = q_ref.shape[1], k_ref.shape[1]
    rows_ref[pl.ds(pl.multiple_of(core * half, half), half)] = own[...]
    rows_ref[pl.ds(pl.multiple_of((1 - core) * half, half), half)] = peer[...]
    for blk in range(seq // QBLK):
        sl = slice(blk * QBLK, (blk + 1) * QBLK)
        pre = dot(rows_ref[sl], w[...], 1, 0)
        c, s = cos[sl], sin[sl]
        for tile in range((qw + kw) // LANES):
            col = pre[:, tile * LANES:(tile + 1) * LANES]
            turned = (col * c + swap_halves(col) * s).astype(bf16)
            if tile * LANES < qw:
                q_ref[sl, tile * LANES:(tile + 1) * LANES] = turned
            else:
                at = tile * LANES - qw
                k_ref[sl, at:at + LANES] = turned
        v_ref[sl] = pre[:, qw + kw:].astype(bf16)
    for g in range(qw // LANES):
        kv = slice(g // 2 * LANES, (g // 2 + 1) * LANES)
        cols = slice(g * LANES, (g + 1) * LANES)
        kd = spread_head(k_ref[:, kv], g % 2)
        vd_t = spread_head(v_ref[:, kv], g % 2).T
        for blk in range(seq // QBLK):
            top = (blk + 1) * QBLK
            sl = slice(blk * QBLK, top)
            s = scores_t(kd[:top], stacked(q_ref[sl, cols]), key_limit(blk * QBLK, QBLK, length))
            peak = jnp.max(s, axis=0, keepdims=True)
            e = jnp.exp(s - peak)
            total = jnp.sum(e, axis=0, keepdims=True)
            p = (e * (1.0 / total)).astype(bf16)
            ctx = dot(vd_t[:, :top], p, 1, 0).T
            tile = jnp.where(in_head(ctx[:QBLK], 0), ctx[:QBLK], ctx[QBLK:])
            ctx_ref[sl, cols] = tile.astype(bf16)
            lse = peak + jnp.log(total)
            lse_ref[2 * g:2 * g + 1, sl] = lse[:, :QBLK]
            lse_ref[2 * g + 1:2 * g + 2, sl] = lse[:, QBLK:]
    mine = ctx_ref[pl.ds(pl.multiple_of(core * half, half), half)]
    other = ctx_ref[pl.ds(pl.multiple_of((1 - core) * half, half), half)]
    send_ref[...] = dot(other, wo[...], 1, 1).astype(bf16)
    keep_ref[...] = dot(mine, wo[...], 1, 1).astype(bf16)


def attend_back_kernel(
    where_ref, own, peer, gb_own, gb_peer, w, wo, cos, sin, q_ref, k_ref, v_ref, ctx_ref, lse_ref,
    dw_ref, dwo_ref, keep_ref, send_ref,
    rows_ref, gb_ref, gc_ref, dqkv_ref, dk_ref, dv_ref,
):
    core, length = where_ref[0], where_ref[1]
    half = own.shape[0]
    seq = 2 * half
    qw, kw = q_ref.shape[1], k_ref.shape[1]
    at_own = pl.ds(pl.multiple_of(core * half, half), half)
    at_peer = pl.ds(pl.multiple_of((1 - core) * half, half), half)
    rows_ref[at_own] = own[...]
    rows_ref[at_peer] = peer[...]
    gb_ref[at_own] = gb_own[...]
    gb_ref[at_peer] = gb_peer[...]
    gc_ref[...] = dot(gb_ref[...], wo[...], 1, 0).astype(bf16)
    dwo_ref[...] = dot(gb_ref[...], ctx_ref[...], 0, 0).astype(bf16)
    scale = 1.0 / math.sqrt(HD)
    folded = {}
    for g in range(qw // LANES):
        kv = slice(g // 2 * LANES, (g // 2 + 1) * LANES)
        cols = slice(g * LANES, (g + 1) * LANES)
        kd = spread_head(k_ref[:, kv], g % 2)
        kd_t = kd.T
        vd = spread_head(v_ref[:, kv], g % 2)
        for blk in reversed(range(seq // QBLK)):
            top = (blk + 1) * QBLK
            sl = slice(blk * QBLK, top)
            qm = stacked(q_ref[sl, cols])
            gm = stacked(gc_ref[sl, cols])
            s = scores_t(kd[:top], qm, key_limit(blk * QBLK, QBLK, length))
            lse = jnp.concatenate([lse_ref[2 * g:2 * g + 1, sl], lse_ref[2 * g + 1:2 * g + 2, sl]], axis=1)
            p = jnp.exp(s - lse)
            gw = dot(vd[:top], gm, 1, 1)
            centre = jnp.sum(p * gw, axis=0, keepdims=True)
            ds = (p * (gw - centre) * scale).astype(bf16)
            dv = dot(p.astype(bf16), gm, 1, 0)
            dk = dot(ds, qm, 1, 0)
            dq = dot(kd_t[:, :top], ds, 1, 0).T
            if top == seq:
                dk_ref[...] = dk
                dv_ref[...] = dv
            else:
                dk_ref[:top] += dk
                dv_ref[:top] += dv
            tile = jnp.where(in_head(dq[:QBLK], 0), dq[:QBLK], dq[QBLK:])
            back = tile * cos[sl] - swap_halves(tile) * sin[sl]
            dqkv_ref[sl, cols] = back.astype(bf16)
        dk_all = dk_ref[...] + pltpu.roll(dk_ref[...], HD, 1)
        dv_all = dv_ref[...] + pltpu.roll(dv_ref[...], HD, 1)
        if g % 2 == 0:
            folded = (dk_all, dv_all)
        else:
            dk_pair = jnp.where(in_head(dk_all, 0), folded[0], dk_all)
            dv_pair = jnp.where(in_head(dv_all, 0), folded[1], dv_all)
            at = qw + g // 2 * LANES
            back = dk_pair * cos[...] - swap_halves(dk_pair) * sin[...]
            dqkv_ref[:, at:at + LANES] = back.astype(bf16)
            dqkv_ref[:, at + kw:at + kw + LANES] = dv_pair.astype(bf16)
    send_ref[...] = dot(dqkv_ref[at_peer], w[...], 1, 1).astype(bf16)
    keep_ref[...] = dot(dqkv_ref[at_own], w[...], 1, 1).astype(bf16)
    dw_ref[...] = dot(rows_ref[...], dqkv_ref[...], 0, 0).astype(bf16)


def mix_norm_kernel(tokens, keep, got, live, gain, hidden_ref, normed_ref, inv_ref):
    branch = keep[...].astype(f32) + got[...].astype(f32)
    hidden = tokens[...].astype(f32) + live[...] * branch
    inverse = lax.rsqrt(jnp.mean(hidden * hidden, axis=1, keepdims=True) + epsilon)
    hidden_ref[...] = hidden
    inv_ref[...] = inverse
    normed_ref[...] = (hidden * inverse * gain[...]).astype(bf16)


def masked_shares(logits, hit, axis):
    peak = jnp.max(jnp.where(hit, logits, -1e30), axis=axis, keepdims=True)
    e = jnp.where(hit, jnp.exp(jnp.where(hit, logits - peak, 0.0)), 0.0)
    total = jnp.sum(e, axis=axis, keepdims=True)
    return e / jnp.where(total > 0.0, total, 1.0)


def split16(v):
    high = v.astype(bf16)
    return high, (v - high.astype(f32)).astype(bf16)


def mix_back_kernel(
    normed, hidden_in, inv, part_a, part_b, part_c, out_grad, router, hits, live, gain,
    grad_hidden_ref, branch_ref, router_grad_ref, gain_grad_ref,
):
    width = normed.shape[1]
    summed = part_a[...].astype(f32) + part_b[...].astype(f32) + part_c[...].astype(f32)
    grad_experts, grad_gates = summed[:, :width], summed[:, width:]
    hit = hits[...] > 0.0
    shares = masked_shares(dot(normed[...], router[...], 1, 0), hit, 1)
    grad_shares = jnp.where(hit, grad_gates, 0.0)
    grad_chosen = shares * (grad_shares - jnp.sum(shares * grad_shares, axis=1, keepdims=True))
    high, low = split16(grad_chosen)
    experts = router_grad_ref.shape[0]
    router_grad_ref[...] = (dot(high, normed[...], 0, 0) + dot(low, normed[...], 0, 0))[:experts]
    grad_mix = grad_experts + dot(high, router[...], 1, 1) + dot(low, router[...], 1, 1)
    hidden, inverse = hidden_in[...], inv[...]
    gain_grad_ref[...] = jnp.sum(grad_mix * hidden * inverse, axis=0, keepdims=True)
    weighted = grad_mix * gain[...]
    centre = jnp.mean(hidden * weighted, axis=1, keepdims=True)
    grad_hidden = out_grad[...].astype(f32) + inverse * weighted - hidden * (inverse * inverse * inverse * centre)
    grad_hidden_ref[...] = grad_hidden
    branch_ref[...] = (live[...] * grad_hidden).astype(bf16)


def token_back_kernel(tokens, keep, got, grad_hidden, gain, out_ref, gain_grad_ref):
    source = tokens[...].astype(f32)
    inverse = lax.rsqrt(jnp.mean(source * source, axis=1, keepdims=True) + epsilon)
    grad = keep[...].astype(f32) + got[...].astype(f32)
    gain_grad_ref[...] = jnp.sum(grad * source * inverse, axis=0, keepdims=True)
    weighted = grad * gain[...]
    centre = jnp.mean(source * weighted, axis=1, keepdims=True)
    total = grad_hidden[...] + inverse * weighted - source * (inverse * inverse * inverse * centre)
    out_ref[...] = total.astype(bf16)


def placing(ranks, cap):
    slot = lax.broadcasted_iota(jnp.int32, (cap, ranks.shape[1]), 0).astype(f32)
    return [(slot == ranks[e:e + 1]).astype(f32) for e in range(ranks.shape[0])]


def pick_block(refs, block_ref):
    step = pl.program_id(0)
    near, far = refs[:5], refs[5:]
    half = near[0].shape[0] // 2
    for j in range(8):
        part = near if j % 2 == 0 else far

        @pl.when(step == j)
        def _():
            if j // 2 < 3:
                block_ref[...] = part[j // 2][...]
            else:
                block_ref[:half] = part[3][...]
                block_ref[half:] = part[4][...]


def dispatch_kernel(local, cap, where_ref, *refs):
    rows, (ranks, out_ref, block_ref) = refs[:10], refs[10:]
    pick_block(rows, block_ref)
    first = pl.multiple_of(where_ref[1] * 8, 8)
    mine = ranks[0, 0, pl.ds(first, 8)].astype(f32)[:local]
    matrix = jnp.concatenate([m.astype(bf16) for m in placing(mine, cap)], axis=0)
    placed = dot(matrix, block_ref[...], 1, 0).astype(bf16)
    out_ref[...] = placed.reshape(out_ref.shape)


def dispatch_gates_kernel(local, cap, where_ref, *refs):
    rows, (ranks, router_t, out_ref, gates_ref, block_ref, shares_ref) = refs[:10], refs[10:]
    pick_block(rows, block_ref)
    all_ranks = ranks[0, 0].astype(f32)
    logits = dot(router_t[...], block_ref[...], 1, 1)
    shares_ref[...] = masked_shares(logits, all_ranks >= 0.0, 0)
    first = pl.multiple_of(where_ref[1] * 8, 8)
    mine = ranks[0, 0, pl.ds(first, 8)].astype(f32)[:local]
    shares = shares_ref[pl.ds(first, 8)]
    places = placing(mine, cap)
    for e in range(local):
        gates_ref[e, 0] = jnp.sum(places[e] * shares[e:e + 1], axis=1, keepdims=True)
    matrix = jnp.concatenate([m.astype(bf16) for m in places], axis=0)
    placed = dot(matrix, block_ref[...], 1, 0).astype(bf16)
    out_ref[...] = placed.reshape(out_ref.shape)


def combine_kernel(local, cap, groups, where_ref, *refs):
    values, (ranks, out_ref) = refs[:groups], refs[groups:]
    first = pl.multiple_of(where_ref[1] * 8, 8)
    mine = ranks[0, 0, pl.ds(first, 8)].astype(f32)[:local]
    matrix = jnp.concatenate([m.astype(bf16) for m in placing(mine, cap)], axis=0)
    rows = jnp.concatenate([v[:, 0].reshape(-1, v.shape[-1]) for v in values], axis=0)
    out_ref[0] = dot(matrix, rows, 0, 0).astype(bf16)


def expert_kernel(base, where_ref, x_ref, g_ref, gates_ref, w_ref, y_ref, dx_ref, dw_ref):
    slots, width = x_ref.shape[1] * x_ref.shape[2], x_ref.shape[3]
    hidden = w_ref.shape[-1]
    x = x_ref[0].reshape(slots, width)
    g = g_ref[0].reshape(slots, width)
    gates = gates_ref[0].reshape(slots, 1)
    w_gate, w_up, w_down = (w_ref[:, 0, i].reshape(width, hidden) for i in range(3))
    gate_lin = dot(x, w_gate, 1, 0)
    up_lin = dot(x, w_up, 1, 0)
    grad_scaled = dot(g, w_down, 1, 0)
    sigmoid = 1.0 / (1.0 + jnp.exp(-gate_lin))
    silu = gate_lin * sigmoid
    grad_gates = jnp.sum(grad_scaled * silu * up_lin, axis=1, keepdims=True)
    scaled_hidden = (gates * silu * up_lin).astype(bf16)
    grad_act = gates * grad_scaled
    grad_gate_lin = (grad_act * up_lin * sigmoid * (1.0 + gate_lin * (1.0 - sigmoid))).astype(bf16)
    grad_up_lin = (grad_act * silu).astype(bf16)
    y_ref[0] = dot(scaled_hidden, w_down, 1, 1).astype(bf16).reshape(y_ref.shape[1:])
    dx = dot(grad_gate_lin, w_gate, 1, 1) + dot(grad_up_lin, w_up, 1, 1)
    dx_ref[0, :, :, :width] = dx.astype(bf16).reshape(dx_ref.shape[1:3] + (width,))
    lane = lax.broadcasted_iota(jnp.int32, (slots, LANES), 1)
    number = where_ref[2] + base + pl.program_id(0)
    tail = jnp.where(lane == number, grad_gates, 0.0).astype(bf16)
    dx_ref[0, :, :, width:] = tail.reshape(dx_ref.shape[1:3] + (LANES,))
    planes, _, _, _, deep, _, = dw_ref.shape[0], 0, 0, 0, dw_ref.shape[4], 0
    quarter = dw_ref.shape[5]
    for i, (left, right) in enumerate(((x, grad_gate_lin), (x, grad_up_lin), (g, scaled_hidden))):
        grad = dot(left, right, 0, 0).astype(bf16)
        for z in range(planes):
            for q in range(8):
                row = (z * 2 + q // 4) * deep
                col = q % 4 * quarter
                dw_ref[z, q, 0, i] = grad[row:row + deep, col:col + quarter]


def shards(
    tokens,
    lengths,
    routes,
    gain_attn,
    w_query,
    w_keyvalue,
    w_out,
    gain_mixer,
    w_router,
    w_gate,
    w_up,
    w_down,
    out_grad,
):
    nd, nt = lax.axis_size("dp"), lax.axis_size("tensor")
    dp_id, t_id = lax.axis_index("dp"), lax.axis_index("tensor")
    rows, width = tokens.shape
    group_rows, top_count = routes.shape
    seq_count = lengths.shape[0]
    seq_len = group_rows // seq_count
    experts = w_router.shape[1]
    local = experts // 8
    planes = nd // 2
    deep = width // nd
    hidden = w_gate.shape[2] * nt
    capacity = (rows * top_count * 17 + experts * 16 - 1) // (experts * 16)
    cap = -(-capacity // 16) * 16
    plane_id = (dp_id % 2) * nt + t_id
    core = t_id % 2
    z_groups = [[x + 2 * z for z in range(planes)] for x in range(2)]
    plane_groups = [[(z * 2 + x) * nt + t for x in range(2) for t in range(nt)] for z in range(planes)]

    q_cols, kv_cols = w_query.shape[1], w_keyvalue.shape[2]
    w_mine = jnp.concatenate([w_query, w_keyvalue[:, 0], w_keyvalue[:, 1], w_out], axis=1)
    w_other = hop_y(w_mine)
    cuts = [0, q_cols, q_cols + kv_cols, q_cols + 2 * kv_cols, 2 * q_cols + 2 * kv_cols]
    w_pairs = []
    for lo, hi in zip(cuts[:-1], cuts[1:]):
        w_pairs += [w_mine[:, lo:hi], w_other[:, lo:hi]]
    w_attn = lax.all_gather(jnp.concatenate(w_pairs, axis=1), "dp", axis=0, tiled=True)
    w_qkv, wo = w_attn[:, : 2 * q_cols + 4 * kv_cols], w_attn[:, 2 * q_cols + 4 * kv_cols:]

    tokens_f = tokens.astype(f32)
    inverse_attn = lax.rsqrt(jnp.mean(tokens_f * tokens_f, axis=1, keepdims=True) + epsilon)
    normed_attn = (tokens_f * inverse_attn * gain_attn[None, :]).astype(bf16)
    normed_peer = hop_c(normed_attn)

    positions = jnp.arange(group_rows, dtype=jnp.int32) % seq_len
    row_length = jnp.repeat(lengths, seq_len)
    live = positions < row_length
    ids = jnp.arange(experts, dtype=jnp.int32)
    hits_t = jnp.any(routes.T[:, None, :] == ids[None, :, None], axis=0) & live[None, :]
    order = jnp.arange(rows, dtype=jnp.int32)
    before = (order[:, None] < order[None, :]).astype(bf16)
    hits_blocks = hits_t.reshape(experts, nt, rows)
    earlier = jnp.einsum("ebr,rs->ebs", hits_blocks.astype(bf16), before, preferred_element_type=f32)
    ranks = jnp.where(hits_blocks, earlier, -1.0).astype(bf16)
    ranks = jnp.transpose(ranks.reshape(8, local, nt, rows), (2, 0, 1, 3))
    ranks = jnp.pad(ranks, ((0, 0), (0, 0), (0, 8 - local), (0, 0)), constant_values=-1.0)
    ranks = ranks.reshape(nt, 64, rows)
    ranks = jnp.stack([ranks, hop_x(ranks)])
    own_start = t_id * rows
    live_own = lax.dynamic_slice_in_dim(live, own_start, rows, 0).astype(f32)[:, None]
    routes_own = lax.dynamic_slice_in_dim(routes, own_start, rows, 0)
    lane_ids = jnp.arange(LANES, dtype=jnp.int32)
    hits_own = jnp.any(routes_own[:, :, None] == lane_ids[None, None, :], axis=1).astype(f32) * live_own
    router = jnp.pad(w_router, ((0, 0), (0, LANES - experts)))
    router_t = jnp.pad(w_router.T.reshape(8, local, width), ((0, 0), (0, 8 - local), (0, 0))).reshape(64, width)

    def for_plane(w):
        return jnp.transpose(w.reshape(deep, 8, local, hidden // nt), (1, 2, 0, 3))

    w_send = jnp.stack([for_plane(w_gate), for_plane(w_up), for_plane(w_down)], axis=2)
    groups = 2
    per = local // groups
    w_groups = []
    for i in range(groups):
        piece = lax.all_to_all(
            w_send[:, i * per:(i + 1) * per], BOTH, 0, 0, tiled=True, axis_index_groups=plane_groups
        )
        piece = piece.reshape(2, nt, per, 3, deep, hidden // nt)
        piece = jnp.transpose(piece, (2, 3, 0, 4, 1, 5)).reshape(per, 3, 2 * deep, hidden)
        w_groups.append(lax.all_gather(piece, "dp", axis_index_groups=z_groups))

    half_head = HD // 2
    exponent = 2.0 * jnp.arange(half_head, dtype=f32) / HD
    angles = jnp.arange(seq_len, dtype=f32)[:, None] * jnp.exp(-math.log(rope_base) * exponent)[None, :]
    cosine, sine = jnp.cos(angles), jnp.sin(angles)
    cos_table = jnp.concatenate([cosine] * 4, axis=1)
    sin_table = jnp.concatenate([-sine, sine] * 2, axis=1)

    place = jnp.stack(
        [core, plane_id, plane_id * local, t_id]
    ).astype(jnp.int32)
    length = lax.dynamic_slice_in_dim(lengths, own_start // seq_len, 1, 0)[0]
    where_attn = jnp.stack([core, length]).astype(jnp.int32)

    q_width, k_width = 2 * q_cols, 2 * kv_cols
    heads = q_width // HD
    q, k, v, ctx, lse, keep, send = call(
        attend_kernel,
        [
            sds((seq_len, q_width), bf16), sds((seq_len, k_width), bf16), sds((seq_len, k_width), bf16),
            sds((seq_len, q_width), bf16), sds((heads, seq_len), f32),
            sds((rows, width), bf16), sds((rows, width), bf16),
        ],
        12 * 10**9, 16 * 2**20,
        in_specs=[SM] + [VM] * 6, out_specs=[VM] * 7,
        scratch_shapes=[pltpu.VMEM((seq_len, width), bf16)],
    )(where_attn, normed_attn, normed_peer, w_qkv, wo, cos_table, sin_table)
    got = hop_c(send)
    hidden_own, normed_mix, inverse_mix = call(
        mix_norm_kernel,
        [sds((rows, width), f32), sds((rows, width), bf16), sds((rows, 1), f32)],
        10**7, 8 * 2**20,
        in_specs=[VM] * 5, out_specs=[VM] * 3,
    )(tokens, keep, got, live_own, gain_mixer[None, :])

    slots_shape = (local, 8, cap, width)

    def ranks_spec(stride, start):
        def index(i, where):
            j = stride * i + start
            return (j // 4, lax.bitwise_xor(where[3], j % 4), 0, 0)
        return pl.BlockSpec((1, 1, 64, rows), index)

    def whole(a):
        return pl.BlockSpec(a.shape, lambda i, where: (0,) * a.ndim)

    def dispatch(blocks, gated):
        out_specs = [pl.BlockSpec((local, 1, cap, width), lambda i, where: (0, i, 0, 0))]
        out_shape = [sds(slots_shape, bf16)]
        scratch = [pltpu.VMEM((rows, width), bf16)]
        extra = []
        if gated:
            extra = [router_t]
            out_specs.append(pl.BlockSpec((local, 1, cap, 1), lambda i, where: (0, i, 0, 0)))
            out_shape.append(sds((local, 8, cap, 1), f32))
            scratch.append(pltpu.VMEM((64, rows), f32))
        return call(
            functools.partial(dispatch_gates_kernel if gated else dispatch_kernel, local, cap),
            out_shape, 5 * 10**9, 20 * 2**20,
            grid_spec=pltpu.PrefetchScalarGridSpec(
                num_scalar_prefetch=1, grid=(8,),
                in_specs=[whole(b) for b in blocks] + [ranks_spec(1, 0)] + [whole(e) for e in extra],
                out_specs=out_specs, scratch_shapes=scratch,
            ),
        )(place, *blocks, ranks, *extra)

    (grads_in,) = dispatch(gather_plane(out_grad), False)
    rows_in, gates_in = dispatch(gather_plane(normed_mix), True)

    ys, dxs, dws = [], [], []
    for i in range(groups):
        def slot_spec(last):
            return pl.BlockSpec((1, 8, cap, last), lambda e, where, i=i: (i * per + e, 0, 0, 0))
        def out_spec(last):
            return pl.BlockSpec((1, 8, cap, last), lambda e, where: (e, 0, 0, 0))
        y, dx, dw = call(
            functools.partial(expert_kernel, i * per),
            [
                sds((per, 8, cap, width), bf16), sds((per, 8, cap, width + LANES), bf16),
                sds((planes, 8, per, 3, deep, hidden // nt), bf16),
            ],
            per * 18 * 8 * cap * width * hidden, per * 20 * 2**20,
            grid_spec=pltpu.PrefetchScalarGridSpec(
                num_scalar_prefetch=1, grid=(per,),
                in_specs=[
                    slot_spec(width), slot_spec(width), slot_spec(1),
                    pl.BlockSpec((planes, 1, 3, 2 * deep, hidden), lambda e, where: (0, e, 0, 0, 0)),
                ],
                out_specs=[
                    out_spec(width), out_spec(width + LANES),
                    pl.BlockSpec((planes, 8, 1, 3, deep, hidden // nt), lambda e, where: (0, 0, e, 0, 0, 0)),
                ],
            ),
        )(place, rows_in, grads_in, gates_in, w_groups[i])
        ys.append(y)
        dxs.append(dx)
        dws.append(dw)

    def combine(values, start):
        last = values[0].shape[-1]
        return call(
            functools.partial(combine_kernel, local, cap, groups),
            sds((4, rows, last), bf16), 25 * 10**8, 12 * 2**20,
            grid_spec=pltpu.PrefetchScalarGridSpec(
                num_scalar_prefetch=1, grid=(4,),
                in_specs=[
                    pl.BlockSpec((per, 1, cap, last), lambda i, where: (0, 2 * i + start, 0, 0)) for _ in values
                ] + [ranks_spec(2, start)],
                out_specs=pl.BlockSpec((1, rows, last), lambda i, where: (i, 0, 0)),
            ),
        )(place, *values, ranks)

    grad_terms = scatter_plane(combine(dxs, 1), combine(dxs, 0))
    grad_hidden, grad_branch, router_grad, gain_mix_grad = call(
        mix_back_kernel,
        [
            sds((rows, width), f32), sds((rows, width), bf16), sds((experts, width), f32), sds((1, width), f32),
        ],
        10**8, 12 * 2**20,
        in_specs=[VM] * 11, out_specs=[VM] * 4,
    )(
        normed_mix, hidden_own, inverse_mix, *grad_terms, out_grad, router, hits_own, live_own,
        gain_mixer[None, :],
    )
    branch_peer = hop_c(grad_branch)

    out_terms = scatter_plane(combine(ys, 1), combine(ys, 0))
    mixed = (hidden_own + sum(term.astype(f32) for term in out_terms)).astype(bf16)

    dw_qkv, dwo, keep_back, send_back = call(
        attend_back_kernel,
        [
            sds((width, q_width + 2 * k_width), bf16), sds((width, q_width), bf16),
            sds((rows, width), bf16), sds((rows, width), bf16),
        ],
        25 * 10**9, 24 * 2**20,
        in_specs=[SM] + [VM] * 13, out_specs=[VM] * 4,
        scratch_shapes=[
            pltpu.VMEM((seq_len, width), bf16), pltpu.VMEM((seq_len, width), bf16),
            pltpu.VMEM((seq_len, q_width), bf16), pltpu.VMEM((seq_len, q_width + 2 * k_width), bf16),
            pltpu.VMEM((seq_len, LANES), f32), pltpu.VMEM((seq_len, LANES), f32),
        ],
    )(
        where_attn, normed_attn, normed_peer, grad_branch, branch_peer, w_qkv, wo, cos_table, sin_table,
        q, k, v, ctx, lse,
    )
    got_back = hop_c(send_back)
    grad_tokens, gain_attn_grad = call(
        token_back_kernel,
        [sds((rows, width), bf16), sds((1, width), f32)],
        10**7, 8 * 2**20,
        in_specs=[VM] * 5, out_specs=[VM] * 2,
    )(tokens, keep_back, got_back, grad_hidden, gain_attn[None, :])

    grad_pieces = []
    for dw in dws:
        mine = lax.psum_scatter(dw, "dp", scatter_dimension=0, axis_index_groups=z_groups)
        grad_pieces.append(
            lax.all_to_all(mine, BOTH, 0, 0, tiled=True, axis_index_groups=plane_groups)
        )

    def to_owner(which):
        parts = [piece[:, :, which].astype(f32) for piece in grad_pieces]
        whole_grad = jnp.concatenate(parts, axis=1).reshape(experts, deep, hidden // nt)
        return jnp.transpose(whole_grad, (1, 0, 2))

    def halves(grad, start, cols):
        return grad[:, start:start + cols], grad[:, start + cols:start + 2 * cols]

    pieces = [
        halves(dw_qkv, 0, q_cols), halves(dw_qkv, q_width, kv_cols),
        halves(dw_qkv, q_width + k_width, kv_cols), halves(dwo, 0, q_cols),
    ]
    mine = jnp.concatenate([a for a, _ in pieces], axis=1)
    other = jnp.concatenate([b for _, b in pieces], axis=1)
    attn_grad = add16(mine, hop_y(other))
    attn_grad = lax.psum_scatter(attn_grad, "dp", scatter_dimension=0, tiled=True).astype(f32)
    grad_query = attn_grad[:, cuts[0]:cuts[1]]
    grad_keyval = jnp.stack([attn_grad[:, cuts[1]:cuts[2]], attn_grad[:, cuts[2]:cuts[3]]], axis=1)
    grad_out = attn_grad[:, cuts[3]:cuts[4]]

    small = lax.psum(jnp.concatenate([router_grad, gain_mix_grad, gain_attn_grad], axis=0), BOTH)
    return (
        mixed,
        grad_tokens,
        small[experts + 1],
        grad_query,
        grad_keyval,
        grad_out,
        small[experts],
        small[:experts].T,
        to_owner(0),
        to_owner(1),
        to_owner(2),
    )


def solution(mesh):
    placed = (
        P(("dp", "tensor"), None),
        P("dp"),
        P("dp", None),
        P(),
        P("dp", "tensor"),
        P("dp", None, "tensor"),
        P("dp", "tensor"),
        P(),
        P(),
        P("dp", None, "tensor"),
        P("dp", None, "tensor"),
        P("dp", None, "tensor"),
        P(("dp", "tensor"), None),
    )
    return jax.shard_map(
        shards,
        mesh=mesh,
        in_specs=placed,
        out_specs=(
            P(("dp", "tensor"), None),
            P(("dp", "tensor"), None),
            P(),
            P("dp", "tensor"),
            P("dp", None, "tensor"),
            P("dp", "tensor"),
            P(),
            P(),
            P("dp", None, "tensor"),
            P("dp", None, "tensor"),
            P("dp", None, "tensor"),
        ),
        check_vma=False,
    )
```

```python
import functools
import math

import jax
import jax.numpy as jnp
from jax import lax
from jax.experimental import pallas as pl
from jax.experimental.pallas import tpu as pltpu
from jax.sharding import PartitionSpec as P

HD = 64
LANES = 128
epsilon = 1e-06
rope_base = 10000.0
bf16 = jnp.bfloat16
f32 = jnp.float32
BOTH = ("dp", "tensor")
VMEM_LIMIT = 60 * 1024 * 1024
QBLK = 256


def dot(a, b, ca, cb):
    return lax.dot_general(a, b, (((ca,), (cb,)), ((), ())), preferred_element_type=f32)


def call(kernel, out_shape, flops, nbytes, **kw):
    return pl.pallas_call(
        kernel,
        out_shape=out_shape,
        compiler_params=pltpu.CompilerParams(vmem_limit_bytes=VMEM_LIMIT),
        cost_estimate=pl.CostEstimate(flops=flops, bytes_accessed=nbytes, transcendentals=0),
        **kw,
    )


def sds(shape, dtype):
    return jax.ShapeDtypeStruct(shape, dtype)


VM = pl.BlockSpec(memory_space=pltpu.VMEM)
SM = pl.BlockSpec(memory_space=pltpu.SMEM)


def hop(x, dp_bit, t_bits):
    nd, nt = lax.axis_size("dp"), lax.axis_size("tensor")
    pairs = [
        (d * nt + t, (d ^ dp_bit) * nt + (t ^ t_bits)) for d in range(nd) for t in range(nt)
    ]
    return lax.ppermute(x, BOTH, pairs)


def hop_c(x):
    return hop(x, 0, 1)


def hop_y(x):
    return hop(x, 0, 2)


def hop_x(x):
    return hop(x, 1, 0)


def gather_plane(x, from_y=None, from_x=None):
    half = x.shape[0] // 2
    if from_y is None:
        from_y, from_x = hop_y(x), hop_x(x)
    diag_a, diag_b = hop_x(from_y[:half]), hop_y(from_x[half:])
    near = (x, from_y, from_x, diag_a, diag_b)
    far = tuple(hop_c(item) for item in near)
    return near + far


def after(x, *others):
    return lax.optimization_barrier((x, *others))[0]


def add16(a, b):
    return (a.astype(f32) + b.astype(f32)).astype(bf16)


def scatter_plane(send, keep):
    total = add16(keep, hop_c(send))
    half = total.shape[1] // 2
    x_a, y_b = total[2, :half], total[1, half:]
    got_xa, got_yb = hop_x(x_a), hop_y(y_b)
    got_da, got_db = hop_x(total[3, :half]), hop_y(total[3, half:])
    got_ya = hop_y(add16(total[1, :half], got_da))
    got_xb = hop_x(add16(total[2, half:], got_db))
    return total[0], jnp.concatenate([got_xa, got_xb]), jnp.concatenate([got_ya, got_yb])


def gather_z(x, planes, z_groups, by_hops):
    if by_hops and planes == 4:
        return (x,) + tuple(hop(x, 2 * k, 0) for k in range(1, planes))
    return (lax.all_gather(x, "dp", axis_index_groups=z_groups),)


def sum_z(x, planes, z, z_groups):
    if planes != 4:
        return lax.psum_scatter(x, "dp", scatter_dimension=0, axis_index_groups=z_groups).astype(f32)
    total = lax.dynamic_index_in_dim(x, z, 0, False).astype(f32)
    for k in range(1, planes):
        total += hop(lax.dynamic_index_in_dim(x, z ^ k, 0, False), 2 * k, 0).astype(f32)
    return total


def sum_all(x, nd):
    for bit in (1, 2):
        x = x + hop(x, 0, bit)
    bit = 1
    while bit < nd:
        x = x + hop(x, bit, 0)
        bit *= 2
    return x


def swap_halves(v):
    lane = lax.broadcasted_iota(jnp.int32, v.shape, 1)
    left = pltpu.roll(v, LANES - HD // 2, 1)
    right = pltpu.roll(v, HD // 2, 1)
    return jnp.where(lane % HD < HD // 2, left, right)


def in_head(tile, h):
    lane = lax.broadcasted_iota(jnp.int32, tile.shape, 1)
    return (lane < HD) if h == 0 else (lane >= HD)


def only_head(tile, h):
    return jnp.where(in_head(tile, h), tile, jnp.zeros_like(tile))


def spread_head(tile, h):
    wide = tile.astype(f32)
    return jnp.where(in_head(wide, h), wide, pltpu.roll(wide, HD, 1)).astype(tile.dtype)


def stacked(tile):
    return jnp.concatenate([only_head(tile, 0), only_head(tile, 1)], axis=0)


def key_limit(start, rows, length):
    column = lax.broadcasted_iota(jnp.int32, (1, 2 * rows), 1)
    position = start + jnp.where(column >= rows, column - rows, column)
    return jnp.minimum(position, length - 1)


def scores_t(kd, qm, limit):
    raw = dot(kd, qm, 1, 1) * (1.0 / math.sqrt(HD))
    key = lax.broadcasted_iota(jnp.int32, raw.shape, 0)
    return jnp.where(key <= limit, raw, -1e30)


def attend_kernel(
    where_ref, rows, w, cos, sin,
    q_ref, k_ref, v_ref, ctx_ref, lse_ref, keep_ref, send_ref,
):
    core, length = where_ref[0], where_ref[1]
    seq, width = rows.shape
    half = seq // 2
    kw = k_ref.shape[1] // 2
    qw = 2 * kw
    cut = qw + 2 * kw
    for blk in range(seq // QBLK):
        sl = slice(blk * QBLK, (blk + 1) * QBLK)
        c, s = cos[sl], sin[sl]
        for y in range(2):
            pre = dot(rows[sl], w[y, :, :, :cut].reshape(width, cut), 1, 0)
            for tile in range((qw + kw) // LANES):
                col = pre[:, tile * LANES:(tile + 1) * LANES]
                turned = (col * c + swap_halves(col) * s).astype(bf16)
                if tile * LANES < qw:
                    q_ref[sl, y * qw + tile * LANES:y * qw + (tile + 1) * LANES] = turned
                else:
                    at = y * kw + tile * LANES - qw
                    k_ref[sl, at:at + LANES] = turned
            v_ref[sl, y * kw:(y + 1) * kw] = pre[:, qw + kw:].astype(bf16)
    for g in range(2 * qw // LANES):
        kv = slice(g // 2 * LANES, (g // 2 + 1) * LANES)
        cols = slice(g * LANES, (g + 1) * LANES)
        kd = spread_head(k_ref[:, kv], g % 2)
        vd_t = spread_head(v_ref[:, kv], g % 2).T
        for blk in range(seq // QBLK):
            top = (blk + 1) * QBLK
            sl = slice(blk * QBLK, top)
            s = scores_t(kd[:top], stacked(q_ref[sl, cols]), key_limit(blk * QBLK, QBLK, length))
            peak = jnp.max(s, axis=0, keepdims=True)
            e = jnp.exp(s - peak)
            total = jnp.sum(e, axis=0, keepdims=True)
            p = (e * (1.0 / total)).astype(bf16)
            ctx = dot(vd_t[:, :top], p, 1, 0).T
            tile = jnp.where(in_head(ctx[:QBLK], 0), ctx[:QBLK], ctx[QBLK:])
            ctx_ref[sl, cols] = tile.astype(bf16)
            lse = peak + jnp.log(total)
            lse_ref[2 * g:2 * g + 1, sl] = lse[:, :QBLK]
            lse_ref[2 * g + 1:2 * g + 2, sl] = lse[:, QBLK:]
    for out_ref, side in ((send_ref, 1 - core), (keep_ref, core)):
        at = pl.ds(pl.multiple_of(side * half, half), half)
        out = dot(ctx_ref[at, :qw], w[0, :, :, cut:].reshape(width, qw), 1, 1)
        out += dot(ctx_ref[at, qw:], w[1, :, :, cut:].reshape(width, qw), 1, 1)
        out_ref[...] = out.astype(bf16)


def attend_back_kernel(
    where_ref, rows, gb_own, gb_peer, w, cos, sin, q_ref, k_ref, v_ref, ctx_ref, lse_ref,
    dw_ref, keep_ref, send_ref,
    gb_ref, gc_ref, dqkv_ref, dk_ref, dv_ref,
):
    core, length = where_ref[0], where_ref[1]
    seq, width = rows.shape
    half = seq // 2
    kw = k_ref.shape[1] // 2
    qw = 2 * kw
    cut = qw + 2 * kw
    per_dp = dw_ref.shape[1:3]
    at_own = pl.ds(pl.multiple_of(core * half, half), half)
    at_peer = pl.ds(pl.multiple_of((1 - core) * half, half), half)
    gb_ref[at_own] = gb_own[...]
    gb_ref[at_peer] = gb_peer[...]
    for y in range(2):
        part = slice(y * qw, (y + 1) * qw)
        gc_ref[:, part] = dot(gb_ref[...], w[y, :, :, cut:].reshape(width, qw), 1, 0).astype(bf16)
        dw_ref[y, :, :, cut:] = dot(gb_ref[...], ctx_ref[:, part], 0, 0).astype(bf16).reshape(per_dp + (qw,))
    scale = 1.0 / math.sqrt(HD)
    folded = None
    for g in range(2 * qw // LANES):
        y = g // 2
        kv = slice(y * LANES, (y + 1) * LANES)
        cols = slice(g * LANES, (g + 1) * LANES)
        kd = spread_head(k_ref[:, kv], g % 2)
        kd_t = kd.T
        vd = spread_head(v_ref[:, kv], g % 2)
        for blk in reversed(range(seq // QBLK)):
            top = (blk + 1) * QBLK
            sl = slice(blk * QBLK, top)
            qm = stacked(q_ref[sl, cols])
            gm = stacked(gc_ref[sl, cols])
            s = scores_t(kd[:top], qm, key_limit(blk * QBLK, QBLK, length))
            lse = jnp.concatenate([lse_ref[2 * g:2 * g + 1, sl], lse_ref[2 * g + 1:2 * g + 2, sl]], axis=1)
            p = jnp.exp(s - lse)
            gw = dot(vd[:top], gm, 1, 1)
            centre = jnp.sum(p * gw, axis=0, keepdims=True)
            ds = (p * (gw - centre) * scale).astype(bf16)
            dv = dot(p.astype(bf16), gm, 1, 0)
            dk = dot(ds, qm, 1, 0)
            dq = dot(kd_t[:, :top], ds, 1, 0).T
            if top == seq:
                dk_ref[...] = dk
                dv_ref[...] = dv
            else:
                dk_ref[:top] += dk
                dv_ref[:top] += dv
            tile = jnp.where(in_head(dq[:QBLK], 0), dq[:QBLK], dq[QBLK:])
            back = tile * cos[sl] - swap_halves(tile) * sin[sl]
            at = y * cut + g % 2 * LANES
            dqkv_ref[sl, at:at + LANES] = back.astype(bf16)
        dk_all = dk_ref[...] + pltpu.roll(dk_ref[...], HD, 1)
        dv_all = dv_ref[...] + pltpu.roll(dv_ref[...], HD, 1)
        if g % 2 == 0:
            folded = (dk_all, dv_all)
        else:
            dk_pair = jnp.where(in_head(dk_all, 0), folded[0], dk_all)
            dv_pair = jnp.where(in_head(dv_all, 0), folded[1], dv_all)
            at = y * cut + qw
            back = dk_pair * cos[...] - swap_halves(dk_pair) * sin[...]
            dqkv_ref[:, at:at + LANES] = back.astype(bf16)
            dqkv_ref[:, at + LANES:at + 2 * LANES] = dv_pair.astype(bf16)
            part = slice(y * cut, (y + 1) * cut)
            dw_ref[y, :, :, :cut] = dot(rows[...], dqkv_ref[:, part], 0, 0).astype(bf16).reshape(per_dp + (cut,))
    for out_ref, at in ((send_ref, at_peer), (keep_ref, at_own)):
        out = dot(dqkv_ref[at, :cut], w[0, :, :, :cut].reshape(width, cut), 1, 1)
        out += dot(dqkv_ref[at, cut:], w[1, :, :, :cut].reshape(width, cut), 1, 1)
        out_ref[...] = out.astype(bf16)


def deal_out(p, plane_peers, w_send, numbers, dealt, send_sem, recv_sem):
    copies = []
    for i, e in enumerate(numbers):
        for j in (6, 7, 2, 4, 3, 5, 1):
            copies.append(
                pltpu.make_async_remote_copy(
                    src_ref=w_send.at[p ^ j, e], dst_ref=dealt[i].at[j], send_sem=send_sem.at[i, j],
                    recv_sem=recv_sem.at[i, j], device_id=plane_peers[j], device_id_type=pl.DeviceIdType.MESH,
                )
            )
        copies.append(pltpu.make_async_copy(w_send.at[p, e], dealt[i].at[0], send_sem.at[i, 0]))
    for copy in copies:
        copy.start()
    return copies


def deal_kernel(w_send, *refs):
    dealt, (send_sem, recv_sem) = refs[:-2], refs[-2:]
    d, t = lax.axis_index("dp"), lax.axis_index("tensor")
    p = d % 2 * 4 + t
    peers = [{"dp": d // 2 * 2 + (p ^ j) // 4, "tensor": (p ^ j) % 4} for j in range(8)]
    barrier = pltpu.get_barrier_semaphore()
    for peer in peers[1:]:
        pl.semaphore_signal(barrier, inc=1, device_id=peer, device_id_type=pl.DeviceIdType.MESH)
    pl.semaphore_wait(barrier, 7)
    for copy in deal_out(p, peers, w_send, range(len(dealt)), dealt, send_sem, recv_sem):
        copy.wait()


def rank_rows(lengths, routes_t, block, ranks_ref):
    blocks, wide = ranks_ref.shape[1:3]
    seq_len = block * blocks // lengths.shape[0]
    local = wide // 16
    row = lax.broadcasted_iota(jnp.int32, (wide, block), 0)
    number = jnp.where(row % 8 < local, row // 8 * local + row % 8, -1)
    low = lax.broadcasted_iota(jnp.int32, (block, block), 0)
    high = lax.broadcasted_iota(jnp.int32, (block, block), 1)
    before = (low < high).astype(f32).astype(bf16)
    for b in range(blocks):
        at = slice(b * block, (b + 1) * block)
        position = lax.broadcasted_iota(jnp.int32, (wide, block), 1) + b * block % seq_len
        hit = jnp.zeros((wide, block), jnp.bool_)
        for k in range(routes_t.shape[0]):
            hit = hit | (routes_t[k:k + 1, at] == number)
        hit = hit & (position < lengths[b * block // seq_len])
        earlier = dot(hit.astype(f32).astype(bf16), before, 1, 0)
        ranks_ref[0, b] = jnp.where(hit, earlier, -1.0).astype(bf16)


def gather_kernel(later, lengths, tokens, gain, routes_t, w_mine, w_send, rows_ref, w_ref, ranks_ref, *refs):
    dealt, (send_sem, recv_sem, row_sem, deal_send, deal_recv) = refs[:-5], refs[-5:]
    d, t = lax.axis_index("dp"), lax.axis_index("tensor")
    planes = w_ref.shape[1] // 2
    half = tokens.shape[0]
    z, x, core = d // 2, d % 2, t % 2

    def device(dp, tensor):
        return {"dp": dp, "tensor": tensor}

    def plane(dz):
        return lax.rem(z + dz, planes)

    x_peer, y_peer = device(z * 2 + 1 - x, t), device(d, (t + 2) % 4)
    core_peer = device(d, t + 1 - 2 * core)
    z_peers = [device(plane(dz) * 2 + x, t) for dz in range(1, planes)]
    barrier = pltpu.get_barrier_semaphore()
    p = x * 4 + t
    plane_peers = [device(z * 2 + (p ^ j) // 4, (p ^ j) % 4) for j in range(8)]
    for peer in [*z_peers, *plane_peers[1:]]:
        pl.semaphore_signal(barrier, inc=1, device_id=peer, device_id_type=pl.DeviceIdType.MESH)
    pl.semaphore_wait(barrier, planes + 6)

    copies = []

    def push(source, side, dp, peer):
        copy = pltpu.make_async_remote_copy(
            src_ref=source, dst_ref=w_ref.at[side, dp], send_sem=send_sem.at[len(copies)],
            recv_sem=recv_sem.at[side, dp], device_id=peer, device_id_type=pl.DeviceIdType.MESH,
        )
        copy.start()
        copies.append(copy)

    def arrive(side, dp):
        slot = w_ref.at[side, dp]
        pltpu.make_async_remote_copy(
            src_ref=slot, dst_ref=slot, send_sem=send_sem.at[0], recv_sem=recv_sem.at[side, dp],
            device_id=x_peer, device_id_type=pl.DeviceIdType.MESH,
        ).wait_recv()

    for peer in z_peers:
        push(w_mine, 0, d, peer)
    push(w_mine, 0, d, x_peer)
    push(w_mine, 1, d, y_peer)
    deals = deal_out(p, plane_peers, w_send, later, dealt, deal_send, deal_recv)
    values = tokens[...].astype(f32)
    inverse = lax.rsqrt(jnp.mean(values * values, axis=1, keepdims=True) + epsilon)
    at = pl.ds(pl.multiple_of(core * half, half), half)
    rows_ref[at] = (values * inverse * gain[...]).astype(bf16)
    row_copy = pltpu.make_async_remote_copy(
        src_ref=rows_ref.at[at], dst_ref=rows_ref.at[at], send_sem=row_sem.at[0], recv_sem=row_sem.at[1],
        device_id=core_peer, device_id_type=pl.DeviceIdType.MESH,
    )
    row_copy.start()
    w_ref[0, d] = w_mine[...]
    rank_rows(lengths, routes_t, half, ranks_ref)
    rank_copy = pltpu.make_async_remote_copy(
        src_ref=ranks_ref.at[0], dst_ref=ranks_ref.at[1], send_sem=row_sem.at[2], recv_sem=row_sem.at[3],
        device_id=x_peer, device_id_type=pl.DeviceIdType.MESH,
    )
    rank_copy.start()
    near = [plane(dz) * 2 + x for dz in range(planes)]
    over = [plane(dz) * 2 + 1 - x for dz in range(planes)]

    def turn(dz):
        arrive(0, over[dz])
        if dz < planes // 2:
            push(w_ref.at[0, over[dz]], 1, over[dz], y_peer)
        arrive(1, near[dz])
        if dz >= planes // 2:
            push(w_ref.at[1, near[dz]], 1, near[dz], x_peer)

    for dz in range(1, planes):
        arrive(0, near[dz])
        push(w_ref.at[0, near[dz]], 0, near[dz], x_peer)
        push(w_ref.at[0, near[dz]], 1, near[dz], y_peer)
        turn(dz - 1)
    turn(planes - 1)
    for dz in range(planes):
        arrive(1, over[dz])
    for copy in copies:
        copy.wait_send()
    row_copy.wait()
    rank_copy.wait()
    for copy in deals:
        copy.wait()


def mix_norm_kernel(tokens, keep, got, live, gain, hidden_ref, normed_ref, inv_ref):
    branch = keep[...].astype(f32) + got[...].astype(f32)
    hidden = tokens[...].astype(f32) + live[...] * branch
    inverse = lax.rsqrt(jnp.mean(hidden * hidden, axis=1, keepdims=True) + epsilon)
    hidden_ref[...] = hidden
    inv_ref[...] = inverse
    normed_ref[...] = (hidden * inverse * gain[...]).astype(bf16)


def masked_shares(logits, hit, axis):
    peak = jnp.max(jnp.where(hit, logits, -1e30), axis=axis, keepdims=True)
    e = jnp.where(hit, jnp.exp(jnp.where(hit, logits - peak, 0.0)), 0.0)
    total = jnp.sum(e, axis=axis, keepdims=True)
    return e / jnp.where(total > 0.0, total, 1.0)


def split16(v):
    high = v.astype(bf16)
    return high, (v - high.astype(f32)).astype(bf16)


def mix_back_kernel(
    normed, hidden_in, inv, part_a, part_b, part_c, out_grad, router, hits, live, gain,
    grad_hidden_ref, branch_ref, router_grad_ref, gain_grad_ref,
):
    width = normed.shape[1]
    summed = part_a[...].astype(f32) + part_b[...].astype(f32) + part_c[...].astype(f32)
    grad_experts, grad_gates = summed[:, :width], summed[:, width:]
    hit = hits[...] > 0.0
    shares = masked_shares(dot(normed[...], router[...], 1, 0), hit, 1)
    grad_shares = jnp.where(hit, grad_gates, 0.0)
    grad_chosen = shares * (grad_shares - jnp.sum(shares * grad_shares, axis=1, keepdims=True))
    high, low = split16(grad_chosen)
    experts = router_grad_ref.shape[0]
    router_grad_ref[...] = (dot(high, normed[...], 0, 0) + dot(low, normed[...], 0, 0))[:experts]
    grad_mix = grad_experts + dot(high, router[...], 1, 1) + dot(low, router[...], 1, 1)
    hidden, inverse = hidden_in[...], inv[...]
    gain_grad_ref[...] = jnp.sum(grad_mix * hidden * inverse, axis=0, keepdims=True)
    weighted = grad_mix * gain[...]
    centre = jnp.mean(hidden * weighted, axis=1, keepdims=True)
    grad_hidden = out_grad[...].astype(f32) + inverse * weighted - hidden * (inverse * inverse * inverse * centre)
    grad_hidden_ref[...] = grad_hidden
    branch_ref[...] = (live[...] * grad_hidden).astype(bf16)


def token_back_kernel(tokens, keep, got, grad_hidden, gain, out_ref, gain_grad_ref):
    source = tokens[...].astype(f32)
    inverse = lax.rsqrt(jnp.mean(source * source, axis=1, keepdims=True) + epsilon)
    grad = keep[...].astype(f32) + got[...].astype(f32)
    gain_grad_ref[...] = jnp.sum(grad * source * inverse, axis=0, keepdims=True)
    weighted = grad * gain[...]
    centre = jnp.mean(source * weighted, axis=1, keepdims=True)
    total = grad_hidden[...] + inverse * weighted - source * (inverse * inverse * inverse * centre)
    out_ref[...] = total.astype(bf16)


def placing(ranks, cap):
    slot = lax.broadcasted_iota(jnp.int32, (cap, ranks.shape[1]), 0).astype(f32)
    return [(slot == ranks[e:e + 1]).astype(f32) for e in range(ranks.shape[0])]


def pick_block(refs, block_ref):
    step = pl.program_id(0)
    near, far = refs[:5], refs[5:]
    half = near[0].shape[0] // 2
    for j in range(8):
        part = near if j % 2 == 0 else far

        @pl.when(step == j)
        def _():
            if j // 2 < 3:
                block_ref[...] = part[j // 2][...]
            else:
                block_ref[:half] = part[3][...]
                block_ref[half:] = part[4][...]


def dispatch_kernel(local, cap, where_ref, *refs):
    rows, (ranks, out_ref, block_ref) = refs[:10], refs[10:]
    pick_block(rows, block_ref)
    first = pl.multiple_of(where_ref[1] * 8, 8)
    mine = ranks[0, 0, pl.ds(first, 8)].astype(f32)[:local]
    matrix = jnp.concatenate([m.astype(bf16) for m in placing(mine, cap)], axis=0)
    placed = dot(matrix, block_ref[...], 1, 0).astype(bf16)
    out_ref[...] = placed.reshape(out_ref.shape)


def dispatch_gates_kernel(local, cap, where_ref, *refs):
    rows, (ranks, router_t, out_ref, gates_ref, block_ref, shares_ref) = refs[:10], refs[10:]
    pick_block(rows, block_ref)
    all_ranks = ranks[0, 0].astype(f32)
    logits = dot(router_t[...], block_ref[...], 1, 1)
    shares_ref[...] = masked_shares(logits, all_ranks >= 0.0, 0)
    first = pl.multiple_of(where_ref[1] * 8, 8)
    mine = ranks[0, 0, pl.ds(first, 8)].astype(f32)[:local]
    shares = shares_ref[pl.ds(first, 8)]
    places = placing(mine, cap)
    for e in range(local):
        gates_ref[e, 0] = jnp.sum(places[e] * shares[e:e + 1], axis=1, keepdims=True)
    matrix = jnp.concatenate([m.astype(bf16) for m in places], axis=0)
    placed = dot(matrix, block_ref[...], 1, 0).astype(bf16)
    out_ref[...] = placed.reshape(out_ref.shape)


def combine_kernel(local, cap, groups, where_ref, *refs):
    values, (ranks, out_ref) = refs[:groups], refs[groups:]
    first = pl.multiple_of(where_ref[1] * 8, 8)
    mine = ranks[0, 0, pl.ds(first, 8)].astype(f32)[:local]
    matrix = jnp.concatenate([m.astype(bf16) for m in placing(mine, cap)], axis=0)
    rows = jnp.concatenate([v[:, 0].reshape(-1, v.shape[-1]) for v in values], axis=0)
    out_ref[0] = dot(matrix, rows, 0, 0).astype(bf16)


def expert_kernel(first, steps, where_ref, x_ref, g_ref, gates_ref, *refs):
    sources, (y_ref, dx_ref, dw_ref, w_buf, sem) = refs[:steps], refs[steps:]
    i = pl.program_id(0)
    last = pl.num_programs(0) - 1
    z = where_ref[4]
    planes = w_buf.shape[1]

    def each(expert, slot, act):
        if steps == 1:
            act(pltpu.make_async_copy(sources[0], w_buf.at[slot], sem.at[slot, 0]))
            return
        for k, source in enumerate(sources):
            act(pltpu.make_async_copy(source, w_buf.at[slot, z ^ k], sem.at[slot, k]))

    @pl.when(i == 0)
    def _():
        each(0, 0, lambda copy: copy.start())

    @pl.when(i < last)
    def _():
        each(i + 1, (i + 1) % 2, lambda copy: copy.start())

    slot = i % 2
    each(i, slot, lambda copy: copy.wait())
    slots, width = x_ref.shape[1] * x_ref.shape[2], x_ref.shape[3]
    deep, quarter = w_buf.shape[4:]
    x = x_ref[0].reshape(slots, width)
    g = g_ref[0].reshape(slots, width)
    gates = gates_ref[0].reshape(slots, 1)

    def weight(which):
        rows = []
        for plane in range(planes):
            for side in range(2):
                rows.append(
                    jnp.concatenate([w_buf[slot, plane, (side * 4 + q) ^ where_ref[1], which] for q in range(4)], axis=1)
                )
        return jnp.concatenate(rows, axis=0)

    w_gate, w_up, w_down = weight(0), weight(1), weight(2)
    gate_lin = dot(x, w_gate, 1, 0)
    up_lin = dot(x, w_up, 1, 0)
    grad_scaled = dot(g, w_down, 1, 0)
    sigmoid = 1.0 / (1.0 + jnp.exp(-gate_lin))
    silu = gate_lin * sigmoid
    grad_gates = jnp.sum(grad_scaled * silu * up_lin, axis=1, keepdims=True)
    scaled_hidden = (gates * silu * up_lin).astype(bf16)
    grad_act = gates * grad_scaled
    grad_gate_lin = (grad_act * up_lin * sigmoid * (1.0 + gate_lin * (1.0 - sigmoid))).astype(bf16)
    grad_up_lin = (grad_act * silu).astype(bf16)
    y_ref[0] = dot(scaled_hidden, w_down, 1, 1).astype(bf16).reshape(y_ref.shape[1:])
    dx = dot(grad_gate_lin, w_gate, 1, 1) + dot(grad_up_lin, w_up, 1, 1)
    dx_ref[0, :, :, :width] = dx.astype(bf16).reshape(dx_ref.shape[1:3] + (width,))
    lane = lax.broadcasted_iota(jnp.int32, (slots, LANES), 1)
    number = where_ref[2] + first + i
    tail = jnp.where(lane == number, grad_gates, 0.0).astype(bf16)
    dx_ref[0, :, :, width:] = tail.reshape(dx_ref.shape[1:3] + (LANES,))
    for which, (left, right) in enumerate(((x, grad_gate_lin), (x, grad_up_lin), (g, scaled_hidden))):
        grad = dot(left, right, 0, 0).astype(bf16)
        for plane in range(planes):
            for q in range(8):
                row = (plane * 2 + q // 4) * deep
                col = q % 4 * quarter
                dw_ref[plane, q, 0, which] = grad[row:row + deep, col:col + quarter]


def shards(
    tokens,
    lengths,
    routes,
    gain_attn,
    w_query,
    w_keyvalue,
    w_out,
    gain_mixer,
    w_router,
    w_gate,
    w_up,
    w_down,
    out_grad,
):
    nd, nt = lax.axis_size("dp"), lax.axis_size("tensor")
    dp_id, t_id = lax.axis_index("dp"), lax.axis_index("tensor")
    rows, width = tokens.shape
    group_rows, top_count = routes.shape
    seq_count = lengths.shape[0]
    seq_len = group_rows // seq_count
    experts = w_router.shape[1]
    local = experts // 8
    planes = nd // 2
    deep = width // nd
    hidden = w_gate.shape[2] * nt
    capacity = (rows * top_count * 17 + experts * 16 - 1) // (experts * 16)
    cap = -(-capacity // 16) * 16
    plane_id = (dp_id % 2) * nt + t_id
    core = t_id % 2
    z_groups = [[x + 2 * z for z in range(planes)] for x in range(2)]
    group_sizes = (1,) * local
    groups = len(group_sizes)
    plane_groups = [[(z * 2 + x) * nt + t for x in range(2) for t in range(nt)] for z in range(planes)]

    quarter = hidden // nt

    def for_plane(w):
        return jnp.transpose(w.reshape(deep, 8, local, quarter), (1, 2, 0, 3))

    w_send = jnp.stack([for_plane(w_gate), for_plane(w_up), for_plane(w_down)], axis=2)
    q_cols, kv_cols = w_query.shape[1], w_keyvalue.shape[2]
    cut = q_cols + 2 * kv_cols
    w_mine = jnp.concatenate([w_query, w_keyvalue[:, 0], w_keyvalue[:, 1], w_out], axis=1)
    pushes = 3 * planes + 2 * (planes - 1)
    hbm = pl.BlockSpec(memory_space=pl.ANY)
    dealt_shape = sds((8, 3, deep, quarter), bf16)
    early = 2
    dealt_early = pl.pallas_call(
        deal_kernel,
        out_shape=[dealt_shape] * early,
        in_specs=[hbm], out_specs=[hbm] * early,
        scratch_shapes=[pltpu.SemaphoreType.DMA((early, 8)), pltpu.SemaphoreType.DMA((early, 8))],
        compiler_params=pltpu.CompilerParams(
            vmem_limit_bytes=VMEM_LIMIT, collective_id=1, has_side_effects=True
        ),
        cost_estimate=pl.CostEstimate(flops=10**6, bytes_accessed=20 * 2**20, transcendentals=0),
    )(w_send)
    later = tuple(range(early, local))
    normed_rows, w_attn, ranks, *dealt = pl.pallas_call(
        functools.partial(gather_kernel, later),
        out_shape=[
            sds((2 * rows, width), bf16), sds((2, nd, deep, cut + q_cols), bf16), sds((2, nt, 64, rows), bf16),
        ]
        + [dealt_shape] * len(later),
        in_specs=[SM] + [VM] * 4 + [hbm], out_specs=[VM] * 3 + [hbm] * len(later),
        scratch_shapes=[
            pltpu.SemaphoreType.DMA((pushes,)), pltpu.SemaphoreType.DMA((2, nd)), pltpu.SemaphoreType.DMA((4,)),
            pltpu.SemaphoreType.DMA((len(later), 8)), pltpu.SemaphoreType.DMA((len(later), 8)),
        ],
        compiler_params=pltpu.CompilerParams(
            vmem_limit_bytes=VMEM_LIMIT, collective_id=0, has_side_effects=True
        ),
        cost_estimate=pl.CostEstimate(flops=10**7, bytes_accessed=100 * 2**20, transcendentals=0),
    )(lengths, tokens, gain_attn[None, :], routes.T, after(w_mine, *dealt_early), w_send)

    w_groups = []
    for n, piece in enumerate([*dealt_early, *dealt]):
        if n > 1:
            piece = after(piece, w_groups[n - 2][0])
        w_groups.append(gather_z(piece, planes, z_groups, False))

    positions = jnp.arange(group_rows, dtype=jnp.int32) % seq_len
    live = positions < jnp.repeat(lengths, seq_len)
    own_start = t_id * rows
    live_own = lax.dynamic_slice_in_dim(live, own_start, rows, 0).astype(f32)[:, None]
    routes_own = lax.dynamic_slice_in_dim(routes, own_start, rows, 0)
    lane_ids = jnp.arange(LANES, dtype=jnp.int32)
    hits_own = jnp.any(routes_own[:, :, None] == lane_ids[None, None, :], axis=1).astype(f32) * live_own
    router = jnp.pad(w_router, ((0, 0), (0, LANES - experts)))
    router_t = jnp.pad(w_router.T.reshape(8, local, width), ((0, 0), (0, 8 - local), (0, 0))).reshape(64, width)

    half_head = HD // 2
    exponent = 2.0 * jnp.arange(half_head, dtype=f32) / HD
    angles = jnp.arange(seq_len, dtype=f32)[:, None] * jnp.exp(-math.log(rope_base) * exponent)[None, :]
    cosine, sine = jnp.cos(angles), jnp.sin(angles)
    cos_table = jnp.concatenate([cosine] * 4, axis=1)
    sin_table = jnp.concatenate([-sine, sine] * 2, axis=1)

    place = jnp.stack(
        [core, plane_id, plane_id * local, t_id, dp_id // 2]
    ).astype(jnp.int32)
    length = lax.dynamic_slice_in_dim(lengths, own_start // seq_len, 1, 0)[0]
    where_attn = jnp.stack([core, length]).astype(jnp.int32)

    out_late = after(out_grad, w_attn)
    out_y, out_x = hop_y(out_late), hop_x(out_late)
    q_width, k_width = 2 * q_cols, 2 * kv_cols
    heads = q_width // HD
    q, k, v, ctx, lse, keep, send = call(
        attend_kernel,
        [
            sds((seq_len, q_width), bf16), sds((seq_len, k_width), bf16), sds((seq_len, k_width), bf16),
            sds((seq_len, q_width), bf16), sds((heads, seq_len), f32),
            sds((rows, width), bf16), sds((rows, width), bf16),
        ],
        12 * 10**9, 16 * 2**20,
        in_specs=[SM] + [VM] * 4, out_specs=[VM] * 7,
    )(where_attn, after(normed_rows, w_groups[0][0]), w_attn, cos_table, sin_table)
    got = hop_c(send)
    hidden_own, normed_mix, inverse_mix = call(
        mix_norm_kernel,
        [sds((rows, width), f32), sds((rows, width), bf16), sds((rows, 1), f32)],
        10**7, 8 * 2**20,
        in_specs=[VM] * 5, out_specs=[VM] * 3,
    )(tokens, after(keep, out_y, out_x), got, live_own, gain_mixer[None, :])

    slots_shape = (local, 8, cap, width)

    def ranks_spec(stride, start):
        def index(i, where):
            j = stride * i + start
            return (j // 4, lax.bitwise_xor(where[3], j % 4), 0, 0)
        return pl.BlockSpec((1, 1, 64, rows), index)

    def whole(a):
        return pl.BlockSpec(a.shape, lambda i, where: (0,) * a.ndim)

    def dispatch(blocks, gated):
        out_specs = [pl.BlockSpec((local, 1, cap, width), lambda i, where: (0, i, 0, 0))]
        out_shape = [sds(slots_shape, bf16)]
        scratch = [pltpu.VMEM((rows, width), bf16)]
        extra = []
        if gated:
            extra = [router_t]
            out_specs.append(pl.BlockSpec((local, 1, cap, 1), lambda i, where: (0, i, 0, 0)))
            out_shape.append(sds((local, 8, cap, 1), f32))
            scratch.append(pltpu.VMEM((64, rows), f32))
        return call(
            functools.partial(dispatch_gates_kernel if gated else dispatch_kernel, local, cap),
            out_shape, 5 * 10**9, 20 * 2**20,
            grid_spec=pltpu.PrefetchScalarGridSpec(
                num_scalar_prefetch=1, grid=(8,),
                in_specs=[whole(b) for b in blocks] + [ranks_spec(1, 0)] + [whole(e) for e in extra],
                out_specs=out_specs, scratch_shapes=scratch,
            ),
        )(place, *blocks, ranks, *extra)

    (grads_in,) = dispatch(gather_plane(out_late, out_y, out_x), False)
    rows_in, gates_in = dispatch(gather_plane(normed_mix), True)

    ys, dxs, dws = [], [], []
    first = 0
    for per, sources in zip(group_sizes, w_groups):
        def slot_spec(last, first=first, per=per):
            return pl.BlockSpec((1, 8, cap, last), lambda e, where: (first + e, 0, 0, 0))

        def out_spec(last):
            return pl.BlockSpec((1, 8, cap, last), lambda e, where: (e, 0, 0, 0))

        y, dx, dw = call(
            functools.partial(expert_kernel, first, len(sources)),
            [
                sds((per, 8, cap, width), bf16), sds((per, 8, cap, width + LANES), bf16),
                sds((planes, 8, per, 3, deep, quarter), bf16),
            ],
            per * 18 * 8 * cap * width * hidden, per * 20 * 2**20,
            grid_spec=pltpu.PrefetchScalarGridSpec(
                num_scalar_prefetch=1, grid=(per,),
                in_specs=[slot_spec(width), slot_spec(width), slot_spec(1)]
                + [pl.BlockSpec(memory_space=pl.ANY)] * len(sources),
                out_specs=[
                    out_spec(width), out_spec(width + LANES),
                    pl.BlockSpec((planes, 8, 1, 3, deep, quarter), lambda e, where: (0, 0, e, 0, 0, 0)),
                ],
                scratch_shapes=[
                    pltpu.VMEM((2, planes, 8, 3, deep, quarter), bf16), pltpu.SemaphoreType.DMA((2, len(sources))),
                ],
            ),
        )(after(place, *dws[-1:], ), rows_in, grads_in, gates_in, *sources)
        ys.append(y)
        dxs.append(dx)
        dws.append(dw)
        first += per

    def combine(values, start):
        last = values[0].shape[-1]
        return call(
            functools.partial(combine_kernel, local, cap, groups),
            sds((4, rows, last), bf16), 25 * 10**8, 12 * 2**20,
            grid_spec=pltpu.PrefetchScalarGridSpec(
                num_scalar_prefetch=1, grid=(4,),
                in_specs=[
                    pl.BlockSpec((v.shape[0], 1, cap, last), lambda i, where: (0, 2 * i + start, 0, 0)) for v in values
                ] + [ranks_spec(2, start)],
                out_specs=pl.BlockSpec((1, rows, last), lambda i, where: (i, 0, 0)),
            ),
        )(place, *values, ranks)

    dx_send = combine(dxs, 1)
    dx_keep = combine(dxs, 0)
    grad_terms = scatter_plane(dx_send, dx_keep)
    y_send = combine([after(v, dx_keep) for v in ys], 1)
    y_keep = combine([after(v, dx_keep) for v in ys], 0)
    grad_hidden, grad_branch, router_grad, gain_mix_grad = call(
        mix_back_kernel,
        [
            sds((rows, width), f32), sds((rows, width), bf16), sds((experts, width), f32), sds((1, width), f32),
        ],
        10**8, 12 * 2**20,
        in_specs=[VM] * 11, out_specs=[VM] * 4,
    )(
        after(normed_mix, y_send, y_keep), hidden_own, inverse_mix, *grad_terms, out_grad, router, hits_own, live_own,
        gain_mixer[None, :],
    )
    branch_peer = hop_c(grad_branch)

    out_terms = scatter_plane(after(y_send, grad_branch), y_keep)
    mixed = (hidden_own + sum(term.astype(f32) for term in out_terms)).astype(bf16)

    dw_attn, keep_back, send_back = call(
        attend_back_kernel,
        [
            sds((2, nd, deep, cut + q_cols), bf16), sds((rows, width), bf16), sds((rows, width), bf16),
        ],
        25 * 10**9, 24 * 2**20,
        in_specs=[SM] + [VM] * 11, out_specs=[VM] * 3,
        scratch_shapes=[
            pltpu.VMEM((seq_len, width), bf16),
            pltpu.VMEM((seq_len, q_width), bf16), pltpu.VMEM((seq_len, 2 * cut), bf16),
            pltpu.VMEM((seq_len, LANES), f32), pltpu.VMEM((seq_len, LANES), f32),
        ],
    )(
        where_attn, normed_rows, grad_branch, branch_peer, w_attn, cos_table, sin_table,
        q, k, v, ctx, lse,
    )
    got_back = hop_c(send_back)
    grad_tokens, gain_attn_grad = call(
        token_back_kernel,
        [sds((rows, width), bf16), sds((1, width), f32)],
        10**7, 8 * 2**20,
        in_specs=[VM] * 5, out_specs=[VM] * 2,
    )(tokens, keep_back, got_back, grad_hidden, gain_attn[None, :])

    grad_pieces = []
    for dw in dws:
        mine = lax.psum_scatter(dw, "dp", scatter_dimension=0, axis_index_groups=z_groups)
        grad_pieces.append(
            lax.all_to_all(mine, BOTH, 0, 0, tiled=True, axis_index_groups=plane_groups)
        )

    def to_owner(which):
        parts = [piece[:, :, which].astype(f32) for piece in grad_pieces]
        whole_grad = jnp.concatenate(parts, axis=1).reshape(experts, deep, hidden // nt)
        return jnp.transpose(whole_grad, (1, 0, 2))

    attn_grad = add16(dw_attn[0], hop_y(dw_attn[1])).reshape(planes, 2, deep, cut + q_cols)
    x_id = dp_id % 2
    attn_grad = add16(
        lax.dynamic_index_in_dim(attn_grad, x_id, 1, False),
        hop_x(lax.dynamic_index_in_dim(attn_grad, 1 - x_id, 1, False)),
    )
    attn_grad = sum_z(attn_grad, planes, dp_id // 2, z_groups)
    grad_query = attn_grad[:, :q_cols]
    grad_keyval = attn_grad[:, q_cols:cut].reshape(deep, 2, kv_cols)
    grad_out = attn_grad[:, cut:]

    router_all = sum_all(jnp.concatenate([router_grad, gain_mix_grad], axis=0), nd)
    gain_attn_all = sum_all(gain_attn_grad, nd)
    return (
        mixed,
        grad_tokens,
        gain_attn_all[0],
        grad_query,
        grad_keyval,
        grad_out,
        router_all[experts],
        router_all[:experts].T,
        to_owner(0),
        to_owner(1),
        to_owner(2),
    )


def solution(mesh):
    placed = (
        P(("dp", "tensor"), None),
        P("dp"),
        P("dp", None),
        P(),
        P("dp", "tensor"),
        P("dp", None, "tensor"),
        P("dp", "tensor"),
        P(),
        P(),
        P("dp", None, "tensor"),
        P("dp", None, "tensor"),
        P("dp", None, "tensor"),
        P(("dp", "tensor"), None),
    )
    return jax.shard_map(
        shards,
        mesh=mesh,
        in_specs=placed,
        out_specs=(
            P(("dp", "tensor"), None),
            P(("dp", "tensor"), None),
            P(),
            P("dp", "tensor"),
            P("dp", None, "tensor"),
            P("dp", "tensor"),
            P(),
            P(),
            P("dp", None, "tensor"),
            P("dp", None, "tensor"),
            P("dp", None, "tensor"),
        ),
        check_vma=False,
    )
```

```python
import functools
import math

import jax
import jax.numpy as jnp
from jax import lax
from jax.experimental import pallas as pl
from jax.experimental.pallas import tpu as pltpu
from jax.sharding import PartitionSpec as P

HD = 64
LANES = 128
epsilon = 1e-06
rope_base = 10000.0
bf16 = jnp.bfloat16
f32 = jnp.float32
BOTH = ("dp", "tensor")
VMEM_LIMIT = 60 * 1024 * 1024
QBLK = 256


def dot(a, b, ca, cb):
    return lax.dot_general(a, b, (((ca,), (cb,)), ((), ())), preferred_element_type=f32)


def call(kernel, out_shape, flops, nbytes, **kw):
    return pl.pallas_call(
        kernel,
        out_shape=out_shape,
        compiler_params=pltpu.CompilerParams(vmem_limit_bytes=VMEM_LIMIT),
        cost_estimate=pl.CostEstimate(flops=flops, bytes_accessed=nbytes, transcendentals=0),
        **kw,
    )


def sds(shape, dtype):
    return jax.ShapeDtypeStruct(shape, dtype)


VM = pl.BlockSpec(memory_space=pltpu.VMEM)
SM = pl.BlockSpec(memory_space=pltpu.SMEM)


def hop(x, dp_bit, t_bits):
    nd, nt = lax.axis_size("dp"), lax.axis_size("tensor")
    pairs = [
        (d * nt + t, (d ^ dp_bit) * nt + (t ^ t_bits)) for d in range(nd) for t in range(nt)
    ]
    return lax.ppermute(x, BOTH, pairs)


def hop_c(x):
    return hop(x, 0, 1)


def hop_y(x):
    return hop(x, 0, 2)


def hop_x(x):
    return hop(x, 1, 0)


def after(x, *others):
    return lax.optimization_barrier((x, *others))[0]


def gather_weights(x, weight_groups):
    return lax.all_gather(x, "dp", axis_index_groups=weight_groups)


def swap_halves(v):
    lane = lax.broadcasted_iota(jnp.int32, v.shape, 1)
    left = pltpu.roll(v, LANES - HD // 2, 1)
    right = pltpu.roll(v, HD // 2, 1)
    return jnp.where(lane % HD < HD // 2, left, right)


def in_head(tile, h):
    lane = lax.broadcasted_iota(jnp.int32, tile.shape, 1)
    return (lane < HD) if h == 0 else (lane >= HD)


def only_head(tile, h):
    return jnp.where(in_head(tile, h), tile, jnp.zeros_like(tile))


def spread_head(tile, h):
    wide = tile.astype(f32)
    return jnp.where(in_head(wide, h), wide, pltpu.roll(wide, HD, 1)).astype(tile.dtype)


def stacked(tile):
    return jnp.concatenate([only_head(tile, 0), only_head(tile, 1)], axis=0)


def key_limit(start, rows, length):
    column = lax.broadcasted_iota(jnp.int32, (1, 2 * rows), 1)
    position = start + jnp.where(column >= rows, column - rows, column)
    return jnp.minimum(position, length - 1)


def scores_t(kd, qm, limit):
    raw = dot(kd, qm, 1, 1) * (1.0 / math.sqrt(HD))
    key = lax.broadcasted_iota(jnp.int32, raw.shape, 0)
    return jnp.where(key <= limit, raw, -1e30)


def attend_kernel(
    where_ref, rows, w, cos, sin,
    q_ref, k_ref, v_ref, ctx_ref, lse_ref, keep_ref, send_ref,
):
    core, length = where_ref[0], where_ref[1]
    seq, width = rows.shape
    half = seq // 2
    kw = k_ref.shape[1] // 2
    qw = 2 * kw
    cut = qw + 2 * kw
    for blk in range(seq // QBLK):
        sl = slice(blk * QBLK, (blk + 1) * QBLK)
        c, s = cos[sl], sin[sl]
        for y in range(2):
            pre = dot(rows[sl], w[y, :, :, :cut].reshape(width, cut), 1, 0)
            for tile in range((qw + kw) // LANES):
                col = pre[:, tile * LANES:(tile + 1) * LANES]
                turned = (col * c + swap_halves(col) * s).astype(bf16)
                if tile * LANES < qw:
                    q_ref[sl, y * qw + tile * LANES:y * qw + (tile + 1) * LANES] = turned
                else:
                    at = y * kw + tile * LANES - qw
                    k_ref[sl, at:at + LANES] = turned
            v_ref[sl, y * kw:(y + 1) * kw] = pre[:, qw + kw:].astype(bf16)
    for g in range(2 * qw // LANES):
        kv = slice(g // 2 * LANES, (g // 2 + 1) * LANES)
        cols = slice(g * LANES, (g + 1) * LANES)
        kd = spread_head(k_ref[:, kv], g % 2)
        vd_t = spread_head(v_ref[:, kv], g % 2).T
        for blk in range(seq // QBLK):
            top = (blk + 1) * QBLK
            sl = slice(blk * QBLK, top)
            s = scores_t(kd[:top], stacked(q_ref[sl, cols]), key_limit(blk * QBLK, QBLK, length))
            peak = jnp.max(s, axis=0, keepdims=True)
            e = jnp.exp(s - peak)
            total = jnp.sum(e, axis=0, keepdims=True)
            p = (e * (1.0 / total)).astype(bf16)
            ctx = dot(vd_t[:, :top], p, 1, 0).T
            tile = jnp.where(in_head(ctx[:QBLK], 0), ctx[:QBLK], ctx[QBLK:])
            ctx_ref[sl, cols] = tile.astype(bf16)
            lse = peak + jnp.log(total)
            lse_ref[2 * g:2 * g + 1, sl] = lse[:, :QBLK]
            lse_ref[2 * g + 1:2 * g + 2, sl] = lse[:, QBLK:]
    for out_ref, side in ((send_ref, 1 - core), (keep_ref, core)):
        at = pl.ds(pl.multiple_of(side * half, half), half)
        out = dot(ctx_ref[at, :qw], w[0, :, :, cut:].reshape(width, qw), 1, 1)
        out += dot(ctx_ref[at, qw:], w[1, :, :, cut:].reshape(width, qw), 1, 1)
        out_ref[...] = out.astype(bf16)


def attend_back_kernel(
    where_ref, rows, gb_ref, w, cos, sin, q_ref, k_ref, v_ref, ctx_ref, lse_ref,
    dw_ref, keep_ref, send_ref,
    gc_ref, dqkv_ref, dk_ref, dv_ref,
):
    core, length = where_ref[0], where_ref[1]
    seq, width = rows.shape
    half = seq // 2
    kw = k_ref.shape[1] // 2
    qw = 2 * kw
    cut = qw + 2 * kw
    per_dp = dw_ref.shape[1:3]
    at_own = pl.ds(pl.multiple_of(core * half, half), half)
    at_peer = pl.ds(pl.multiple_of((1 - core) * half, half), half)
    for y in range(2):
        part = slice(y * qw, (y + 1) * qw)
        gc_ref[:, part] = dot(gb_ref[...], w[y, :, :, cut:].reshape(width, qw), 1, 0).astype(bf16)
        dw_ref[y, :, :, cut:] = dot(gb_ref[...], ctx_ref[:, part], 0, 0).astype(bf16).reshape(per_dp + (qw,))
    scale = 1.0 / math.sqrt(HD)
    folded = None
    for g in range(2 * qw // LANES):
        y = g // 2
        kv = slice(y * LANES, (y + 1) * LANES)
        cols = slice(g * LANES, (g + 1) * LANES)
        kd = spread_head(k_ref[:, kv], g % 2)
        kd_t = kd.T
        vd = spread_head(v_ref[:, kv], g % 2)
        for blk in reversed(range(seq // QBLK)):
            top = (blk + 1) * QBLK
            sl = slice(blk * QBLK, top)
            qm = stacked(q_ref[sl, cols])
            gm = stacked(gc_ref[sl, cols])
            s = scores_t(kd[:top], qm, key_limit(blk * QBLK, QBLK, length))
            lse = jnp.concatenate([lse_ref[2 * g:2 * g + 1, sl], lse_ref[2 * g + 1:2 * g + 2, sl]], axis=1)
            p = jnp.exp(s - lse)
            gw = dot(vd[:top], gm, 1, 1)
            centre = jnp.sum(p * gw, axis=0, keepdims=True)
            ds = (p * (gw - centre) * scale).astype(bf16)
            dv = dot(p.astype(bf16), gm, 1, 0)
            dk = dot(ds, qm, 1, 0)
            dq = dot(kd_t[:, :top], ds, 1, 0).T
            if top == seq:
                dk_ref[...] = dk
                dv_ref[...] = dv
            else:
                dk_ref[:top] += dk
                dv_ref[:top] += dv
            tile = jnp.where(in_head(dq[:QBLK], 0), dq[:QBLK], dq[QBLK:])
            back = tile * cos[sl] - swap_halves(tile) * sin[sl]
            at = y * cut + g % 2 * LANES
            dqkv_ref[sl, at:at + LANES] = back.astype(bf16)
        dk_all = dk_ref[...] + pltpu.roll(dk_ref[...], HD, 1)
        dv_all = dv_ref[...] + pltpu.roll(dv_ref[...], HD, 1)
        if g % 2 == 0:
            folded = (dk_all, dv_all)
        else:
            dk_pair = jnp.where(in_head(dk_all, 0), folded[0], dk_all)
            dv_pair = jnp.where(in_head(dv_all, 0), folded[1], dv_all)
            at = y * cut + qw
            back = dk_pair * cos[...] - swap_halves(dk_pair) * sin[...]
            dqkv_ref[:, at:at + LANES] = back.astype(bf16)
            dqkv_ref[:, at + LANES:at + 2 * LANES] = dv_pair.astype(bf16)
            part = slice(y * cut, (y + 1) * cut)
            dw_ref[y, :, :, :cut] = dot(rows[...], dqkv_ref[:, part], 0, 0).astype(bf16).reshape(per_dp + (cut,))
    for out_ref, at in ((send_ref, at_peer), (keep_ref, at_own)):
        out = dot(dqkv_ref[at, :cut], w[0, :, :, :cut].reshape(width, cut), 1, 1)
        out += dot(dqkv_ref[at, cut:], w[1, :, :, :cut].reshape(width, cut), 1, 1)
        out_ref[...] = out.astype(bf16)


def own_place():
    return lax.axis_index("dp") % 2 * 4 + lax.axis_index("tensor")


def plane_devices():
    d, p = lax.axis_index("dp"), own_place()
    return [{"dp": d + ((p ^ j) // 4 - p // 4), "tensor": (p ^ j) % 4} for j in range(8)]


def deal_out(p, plane_peers, w_send, numbers, dealt, send_sem, recv_sem):
    copies = []
    for i, e in enumerate(numbers):
        for j in (6, 7, 2, 4, 3, 5, 1):
            copies.append(
                pltpu.make_async_remote_copy(
                    src_ref=w_send.at[p ^ j, e], dst_ref=dealt[i].at[j], send_sem=send_sem.at[i, j],
                    recv_sem=recv_sem.at[i, j], device_id=plane_peers[j], device_id_type=pl.DeviceIdType.MESH,
                )
            )
        copies.append(pltpu.make_async_copy(w_send.at[p, e], dealt[i].at[0], send_sem.at[i, 0]))
    for copy in copies:
        copy.start()
    return copies


def deal_kernel(w_send, *refs):
    dealt, (send_sem, recv_sem) = refs[:-2], refs[-2:]
    p = own_place()
    peers = plane_devices()
    barrier = pltpu.get_barrier_semaphore()
    for peer in peers[1:]:
        pl.semaphore_signal(barrier, inc=1, device_id=peer, device_id_type=pl.DeviceIdType.MESH)
    pl.semaphore_wait(barrier, 7)
    for copy in deal_out(p, peers, w_send, range(len(dealt)), dealt, send_sem, recv_sem):
        copy.wait()


def rank_rows(lengths, routes_t, block, ranks_ref):
    blocks, wide = ranks_ref.shape[1:3]
    seq_len = block * blocks // lengths.shape[0]
    local = wide // 16
    row = lax.broadcasted_iota(jnp.int32, (wide, block), 0)
    number = jnp.where(row % 8 < local, row // 8 * local + row % 8, -1)
    low = lax.broadcasted_iota(jnp.int32, (block, block), 0)
    high = lax.broadcasted_iota(jnp.int32, (block, block), 1)
    before = (low < high).astype(f32).astype(bf16)
    for b in range(blocks):
        at = slice(b * block, (b + 1) * block)
        position = lax.broadcasted_iota(jnp.int32, (wide, block), 1) + b * block % seq_len
        hit = jnp.zeros((wide, block), jnp.bool_)
        for k in range(routes_t.shape[0]):
            hit = hit | (routes_t[k:k + 1, at] == number)
        hit = hit & (position < lengths[b * block // seq_len])
        earlier = dot(hit.astype(f32).astype(bf16), before, 1, 0)
        ranks_ref[0, b] = jnp.where(hit, earlier, -1.0).astype(bf16)


def gather_kernel(later, lengths, tokens, gain, routes_t, w_mine, w_send, rows_ref, w_ref, ranks_ref, *refs):
    dealt, (send_sem, recv_sem, row_sem, deal_send, deal_recv) = refs[:-5], refs[-5:]
    d, t = lax.axis_index("dp"), lax.axis_index("tensor")
    planes = w_ref.shape[1] // 2
    half = tokens.shape[0]
    z, x, core = d // 2, d % 2, t % 2

    def device(dp, tensor):
        return {"dp": dp, "tensor": tensor}

    def plane(dz):
        return lax.rem(z + dz, planes)

    x_peer, y_peer = device(z * 2 + 1 - x, t), device(d, (t + 2) % 4)
    core_peer = device(d, t + 1 - 2 * core)
    z_peers = [device(plane(dz) * 2 + x, t) for dz in range(1, planes)]
    barrier = pltpu.get_barrier_semaphore()
    p = own_place()
    plane_peers = plane_devices()
    for peer in [*z_peers, x_peer, *plane_peers[1:4], *plane_peers[5:]]:
        pl.semaphore_signal(barrier, inc=1, device_id=peer, device_id_type=pl.DeviceIdType.MESH)
    pl.semaphore_wait(barrier, planes + 6)

    copies = []

    def push(source, side, dp, peer):
        copy = pltpu.make_async_remote_copy(
            src_ref=source, dst_ref=w_ref.at[side, dp], send_sem=send_sem.at[len(copies)],
            recv_sem=recv_sem.at[side, dp], device_id=peer, device_id_type=pl.DeviceIdType.MESH,
        )
        copy.start()
        copies.append(copy)

    def arrive(side, dp):
        slot = w_ref.at[side, dp]
        pltpu.make_async_remote_copy(
            src_ref=slot, dst_ref=slot, send_sem=send_sem.at[0], recv_sem=recv_sem.at[side, dp],
            device_id=x_peer, device_id_type=pl.DeviceIdType.MESH,
        ).wait_recv()

    for peer in z_peers:
        push(w_mine, 0, d, peer)
    push(w_mine, 0, d, x_peer)
    push(w_mine, 1, d, y_peer)
    pair, last = dealt
    deals = deal_out(p, plane_peers, w_send, later, (pair.at[0], pair.at[1], last), deal_send, deal_recv)
    values = tokens[...].astype(f32)
    inverse = lax.rsqrt(jnp.mean(values * values, axis=1, keepdims=True) + epsilon)
    at = pl.ds(pl.multiple_of(core * half, half), half)
    rows_ref[at] = (values * inverse * gain[...]).astype(bf16)
    row_copy = pltpu.make_async_remote_copy(
        src_ref=rows_ref.at[at], dst_ref=rows_ref.at[at], send_sem=row_sem.at[0], recv_sem=row_sem.at[1],
        device_id=core_peer, device_id_type=pl.DeviceIdType.MESH,
    )
    row_copy.start()
    w_ref[0, d] = w_mine[...]
    rank_rows(lengths, routes_t, half, ranks_ref)
    rank_copy = pltpu.make_async_remote_copy(
        src_ref=ranks_ref.at[0], dst_ref=ranks_ref.at[1], send_sem=row_sem.at[2], recv_sem=row_sem.at[3],
        device_id=plane_peers[4], device_id_type=pl.DeviceIdType.MESH,
    )
    rank_copy.start()
    near = [plane(dz) * 2 + x for dz in range(planes)]
    over = [plane(dz) * 2 + 1 - x for dz in range(planes)]

    def turn(dz):
        arrive(0, over[dz])
        if dz < planes // 2:
            push(w_ref.at[0, over[dz]], 1, over[dz], y_peer)
        arrive(1, near[dz])
        if dz >= planes // 2:
            push(w_ref.at[1, near[dz]], 1, near[dz], x_peer)

    for dz in range(1, planes):
        arrive(0, near[dz])
        push(w_ref.at[0, near[dz]], 0, near[dz], x_peer)
        push(w_ref.at[0, near[dz]], 1, near[dz], y_peer)
        turn(dz - 1)
    turn(planes - 1)
    for dz in range(planes):
        arrive(1, over[dz])
    for copy in copies:
        copy.wait_send()
    row_copy.wait()
    rank_copy.wait()
    for copy in deals:
        copy.wait()


def masked_shares(logits, hit, axis):
    peak = jnp.max(jnp.where(hit, logits, -1e30), axis=axis, keepdims=True)
    e = jnp.where(hit, jnp.exp(jnp.where(hit, logits - peak, 0.0)), 0.0)
    total = jnp.sum(e, axis=axis, keepdims=True)
    return e / jnp.where(total > 0.0, total, 1.0)


def split16(v):
    high = v.astype(bf16)
    return high, (v - high.astype(f32)).astype(bf16)


def neighbours():
    peers = plane_devices()
    return peers[4], peers[2], peers[1]


def greet(peers):
    barrier = pltpu.get_barrier_semaphore()
    for peer in peers:
        pl.semaphore_signal(barrier, inc=1, device_id=peer, device_id_type=pl.DeviceIdType.MESH)
    pl.semaphore_wait(barrier, len(peers))


def remote(source, target, send_sem, recv_sem, peer):
    return pltpu.make_async_remote_copy(
        src_ref=source, dst_ref=target, send_sem=send_sem, recv_sem=recv_sem,
        device_id=peer, device_id_type=pl.DeviceIdType.MESH,
    )


def block_ranks(ranks, j):
    return ranks[j // 4, lax.axis_index("tensor") ^ (j % 4)].astype(f32)


def own_group():
    return pl.multiple_of(own_place() * 8, 8)


def placing(ranks, cap):
    slot = lax.broadcasted_iota(jnp.int32, (cap, ranks.shape[1]), 0).astype(f32)
    return [(slot == ranks[e:e + 1]).astype(f32) for e in range(ranks.shape[0])]


def mix_kernel(
    local, cap, tokens, keep, send, live, gain, out_own, out_y, out_x, ranks, router_t,
    hidden_ref, normed_ref, inv_ref, gates_ref, x_hbm, g_hbm,
    normed_buf, out_buf, got_ref, stage_ref, ranks_ref, shares_ref,
    send_sem, recv_sem, core_sem, stage_sem,
):
    x_peer, y_peer, core_peer = neighbours()
    greet((x_peer, y_peer, core_peer))
    rows = tokens.shape[0]
    low, high = pl.ds(0, rows // 2), pl.ds(rows // 2, rows // 2)
    sent = []

    def push(kind, source, target, slot, peer):
        copy = remote(source, target, send_sem.at[kind, slot], recv_sem.at[kind, slot], peer)
        copy.start()
        sent.append(copy)

    def arrive(kind, target, slot):
        remote(target, target, send_sem.at[kind, slot], recv_sem.at[kind, slot], x_peer).wait_recv()

    core_copy = remote(send, got_ref, core_sem.at[0], core_sem.at[1], core_peer)
    core_copy.start()
    push(1, out_y.at[low], out_buf.at[6, low], 6, x_peer)
    push(1, out_x.at[high], out_buf.at[6, high], 8, y_peer)
    push(1, out_own, out_buf.at[1], 1, core_peer)
    push(1, out_y, out_buf.at[3], 3, core_peer)
    push(1, out_x, out_buf.at[5], 5, core_peer)
    core_copy.wait()
    branch = keep[...].astype(f32) + got_ref[...].astype(f32)
    hidden = tokens[...].astype(f32) + live[...] * branch
    inverse = lax.rsqrt(jnp.mean(hidden * hidden, axis=1, keepdims=True) + epsilon)
    hidden_ref[...] = hidden
    inv_ref[...] = inverse
    normed = (hidden * inverse * gain[...]).astype(bf16)
    normed_ref[...] = normed
    normed_buf[0] = normed
    own = normed_buf.at[0]
    push(0, own, normed_buf.at[2], 2, y_peer)
    push(0, own, normed_buf.at[4], 4, x_peer)
    push(0, own, normed_buf.at[1], 1, core_peer)

    staged = []

    def place(kind, j, source):
        n = len(staged)
        if n >= 2:
            staged[n - 2].wait()
        group = own_group()
        ranks_ref[...] = block_ranks(ranks, j)
        places = placing(ranks_ref[pl.ds(group, 8)][:local], cap)
        if kind == 0:
            logits = dot(router_t[...], source[...], 1, 1)
            shares_ref[...] = masked_shares(logits, ranks_ref[...] >= 0.0, 0)
            shares = shares_ref[pl.ds(group, 8)]
            for e in range(local):
                gates_ref[e, j] = jnp.sum(places[e] * shares[e:e + 1], axis=1, keepdims=True)
        matrix = jnp.concatenate([m.astype(bf16) for m in places], axis=0)
        placed = dot(matrix, source[...], 1, 0).astype(bf16)
        stage_ref[n % 2] = placed.reshape(local, cap, -1)
        copy = pltpu.make_async_copy(
            stage_ref.at[n % 2], (x_hbm if kind == 0 else g_hbm).at[:, j], stage_sem.at[n % 2]
        )
        copy.start()
        staged.append(copy)

    place(1, 0, out_own)
    place(1, 2, out_y)
    place(1, 4, out_x)
    place(0, 0, own)
    for j in (1, 3, 5):
        arrive(1, out_buf.at[j], j)
        place(1, j, out_buf.at[j])
    arrive(1, out_buf.at[6, low], 6)
    arrive(1, out_buf.at[6, high], 8)
    push(1, out_buf.at[6], out_buf.at[7], 7, core_peer)
    arrive(0, normed_buf.at[1], 1)
    place(0, 1, normed_buf.at[1])
    place(1, 6, out_buf.at[6])
    arrive(0, normed_buf.at[2], 2)
    push(0, normed_buf.at[2, low], normed_buf.at[6, low], 6, x_peer)
    push(0, normed_buf.at[2], normed_buf.at[3], 3, core_peer)
    arrive(0, normed_buf.at[4], 4)
    push(0, normed_buf.at[4, high], normed_buf.at[6, high], 8, y_peer)
    push(0, normed_buf.at[4], normed_buf.at[5], 5, core_peer)
    arrive(1, out_buf.at[7], 7)
    place(1, 7, out_buf.at[7])
    place(0, 2, normed_buf.at[2])
    place(0, 4, normed_buf.at[4])
    for j in (3, 5):
        arrive(0, normed_buf.at[j], j)
        place(0, j, normed_buf.at[j])
    arrive(0, normed_buf.at[6, low], 6)
    arrive(0, normed_buf.at[6, high], 8)
    push(0, normed_buf.at[6], normed_buf.at[7], 7, core_peer)
    place(0, 6, normed_buf.at[6])
    arrive(0, normed_buf.at[7], 7)
    place(0, 7, normed_buf.at[7])
    for copy in sent:
        copy.wait_send()
    for copy in staged[-2:]:
        copy.wait()


def return_kernel(local, cap, *refs):
    dxs, ys, refs = refs[:local], refs[local:2 * local], refs[2 * local:]
    (
        ranks, normed, hidden_in, inv, out_grad, router, hits, live, gain,
        grad_hidden_ref, branch_ref, router_grad_ref, gain_grad_ref, y_ref,
        load_ref, part_ref, core_ref, total_ref, diag_ref, last_ref, y_part, y_core, ranks_ref,
        load_sem, send_sem, recv_sem, y_send, y_recv, branch_sem,
    ) = refs
    x_peer, y_peer, core_peer = neighbours()
    core = lax.axis_index("tensor") % 2
    greet((x_peer, y_peer, core_peer))
    rows, width = normed.shape
    wide = part_ref.shape[-1]
    half = rows // 2
    low, high = pl.ds(0, half), pl.ds(half, half)
    order = [(0, j) for j in (7, 6, 5, 4, 3, 2, 1, 0)] + [(1, j) for j in (7, 5, 3, 1, 6, 4, 2, 0)]
    depth = load_ref.shape[0]
    sent = []

    def loads(n):
        kind, j = order[n]
        slot = n % depth
        cols = wide if kind == 0 else width
        return [
            pltpu.make_async_copy(
                (ys if kind else dxs)[e].at[j],
                load_ref.at[slot, pl.ds(e * cap, cap), pl.ds(0, cols)], load_sem.at[slot, e],
            )
            for e in range(local)
        ]

    def start(n):
        if n < len(order):
            for copy in loads(n):
                copy.start()

    for n in range(depth - 1):
        start(n)
    done = [0]

    def combined():
        n = done[0]
        done[0] += 1
        start(n + depth - 1)
        for copy in loads(n):
            copy.wait()
        kind, j = order[n]
        ranks_ref[...] = block_ranks(ranks, j)
        places = placing(ranks_ref[pl.ds(own_group(), 8)][:local], cap)
        matrix = jnp.concatenate([m.astype(bf16) for m in places], axis=0)
        values = load_ref[n % depth] if kind == 0 else load_ref[n % depth, :, :width]
        return dot(matrix, values, 0, 0)

    def push(source, target, n, peer):
        copy = remote(source, target, send_sem.at[n], recv_sem.at[n], peer)
        copy.start()
        sent.append(copy)

    def arrive(target, n):
        remote(target, target, send_sem.at[n], recv_sem.at[n], x_peer).wait_recv()

    def far_core(k):
        part_ref[k] = combined().astype(bf16)
        push(part_ref.at[k], core_ref.at[k], k, core_peer)

    def near_core(k):
        mine = combined()
        arrive(core_ref.at[k], k)
        return mine + core_ref[k].astype(f32)

    far_core(3)
    total_ref[2] = near_core(3).astype(bf16)
    push(total_ref.at[2, low], diag_ref.at[0], 4, x_peer)
    push(total_ref.at[2, high], diag_ref.at[1], 5, y_peer)
    far_core(2)
    total_ref[1] = near_core(2).astype(bf16)
    push(total_ref.at[1, low], last_ref.at[0, low], 6, x_peer)
    far_core(1)
    total_ref[0] = near_core(1).astype(bf16)
    push(total_ref.at[0, high], last_ref.at[1, high], 7, y_peer)
    far_core(0)
    part_own = near_core(0).astype(bf16)
    y_copies = []
    total_ref[3] = part_own

    def y_far(k):
        y_part[k] = combined().astype(bf16)
        copy = remote(y_part.at[k], y_core.at[k], y_send.at[k], y_recv.at[k], core_peer)
        copy.start()
        y_copies.append(copy)

    y_far(3)
    y_far(2)
    arrive(diag_ref.at[1], 5)
    total_ref[1, high] = (total_ref[1, high].astype(f32) + diag_ref[1].astype(f32)).astype(bf16)
    push(total_ref.at[1, high], last_ref.at[0, high], 8, x_peer)
    arrive(diag_ref.at[0], 4)
    total_ref[0, low] = (total_ref[0, low].astype(f32) + diag_ref[0].astype(f32)).astype(bf16)
    push(total_ref.at[0, low], last_ref.at[1, low], 9, y_peer)
    y_far(1)
    y_far(0)
    for k in (3, 2, 1, 0):
        mine = combined()
        y_copies[3 - k].wait()
        y_ref[k ^ (own_place() // 2)] = (mine + y_core[k].astype(f32)).astype(bf16)

    hit = hits[...] > 0.0
    shares = masked_shares(dot(normed[...], router[...], 1, 0), hit, 1)
    arrive(last_ref.at[0, low], 6)
    arrive(last_ref.at[1, high], 7)
    arrive(last_ref.at[0, high], 8)
    arrive(last_ref.at[1, low], 9)
    for copy in sent:
        copy.wait_send()

    def summed(lo, hi):
        cols = pl.ds(lo, hi - lo)
        return (
            total_ref[3, :, cols].astype(f32) + last_ref[0, :, cols].astype(f32) + last_ref[1, :, cols].astype(f32)
        )

    grad_shares = jnp.where(hit, summed(width, wide), 0.0)
    grad_chosen = shares * (grad_shares - jnp.sum(shares * grad_shares, axis=1, keepdims=True))
    top, rest = split16(grad_chosen)
    hidden, inverse = hidden_in[...], inv[...]
    grad_mix = summed(0, width) + dot(top, router[...], 1, 1) + dot(rest, router[...], 1, 1)
    weighted = grad_mix * gain[...]
    centre = jnp.mean(hidden * weighted, axis=1, keepdims=True)
    grad_hidden = out_grad[...].astype(f32) + inverse * weighted - hidden * (inverse * inverse * inverse * centre)
    grad_hidden_ref[...] = grad_hidden
    at = pl.ds(pl.multiple_of(core * rows, rows), rows)
    branch_ref[at] = (live[...] * grad_hidden).astype(bf16)
    branch_copy = remote(branch_ref.at[at], branch_ref.at[at], branch_sem.at[0], branch_sem.at[1], core_peer)
    branch_copy.start()
    gain_grad_ref[...] = jnp.sum(grad_mix * hidden * inverse, axis=0, keepdims=True)
    experts = router_grad_ref.shape[0]
    router_grad_ref[...] = (dot(top, normed[...], 0, 0) + dot(rest, normed[...], 0, 0))[:experts]
    branch_copy.wait()


def expert_kernel(expert, local, steps, carry, chained, x_hbm, g_hbm, gates_hbm, *refs):
    sources, refs = refs[:steps], refs[steps:]
    if carry:
        (up_from, down_from), refs = refs[:2], refs[2:]
    if expert % 2:
        refs = refs[1:]
    if carry:
        (up_to, down_to), refs = refs[3:5], refs[:3] + refs[5:]
    y_hbm, dx_hbm, dw_hbm, x_ref, g_ref, gates_ref, w_buf, y_ref, dx_ref, dw_ref, in_sem, w_sem, out_sem, z_sem = refs
    d, t, p = lax.axis_index("dp"), lax.axis_index("tensor"), own_place()
    members, _, _, deep, quarter = w_buf.shape
    blocks = [(dp // 2, dp % 2 * 4) for dp in range(2 * members)]
    z = d // 2
    if carry:
        above = {"dp": lax.rem(z + 1, members) * 2 + d % 2, "tensor": t}
        below = {"dp": lax.rem(z + members - 1, members) * 2 + d % 2, "tensor": t}
        greet((above, below))
        up = remote(up_from, up_to, z_sem.at[0], z_sem.at[1], above)
        down = remote(down_from, down_to, z_sem.at[2], z_sem.at[3], below)

        @pl.when((z >= carry - 1) & (z < members - 1))
        def _():
            up.start()

        @pl.when((z > 0) & (z <= members - carry))
        def _():
            down.start()

    def settle():
        @pl.when((z >= carry - 1) & (z < members - 1))
        def _():
            up.wait_send()

        @pl.when(z >= carry)
        def _():
            up.wait_recv()

        @pl.when((z > 0) & (z <= members - carry))
        def _():
            down.wait_send()

        @pl.when(z < members - carry)
        def _():
            down.wait_recv()

    def fetch(act):
        if not chained:
            source = sources[0] if expert in (0, local - 1) else sources[0].at[:, expert - 1]
            act(pltpu.make_async_copy(source, w_buf, w_sem.at[0]))
            return
        act(pltpu.make_async_copy(sources[0], w_buf.at[z], w_sem.at[0]))
        for n, source in enumerate(sources[1:]):
            origin = z - (n // 2 + 1) if n % 2 == 0 else z + n // 2 + 1

            @pl.when((origin >= 0) & (origin < members))
            def _():
                act(pltpu.make_async_copy(source, w_buf.at[origin], w_sem.at[n + 1]))

    x_copy = pltpu.make_async_copy(x_hbm.at[expert], x_ref, in_sem.at[0])
    g_copy = pltpu.make_async_copy(g_hbm.at[expert], g_ref, in_sem.at[1])
    gates_copy = pltpu.make_async_copy(gates_hbm.at[expert], gates_ref, in_sem.at[2])
    x_copy.start()
    fetch(lambda copy: copy.start())
    g_copy.start()
    gates_copy.start()
    slots, width = x_ref.shape[0] * x_ref.shape[1], x_ref.shape[2]

    def weight(which):
        rows = [
            jnp.concatenate([w_buf[at, (side + q) ^ p, which] for q in range(4)], axis=1) for at, side in blocks
        ]
        return jnp.concatenate(rows, axis=0)

    outs = []

    def send(source, target):
        copy = pltpu.make_async_copy(source, target, out_sem.at[len(outs)])
        copy.start()
        outs.append(copy)

    x_copy.wait()
    fetch(lambda copy: copy.wait())
    x = x_ref[...].reshape(slots, width)
    w_gate, w_up, w_down = weight(0), weight(1), weight(2)
    gate_lin = dot(x, w_gate, 1, 0)
    up_lin = dot(x, w_up, 1, 0)
    g_copy.wait()
    gates_copy.wait()
    g = g_ref[...].reshape(slots, width)
    gates = gates_ref[...].reshape(slots, 1)
    grad_scaled = dot(g, w_down, 1, 0)
    sigmoid = 1.0 / (1.0 + jnp.exp(-gate_lin))
    silu = gate_lin * sigmoid
    product = silu * up_lin
    grad_gates = jnp.sum(grad_scaled * product, axis=1, keepdims=True)
    scaled_hidden = (gates * product).astype(bf16)
    grad_act = gates * grad_scaled
    grad_gate_lin = (grad_act * up_lin * sigmoid * (1.0 + gate_lin * (1.0 - sigmoid))).astype(bf16)
    grad_up_lin = (grad_act * silu).astype(bf16)
    y_ref[...] = dot(scaled_hidden, w_down, 1, 1).astype(bf16).reshape(y_ref.shape)
    send(y_ref, y_hbm)
    dx = dot(grad_gate_lin, w_gate, 1, 1) + dot(grad_up_lin, w_up, 1, 1)
    dx_ref[:, :, :width] = dx.astype(bf16).reshape(y_ref.shape)
    lane = lax.broadcasted_iota(jnp.int32, (slots, LANES), 1)
    tail = jnp.where(lane == p * local + expert, grad_gates, 0.0).astype(bf16)
    dx_ref[:, :, width:] = tail.reshape(dx_ref.shape[:2] + (LANES,))
    send(dx_ref, dx_hbm)
    for which, (left, right) in enumerate(((x, grad_gate_lin), (x, grad_up_lin), (g, scaled_hidden))):
        grad = dot(left, right, 0, 0).astype(bf16)
        for dp, (at, side) in enumerate(blocks):
            for q in range(4):
                dw_ref[at, side + q, which] = grad[dp * deep:(dp + 1) * deep, q * quarter:(q + 1) * quarter]
        send(dw_ref.at[:, :, which], dw_hbm.at[:, expert % 2, :, which])
    for copy in outs:
        copy.wait()
    if carry:
        settle()


def all_peers(d, t, planes):
    peers = [{"dp": d, "tensor": t ^ 1}, {"dp": d, "tensor": t ^ 2}]
    bit = 1
    while bit < 2 * planes:
        peers.append({"dp": d ^ bit, "tensor": t})
        bit *= 2
    return peers


def tail_kernel(
    tokens, keep, send, grad_hidden, gain, router_grad, gain_mix_grad, dw, sums,
    out_ref, small_ref, grad_ref, back_ref,
    got_ref, first_ref, second_ref, diag_ref, own_ref, far_ref, small_buf,
    core_sem, send_sem, recv_sem, far_send, far_recv, small_send, small_recv, back_send, back_recv,
):
    d, t = lax.axis_index("dp"), lax.axis_index("tensor")
    planes = dw.shape[1] // 2
    half = planes // 2
    z, x = d // 2, d % 2
    doubling = all_peers(d, t, planes)
    core_peer, y_peer, x_peer = doubling[:3]
    z_peers = [{"dp": lax.rem(z + k, planes) * 2 + x, "tensor": t} for k in range(1, planes)]
    p, plane_peers = own_place(), plane_devices()
    greet((*plane_peers[1:], *z_peers))
    experts = router_grad.shape[0]
    sent = []

    def push(source, target, kind, k, peer):
        copy = remote(source, target, send_sem.at[kind, k], recv_sem.at[kind, k], peer)
        copy.start()
        sent.append(copy)

    def arrive(target, kind, k):
        remote(target, target, send_sem.at[kind, k], recv_sem.at[kind, k], x_peer).wait_recv()

    core_copy = remote(send, got_ref, core_sem.at[0], core_sem.at[1], core_peer)
    core_copy.start()
    near = [k * 2 + x for k in range(planes)]
    over = [k * 2 + 1 - x for k in range(planes)]
    for k in range(half):
        push(dw.at[1, over[k]], diag_ref.at[k], 2, k, x_peer)
        push(dw.at[1, over[half + k]], diag_ref.at[half + k], 2, half + k, y_peer)
    for k in range(half):
        push(dw.at[0, over[k]], first_ref.at[k], 0, k, x_peer)
        push(dw.at[1, near[half + k]], second_ref.at[half + k], 1, half + k, y_peer)
    backs = []
    for e in range(2):
        for j in (6, 7, 2, 4, 3, 5, 1):
            backs.append(
                remote(sums.at[e, p ^ j], back_ref.at[e, p], back_send.at[e, j], back_recv.at[e, j], plane_peers[j])
            )
        backs.append(pltpu.make_async_copy(sums.at[e, p], back_ref.at[e, p], back_send.at[e, 0]))
    for copy in backs:
        copy.start()

    core_copy.wait()
    source = tokens[...].astype(f32)
    inverse = lax.rsqrt(jnp.mean(source * source, axis=1, keepdims=True) + epsilon)
    grad = keep[...].astype(f32) + got_ref[...].astype(f32)
    small_ref[:experts] = router_grad[...]
    small_ref[experts:experts + 1] = gain_mix_grad[...]
    small_ref[experts + 1:experts + 2] = jnp.sum(grad * source * inverse, axis=0, keepdims=True)
    small_ref[experts + 2:] = jnp.zeros_like(small_ref[experts + 2:])
    small_copies = []

    def small_start(n):
        copy = remote(small_ref, small_buf.at[n], small_send.at[n], small_recv.at[n], doubling[n])
        copy.start()
        small_copies.append(copy)

    def small_end(n):
        small_copies[n].wait()
        small_ref[...] = small_ref[...] + small_buf[n]

    small_start(0)
    weighted = grad * gain[...]
    centre = jnp.mean(source * weighted, axis=1, keepdims=True)
    total = grad_hidden[...] + inverse * weighted - source * (inverse * inverse * inverse * centre)
    out_ref[...] = total.astype(bf16)
    small_end(0)
    small_start(1)
    for k in range(half):
        arrive(diag_ref.at[k], 2, k)
        own_ref[k] = (dw[1, near[k]].astype(f32) + diag_ref[k].astype(f32)).astype(bf16)
        push(own_ref.at[k], second_ref.at[k], 1, k, y_peer)
        arrive(diag_ref.at[half + k], 2, half + k)
        own_ref[half + k] = (dw[0, over[half + k]].astype(f32) + diag_ref[half + k].astype(f32)).astype(bf16)
        push(own_ref.at[half + k], first_ref.at[half + k], 0, half + k, x_peer)
    small_end(1)
    small_start(2)
    for copy in sent:
        copy.wait_send()
    for k in range(planes):
        arrive(first_ref.at[k], 0, k)
        arrive(second_ref.at[k], 1, k)
        own_ref[k] = (
            dw[0, near[k]].astype(f32) + first_ref[k].astype(f32) + second_ref[k].astype(f32)
        ).astype(bf16)
    far = []
    for k, peer in enumerate(z_peers):
        copy = remote(
            own_ref.at[lax.rem(z + k + 1, planes)], far_ref.at[k], far_send.at[k], far_recv.at[k], peer
        )
        copy.start()
        far.append(copy)
    small_end(2)
    for n in range(3, len(doubling)):
        small_start(n)
        small_end(n)
    mine = own_ref[z].astype(f32)
    for k, copy in enumerate(far):
        copy.wait()
        mine += far_ref[k].astype(f32)
    grad_ref[...] = mine
    for e in range(2):
        for n, j in enumerate((6, 7, 2, 4, 3, 5, 1)):
            backs[8 * e + n].wait_send()
            slot = back_ref.at[e, p ^ j]
            remote(slot, slot, back_send.at[e, j], back_recv.at[e, j], x_peer).wait_recv()
        backs[8 * e + 7].wait()


def shards(
    tokens,
    lengths,
    routes,
    gain_attn,
    w_query,
    w_keyvalue,
    w_out,
    gain_mixer,
    w_router,
    w_gate,
    w_up,
    w_down,
    out_grad,
):
    nd, nt = lax.axis_size("dp"), lax.axis_size("tensor")
    dp_id, t_id = lax.axis_index("dp"), lax.axis_index("tensor")
    rows, width = tokens.shape
    group_rows, top_count = routes.shape
    seq_count = lengths.shape[0]
    seq_len = group_rows // seq_count
    experts = w_router.shape[1]
    local = experts // 8
    planes = nd // 2
    deep = width // nd
    hidden = w_gate.shape[2] * nt
    capacity = (rows * top_count * 17 + experts * 16 - 1) // (experts * 16)
    cap = -(-capacity // 16) * 16
    core = t_id % 2
    z_groups = [[x + 2 * z for z in range(planes)] for x in range(2)]
    members = nd // 2
    with_place = [[a * 2 + side for a in range(members)] for side in range(2)]
    plane_groups = [
        [with_place[side][a] * nt + t for side in range(2) for t in range(nt)] for a in range(members)
    ]

    quarter = hidden // nt

    def for_plane(w):
        return jnp.transpose(w.reshape(deep, 8, local, quarter), (1, 2, 0, 3))

    w_send = jnp.stack([for_plane(w_gate), for_plane(w_up), for_plane(w_down)], axis=2)
    q_cols, kv_cols = w_query.shape[1], w_keyvalue.shape[2]
    cut = q_cols + 2 * kv_cols
    w_mine = jnp.concatenate([w_query, w_keyvalue[:, 0], w_keyvalue[:, 1], w_out], axis=1)
    pushes = 3 * planes + 2 * (planes - 1)
    hbm = pl.BlockSpec(memory_space=pl.ANY)
    dealt_shape = sds((8, 3, deep, quarter), bf16)
    early = 1
    dealt_early = pl.pallas_call(
        deal_kernel,
        out_shape=[dealt_shape] * early,
        in_specs=[hbm], out_specs=[hbm] * early,
        scratch_shapes=[pltpu.SemaphoreType.DMA((early, 8)), pltpu.SemaphoreType.DMA((early, 8))],
        compiler_params=pltpu.CompilerParams(
            vmem_limit_bytes=VMEM_LIMIT, collective_id=1, has_side_effects=True
        ),
        cost_estimate=pl.CostEstimate(flops=10**6, bytes_accessed=20 * 2**20, transcendentals=0),
    )(w_send)
    later = tuple(range(early, local))
    normed_rows, w_attn, ranks, dealt_pair, dealt_last = pl.pallas_call(
        functools.partial(gather_kernel, later),
        out_shape=[
            sds((2 * rows, width), bf16), sds((2, nd, deep, cut + q_cols), bf16), sds((2, nt, 64, rows), bf16),
        ]
        + [sds((2,) + dealt_shape.shape, bf16), dealt_shape],
        in_specs=[SM] + [VM] * 4 + [hbm], out_specs=[VM] * 3 + [hbm] * 2,
        scratch_shapes=[
            pltpu.SemaphoreType.DMA((pushes,)), pltpu.SemaphoreType.DMA((2, nd)), pltpu.SemaphoreType.DMA((4,)),
            pltpu.SemaphoreType.DMA((len(later), 8)), pltpu.SemaphoreType.DMA((len(later), 8)),
        ],
        compiler_params=pltpu.CompilerParams(
            vmem_limit_bytes=VMEM_LIMIT, collective_id=0, has_side_effects=True
        ),
        cost_estimate=pl.CostEstimate(flops=10**7, bytes_accessed=100 * 2**20, transcendentals=0),
    )(lengths, tokens, gain_attn[None, :], routes.T, after(w_mine, *dealt_early), w_send)

    w_first = gather_weights(dealt_early[0], with_place)
    w_pair = gather_weights(dealt_pair, with_place)
    by_steps = members == local == 4
    w_last = dealt_last if by_steps else gather_weights(dealt_last, with_place)

    positions = jnp.arange(group_rows, dtype=jnp.int32) % seq_len
    live = positions < jnp.repeat(lengths, seq_len)
    own_start = t_id * rows
    live_own = lax.dynamic_slice_in_dim(live, own_start, rows, 0).astype(f32)[:, None]
    routes_own = lax.dynamic_slice_in_dim(routes, own_start, rows, 0)
    lane_ids = jnp.arange(LANES, dtype=jnp.int32)
    hits_own = jnp.any(routes_own[:, :, None] == lane_ids[None, None, :], axis=1).astype(f32) * live_own
    router = jnp.pad(w_router, ((0, 0), (0, LANES - experts)))
    router_t = jnp.pad(w_router.T.reshape(8, local, width), ((0, 0), (0, 8 - local), (0, 0))).reshape(64, width)

    half_head = HD // 2
    exponent = 2.0 * jnp.arange(half_head, dtype=f32) / HD
    angles = jnp.arange(seq_len, dtype=f32)[:, None] * jnp.exp(-math.log(rope_base) * exponent)[None, :]
    cosine, sine = jnp.cos(angles), jnp.sin(angles)
    cos_table = jnp.concatenate([cosine] * 4, axis=1)
    sin_table = jnp.concatenate([-sine, sine] * 2, axis=1)

    length = lax.dynamic_slice_in_dim(lengths, own_start // seq_len, 1, 0)[0]
    where_attn = jnp.stack([core, length]).astype(jnp.int32)

    out_late = after(out_grad, w_attn)
    out_y, out_x = hop_y(out_late), hop_x(out_late)
    q_width, k_width = 2 * q_cols, 2 * kv_cols
    heads = q_width // HD
    q, k, v, ctx, lse, keep, send = call(
        attend_kernel,
        [
            sds((seq_len, q_width), bf16), sds((seq_len, k_width), bf16), sds((seq_len, k_width), bf16),
            sds((seq_len, q_width), bf16), sds((heads, seq_len), f32),
            sds((rows, width), bf16), sds((rows, width), bf16),
        ],
        12 * 10**9, 16 * 2**20,
        in_specs=[SM] + [VM] * 4, out_specs=[VM] * 7,
    )(where_attn, normed_rows, w_attn, cos_table, sin_table)

    def remote_call(kernel, number, out_shape, flops, nbytes, **kw):
        return pl.pallas_call(
            kernel, out_shape=out_shape,
            compiler_params=pltpu.CompilerParams(
                vmem_limit_bytes=VMEM_LIMIT, collective_id=number, has_side_effects=True
            ),
            cost_estimate=pl.CostEstimate(flops=flops, bytes_accessed=nbytes, transcendentals=0),
            **kw,
        )

    dma = pltpu.SemaphoreType.DMA
    slots_shape = (local, 8, cap, width)
    hidden_own, normed_mix, inverse_mix, gates_in, rows_in, grads_in = remote_call(
        functools.partial(mix_kernel, local, cap), 2,
        [
            sds((rows, width), f32), sds((rows, width), bf16), sds((rows, 1), f32),
            sds((local, 8, cap, 1), f32), sds(slots_shape, bf16), sds(slots_shape, bf16),
        ],
        10**10, 100 * 2**20,
        in_specs=[VM] * 10, out_specs=[VM] * 4 + [hbm] * 2,
        scratch_shapes=[
            pltpu.VMEM((8, rows, width), bf16), pltpu.VMEM((8, rows, width), bf16), pltpu.VMEM((rows, width), bf16),
            pltpu.VMEM((2, local, cap, width), bf16), pltpu.VMEM((64, rows), f32), pltpu.VMEM((64, rows), f32),
            dma((2, 9)), dma((2, 9)), dma((2,)), dma((2,)),
        ],
    )(
        tokens, after(keep, w_first), send, live_own, gain_mixer[None, :], out_grad, out_y, out_x, ranks, router_t
    )
    ys, dxs, dw_pairs = [], [], []
    moving = (dealt_last, dealt_last)
    arrived = (w_last,)
    pair_shape = sds((members, 2, 8, 3, deep, quarter), bf16)
    before = []
    for e in range(local):
        step = e + 1 if by_steps and e < local - 1 else 0
        sources = ((w_first,), (w_pair,), (w_pair,), arrived)[e]
        inputs = [after(rows_in, *before), grads_in, gates_in, *sources, *(moving if step else ())]
        aliases = {}
        if e % 2:
            aliases = {len(inputs): 2}
            inputs.append(dw_pairs.pop())
        y, dx, dw, *moved = pl.pallas_call(
            functools.partial(expert_kernel, e, local, len(sources), step, len(sources) > 1),
            out_shape=[
                sds((8, cap, width), bf16), sds((8, cap, width + LANES), bf16), pair_shape,
            ] + [dealt_shape] * (2 if step else 0),
            in_specs=[hbm] * len(inputs),
            out_specs=[hbm] * (5 if step else 3),
            scratch_shapes=[
                pltpu.VMEM((8, cap, width), bf16), pltpu.VMEM((8, cap, width), bf16), pltpu.VMEM((8, cap, 1), f32),
                pltpu.VMEM((members, 8, 3, deep, quarter), bf16),
                pltpu.VMEM((8, cap, width), bf16), pltpu.VMEM((8, cap, width + LANES), bf16),
                pltpu.VMEM((members, 8, 3, deep, quarter), bf16),
                dma((3,)), dma((len(sources),)), dma((5,)), dma((4,)),
            ],
            input_output_aliases=aliases,
            compiler_params=pltpu.CompilerParams(
                vmem_limit_bytes=VMEM_LIMIT, **(dict(collective_id=3 + step, has_side_effects=True) if step else {})
            ),
            cost_estimate=pl.CostEstimate(flops=10**10, bytes_accessed=20 * 2**20, transcendentals=0),
        )(*inputs)
        if step:
            moving = tuple(moved)
            arrived += moving
        ys.append(y)
        dxs.append(dx)
        dw_pairs.append(dw)
        before = [y]

    wide = width + LANES
    grad_hidden, grad_branch, router_grad, gain_mix_grad, y_totals = remote_call(
        functools.partial(return_kernel, local, cap), 3,
        [
            sds((rows, width), f32), sds((2 * rows, width), bf16), sds((experts, width), f32), sds((1, width), f32),
            sds((4, rows, width), bf16),
        ],
        10**10, 100 * 2**20,
        in_specs=[hbm] * (2 * local) + [VM] * 9, out_specs=[VM] * 5,
        scratch_shapes=[
            pltpu.VMEM((3, local * cap, wide), bf16),
            pltpu.VMEM((4, rows, wide), bf16), pltpu.VMEM((4, rows, wide), bf16), pltpu.VMEM((4, rows, wide), bf16),
            pltpu.VMEM((2, rows // 2, wide), bf16), pltpu.VMEM((2, rows, wide), bf16),
            pltpu.VMEM((4, rows, width), bf16), pltpu.VMEM((4, rows, width), bf16), pltpu.VMEM((64, rows), f32),
            dma((3, local)), dma((10,)), dma((10,)), dma((4,)), dma((4,)), dma((2,)),
        ],
    )(
        *dxs, *ys, ranks, normed_mix, hidden_own, inverse_mix, out_grad, router, hits_own, live_own,
        gain_mixer[None, :],
    )
    chip_groups = [
        [with_place[side][a] * nt + y * 2 + c for side in range(2) for y in range(2)]
        for a in range(members) for c in range(2)
    ]
    y_terms = lax.all_to_all(y_totals, BOTH, 0, 0, tiled=True, axis_index_groups=chip_groups)
    mixed = (hidden_own + jnp.sum(y_terms.astype(f32), axis=0)).astype(bf16)

    dw_attn, keep_back, send_back = call(
        attend_back_kernel,
        [
            sds((2, nd, deep, cut + q_cols), bf16), sds((rows, width), bf16), sds((rows, width), bf16),
        ],
        25 * 10**9, 24 * 2**20,
        in_specs=[SM] + [VM] * 10, out_specs=[VM] * 3,
        scratch_shapes=[
            pltpu.VMEM((seq_len, q_width), bf16), pltpu.VMEM((seq_len, 2 * cut), bf16),
            pltpu.VMEM((seq_len, LANES), f32), pltpu.VMEM((seq_len, LANES), f32),
        ],
    )(
        where_attn, normed_rows, grad_branch, w_attn, cos_table, sin_table,
        q, k, v, ctx, lse,
    )
    doublings = 2 + (nd - 1).bit_length()
    per_dp = (deep, cut + q_cols)
    sums = [
        lax.psum_scatter(dw, "dp", scatter_dimension=0, axis_index_groups=with_place) for dw in dw_pairs
    ]
    grad_tokens, small, attn_grad, back_first = remote_call(
        tail_kernel, 8,
        [
            sds((rows, width), bf16), sds((experts + 8, width), f32), sds(per_dp, f32),
            sds((2, 8, 3, deep, quarter), bf16),
        ],
        10**8, 30 * 2**20,
        in_specs=[VM] * 8 + [hbm], out_specs=[VM] * 3 + [hbm],
        scratch_shapes=[pltpu.VMEM((rows, width), bf16)]
        + [pltpu.VMEM((planes,) + per_dp, bf16)] * 4
        + [
            pltpu.VMEM((planes - 1,) + per_dp, bf16), pltpu.VMEM((doublings, experts + 8, width), f32),
            dma((2,)), dma((3, planes)), dma((3, planes)), dma((planes - 1,)), dma((planes - 1,)),
            dma((doublings,)), dma((doublings,)), dma((2, 8)), dma((2, 8)),
        ],
    )(
        after(tokens, y_terms), keep_back, send_back, grad_hidden, gain_attn[None, :], router_grad, gain_mix_grad,
        dw_attn, sums[0],
    )

    back_last = lax.all_to_all(
        after(sums[1], grad_tokens), BOTH, 1, 1, tiled=True, axis_index_groups=plane_groups
    )

    def to_owner(which):
        parts = jnp.concatenate([back_first[:, :, which], back_last[:, :, which]], axis=0).astype(f32)
        return jnp.transpose(parts, (2, 1, 0, 3)).reshape(deep, experts, quarter)

    grad_query = attn_grad[:, :q_cols]
    grad_keyval = attn_grad[:, q_cols:cut].reshape(deep, 2, kv_cols)
    grad_out = attn_grad[:, cut:]
    return (
        mixed,
        grad_tokens,
        small[experts + 1],
        grad_query,
        grad_keyval,
        grad_out,
        small[experts],
        small[:experts].T,
        to_owner(0),
        to_owner(1),
        to_owner(2),
    )


def solution(mesh):
    placed = (
        P(("dp", "tensor"), None),
        P("dp"),
        P("dp", None),
        P(),
        P("dp", "tensor"),
        P("dp", None, "tensor"),
        P("dp", "tensor"),
        P(),
        P(),
        P("dp", None, "tensor"),
        P("dp", None, "tensor"),
        P("dp", None, "tensor"),
        P(("dp", "tensor"), None),
    )
    return jax.shard_map(
        shards,
        mesh=mesh,
        in_specs=placed,
        out_specs=(
            P(("dp", "tensor"), None),
            P(("dp", "tensor"), None),
            P(),
            P("dp", "tensor"),
            P("dp", None, "tensor"),
            P("dp", "tensor"),
            P(),
            P(),
            P("dp", None, "tensor"),
            P("dp", None, "tensor"),
            P("dp", None, "tensor"),
        ),
        check_vma=False,
    )
```

```python
import functools
import math

import jax
import jax.numpy as jnp
import numpy as np
from jax import lax
from jax.experimental import pallas as pl
from jax.experimental.pallas import tpu as pltpu
from jax.sharding import PartitionSpec as P

HD = 64
LANES = 128
epsilon = 1e-06
rope_base = 10000.0
bf16 = jnp.bfloat16
f32 = jnp.float32
BOTH = ("dp", "tensor")
VMEM_LIMIT = 60 * 1024 * 1024
QBLK = 256


def dot(a, b, ca, cb):
    return lax.dot_general(a, b, (((ca,), (cb,)), ((), ())), preferred_element_type=f32)


def call(kernel, out_shape, flops, nbytes, **kw):
    return pl.pallas_call(
        kernel,
        out_shape=out_shape,
        compiler_params=pltpu.CompilerParams(vmem_limit_bytes=VMEM_LIMIT),
        cost_estimate=pl.CostEstimate(flops=flops, bytes_accessed=nbytes, transcendentals=0),
        **kw,
    )


def sds(shape, dtype):
    return jax.ShapeDtypeStruct(shape, dtype)


VM = pl.BlockSpec(memory_space=pltpu.VMEM)
SM = pl.BlockSpec(memory_space=pltpu.SMEM)


def hop(x, dp_bit, t_bits):
    nd, nt = lax.axis_size("dp"), lax.axis_size("tensor")
    pairs = [
        (d * nt + t, (d ^ dp_bit) * nt + (t ^ t_bits)) for d in range(nd) for t in range(nt)
    ]
    return lax.ppermute(x, BOTH, pairs)


def hop_c(x):
    return hop(x, 0, 1)


def hop_y(x):
    return hop(x, 0, 2)


def hop_x(x):
    return hop(x, 1, 0)


def after(x, *others):
    return lax.optimization_barrier((x, *others))[0]


def gather_weights(x, weight_groups):
    return lax.all_gather(x, "dp", axis_index_groups=weight_groups)


def swap_halves(v):
    lane = lax.broadcasted_iota(jnp.int32, v.shape, 1)
    left = pltpu.roll(v, LANES - HD // 2, 1)
    right = pltpu.roll(v, HD // 2, 1)
    return jnp.where(lane % HD < HD // 2, left, right)


def in_head(tile, h):
    lane = lax.broadcasted_iota(jnp.int32, tile.shape, 1)
    return (lane < HD) if h == 0 else (lane >= HD)


def only_head(tile, h):
    return jnp.where(in_head(tile, h), tile, jnp.zeros_like(tile))


def spread_head(tile, h):
    wide = tile.astype(f32)
    return jnp.where(in_head(wide, h), wide, pltpu.roll(wide, HD, 1)).astype(tile.dtype)


def stacked(tile):
    return jnp.concatenate([only_head(tile, 0), only_head(tile, 1)], axis=0)


def key_limit(start, rows, length):
    column = lax.broadcasted_iota(jnp.int32, (1, 2 * rows), 1)
    position = start + jnp.where(column >= rows, column - rows, column)
    return jnp.minimum(position, length - 1)


def scores_t(kd, qm, limit):
    raw = dot(kd, qm, 1, 1) * (1.0 / math.sqrt(HD))
    key = lax.broadcasted_iota(jnp.int32, raw.shape, 0)
    return jnp.where(key <= limit, raw, -1e30)


def attend_kernel(
    lengths, rows, w, cos, sin,
    q_ref, k_ref, v_ref, ctx_ref, lse_ref, keep_ref, send_ref,
):
    core = lax.axis_index("tensor") % 2
    length = lengths[lax.axis_index("tensor") // 2]
    seq, width = rows.shape
    half = seq // 2
    kw = k_ref.shape[1] // 2
    qw = 2 * kw
    cut = qw + 2 * kw
    for blk in range(seq // QBLK):
        sl = slice(blk * QBLK, (blk + 1) * QBLK)
        c, s = cos[sl], sin[sl]
        for y in range(2):
            pre = dot(rows[sl], w[y, :, :, :cut].reshape(width, cut), 1, 0)
            for tile in range((qw + kw) // LANES):
                col = pre[:, tile * LANES:(tile + 1) * LANES]
                turned = (col * c + swap_halves(col) * s).astype(bf16)
                if tile * LANES < qw:
                    q_ref[sl, y * qw + tile * LANES:y * qw + (tile + 1) * LANES] = turned
                else:
                    at = y * kw + tile * LANES - qw
                    k_ref[sl, at:at + LANES] = turned
            v_ref[sl, y * kw:(y + 1) * kw] = pre[:, qw + kw:].astype(bf16)
    for g in range(2 * qw // LANES):
        kv = slice(g // 2 * LANES, (g // 2 + 1) * LANES)
        cols = slice(g * LANES, (g + 1) * LANES)
        kd = spread_head(k_ref[:, kv], g % 2)
        vd_t = spread_head(v_ref[:, kv], g % 2).T
        for blk in range(seq // QBLK):
            top = (blk + 1) * QBLK
            sl = slice(blk * QBLK, top)
            s = scores_t(kd[:top], stacked(q_ref[sl, cols]), key_limit(blk * QBLK, QBLK, length))
            peak = jnp.max(s, axis=0, keepdims=True)
            e = jnp.exp(s - peak)
            total = jnp.sum(e, axis=0, keepdims=True)
            p = (e * (1.0 / total)).astype(bf16)
            ctx = dot(vd_t[:, :top], p, 1, 0).T
            tile = jnp.where(in_head(ctx[:QBLK], 0), ctx[:QBLK], ctx[QBLK:])
            ctx_ref[sl, cols] = tile.astype(bf16)
            lse = peak + jnp.log(total)
            lse_ref[2 * g:2 * g + 1, sl] = lse[:, :QBLK]
            lse_ref[2 * g + 1:2 * g + 2, sl] = lse[:, QBLK:]
    for out_ref, side in ((send_ref, 1 - core), (keep_ref, core)):
        at = pl.ds(pl.multiple_of(side * half, half), half)
        out = dot(ctx_ref[at, :qw], w[0, :, :, cut:].reshape(width, qw), 1, 1)
        out += dot(ctx_ref[at, qw:], w[1, :, :, cut:].reshape(width, qw), 1, 1)
        out_ref[...] = out.astype(bf16)


def attend_back_kernel(
    lengths, rows, gb_ref, w, cos, sin, q_ref, k_ref, v_ref, ctx_ref, lse_ref,
    dw_ref, keep_ref, send_ref,
    gc_ref, dqkv_ref, dk_ref, dv_ref,
):
    core = lax.axis_index("tensor") % 2
    length = lengths[lax.axis_index("tensor") // 2]
    seq, width = rows.shape
    half = seq // 2
    kw = k_ref.shape[1] // 2
    qw = 2 * kw
    cut = qw + 2 * kw
    per_dp = dw_ref.shape[1:3]
    at_own = pl.ds(pl.multiple_of(core * half, half), half)
    at_peer = pl.ds(pl.multiple_of((1 - core) * half, half), half)
    for y in range(2):
        part = slice(y * qw, (y + 1) * qw)
        gc_ref[:, part] = dot(gb_ref[...], w[y, :, :, cut:].reshape(width, qw), 1, 0).astype(bf16)
        dw_ref[y, :, :, cut:] = dot(gb_ref[...], ctx_ref[:, part], 0, 0).astype(bf16).reshape(per_dp + (qw,))
    scale = 1.0 / math.sqrt(HD)
    folded = None
    for g in range(2 * qw // LANES):
        y = g // 2
        kv = slice(y * LANES, (y + 1) * LANES)
        cols = slice(g * LANES, (g + 1) * LANES)
        kd = spread_head(k_ref[:, kv], g % 2)
        kd_t = kd.T
        vd = spread_head(v_ref[:, kv], g % 2)
        for blk in reversed(range(seq // QBLK)):
            top = (blk + 1) * QBLK
            sl = slice(blk * QBLK, top)
            qm = stacked(q_ref[sl, cols])
            gm = stacked(gc_ref[sl, cols])
            s = scores_t(kd[:top], qm, key_limit(blk * QBLK, QBLK, length))
            lse = jnp.concatenate([lse_ref[2 * g:2 * g + 1, sl], lse_ref[2 * g + 1:2 * g + 2, sl]], axis=1)
            p = jnp.exp(s - lse)
            gw = dot(vd[:top], gm, 1, 1)
            centre = jnp.sum(p * gw, axis=0, keepdims=True)
            ds = (p * (gw - centre) * scale).astype(bf16)
            dv = dot(p.astype(bf16), gm, 1, 0)
            dk = dot(ds, qm, 1, 0)
            dq = dot(kd_t[:, :top], ds, 1, 0).T
            if top == seq:
                dk_ref[...] = dk
                dv_ref[...] = dv
            else:
                dk_ref[:top] += dk
                dv_ref[:top] += dv
            tile = jnp.where(in_head(dq[:QBLK], 0), dq[:QBLK], dq[QBLK:])
            back = tile * cos[sl] - swap_halves(tile) * sin[sl]
            at = y * cut + g % 2 * LANES
            dqkv_ref[sl, at:at + LANES] = back.astype(bf16)
        dk_all = dk_ref[...] + pltpu.roll(dk_ref[...], HD, 1)
        dv_all = dv_ref[...] + pltpu.roll(dv_ref[...], HD, 1)
        if g % 2 == 0:
            folded = (dk_all, dv_all)
        else:
            dk_pair = jnp.where(in_head(dk_all, 0), folded[0], dk_all)
            dv_pair = jnp.where(in_head(dv_all, 0), folded[1], dv_all)
            at = y * cut + qw
            back = dk_pair * cos[...] - swap_halves(dk_pair) * sin[...]
            dqkv_ref[:, at:at + LANES] = back.astype(bf16)
            dqkv_ref[:, at + LANES:at + 2 * LANES] = dv_pair.astype(bf16)
            part = slice(y * cut, (y + 1) * cut)
            dw_ref[y, :, :, :cut] = dot(rows[...], dqkv_ref[:, part], 0, 0).astype(bf16).reshape(per_dp + (cut,))
    for out_ref, at in ((send_ref, at_peer), (keep_ref, at_own)):
        out = dot(dqkv_ref[at, :cut], w[0, :, :, :cut].reshape(width, cut), 1, 1)
        out += dot(dqkv_ref[at, cut:], w[1, :, :, :cut].reshape(width, cut), 1, 1)
        out_ref[...] = out.astype(bf16)


def own_place():
    return lax.axis_index("dp") % 2 * 4 + lax.axis_index("tensor")


def plane_devices():
    d, p = lax.axis_index("dp"), own_place()
    return [{"dp": d + ((p ^ j) // 4 - p // 4), "tensor": (p ^ j) % 4} for j in range(8)]


def deal_out(p, plane_peers, w_send, numbers, dealt, send_sem, recv_sem):
    copies = []
    for i, e in enumerate(numbers):
        for j in (6, 7, 2, 4, 3, 5, 1):
            copies.append(
                pltpu.make_async_remote_copy(
                    src_ref=w_send.at[p ^ j, e], dst_ref=dealt[i].at[j], send_sem=send_sem.at[i, j],
                    recv_sem=recv_sem.at[i, j], device_id=plane_peers[j], device_id_type=pl.DeviceIdType.MESH,
                )
            )
        copies.append(pltpu.make_async_copy(w_send.at[p, e], dealt[i].at[0], send_sem.at[i, 0]))
    for copy in copies:
        copy.start()
    return copies


def deal_kernel(w_send, w_mine, *refs):
    dealt, (line_ref, send_sem, recv_sem, line_send, line_recv) = refs[:-5], refs[-5:]
    d, t = lax.axis_index("dp"), lax.axis_index("tensor")
    planes = line_ref.shape[0]
    z, x = d // 2, d % 2
    p = own_place()
    peers = plane_devices()
    z_peers = [{"dp": lax.rem(z + k, planes) * 2 + x, "tensor": t} for k in range(1, planes)]
    greet((*peers[1:], *z_peers))
    copies = deal_out(p, peers, w_send, range(len(dealt)), dealt, send_sem, recv_sem)
    lines = []
    for k, peer in enumerate(z_peers):
        copy = remote(w_mine, line_ref.at[z], line_send.at[k], line_recv.at[z], peer)
        copy.start()
        lines.append(copy)
    line_ref[z] = w_mine[...]
    for copy in copies:
        copy.wait()
    for k in range(1, planes):
        lines[k - 1].wait_send()
        at = lax.rem(z + k, planes)
        remote(line_ref.at[at], line_ref.at[at], line_send.at[0], line_recv.at[at], peers[1]).wait_recv()


def group_rows_of(experts):
    local = experts // 8
    row = lax.broadcasted_iota(jnp.int32, (64, experts), 0)
    expert = lax.broadcasted_iota(jnp.int32, (64, experts), 1)
    return ((row % 8 < local) & (row // 8 * local + row % 8 == expert)).astype(f32).astype(bf16)


def rank_rows(lengths, routes_t, block, ranks_ref):
    blocks, wide = ranks_ref.shape[1:3]
    seq_len = block * blocks // lengths.shape[0]
    local = wide // 16
    row = lax.broadcasted_iota(jnp.int32, (wide, block), 0)
    number = jnp.where(row % 8 < local, row // 8 * local + row % 8, -1)
    low = lax.broadcasted_iota(jnp.int32, (block, block), 0)
    high = lax.broadcasted_iota(jnp.int32, (block, block), 1)
    before = (low < high).astype(f32).astype(bf16)
    for b in range(blocks):
        at = slice(b * block, (b + 1) * block)
        position = lax.broadcasted_iota(jnp.int32, (wide, block), 1) + b * block % seq_len
        hit = jnp.zeros((wide, block), jnp.bool_)
        for k in range(routes_t.shape[0]):
            hit = hit | (routes_t[k:k + 1, at] == number)
        hit = hit & (position < lengths[b * block // seq_len])
        earlier = dot(hit.astype(f32).astype(bf16), before, 1, 0)
        ranks_ref[0, b] = jnp.where(hit, earlier, -1.0).astype(bf16)


def gather_kernel(
    later, lengths, tokens, gain, routes_t, router, line, w_send, rows_ref, w_ref, ranks_ref, router_ref, *refs
):
    (pair, last), (send_sem, recv_sem, row_sem, deal_send, deal_recv) = refs[:-5], refs[-5:]
    planes = line.shape[0]
    half = tokens.shape[0]
    x, core = lax.axis_index("dp") % 2, lax.axis_index("tensor") % 2
    p, plane_peers = own_place(), plane_devices()
    x_peer, y_peer, core_peer = neighbours()
    greet(plane_peers[1:])
    copies = []

    def push(source, side, dp, peer):
        copy = remote(source, w_ref.at[side, dp], send_sem.at[len(copies)], recv_sem.at[side, dp], peer)
        copy.start()
        copies.append(copy)

    def arrive(side, dp):
        slot = w_ref.at[side, dp]
        remote(slot, slot, send_sem.at[0], recv_sem.at[side, dp], x_peer).wait_recv()

    near = [k * 2 + x for k in range(planes)]
    over = [k * 2 + 1 - x for k in range(planes)]
    for k in range(planes):
        push(line.at[k], 0, near[k], x_peer)
        push(line.at[k], 1, near[k], y_peer)
    deals = deal_out(p, plane_peers, w_send, later, (pair.at[0], pair.at[1], last), deal_send, deal_recv)
    values = tokens[...].astype(f32)
    inverse = lax.rsqrt(jnp.mean(values * values, axis=1, keepdims=True) + epsilon)
    at = pl.ds(pl.multiple_of(core * half, half), half)
    rows_ref[at] = (values * inverse * gain[...]).astype(bf16)
    row_copy = remote(rows_ref.at[at], rows_ref.at[at], row_sem.at[0], row_sem.at[1], core_peer)
    row_copy.start()
    rank_rows(lengths, routes_t, half, ranks_ref)
    rank_copy = remote(ranks_ref.at[0], ranks_ref.at[1], row_sem.at[2], row_sem.at[3], x_peer)
    rank_copy.start()
    router_ref[...] = dot(group_rows_of(router.shape[1]), router[...], 1, 1).astype(bf16)
    for k in range(planes):
        w_ref[0, near[k]] = line[k]
    for k in range(planes):
        arrive(0, over[k])
        if k < planes // 2:
            push(w_ref.at[0, over[k]], 1, over[k], y_peer)
        arrive(1, near[k])
        if k >= planes // 2:
            push(w_ref.at[1, near[k]], 1, near[k], x_peer)
    for k in range(planes):
        arrive(1, over[k])
    for copy in copies:
        copy.wait_send()
    row_copy.wait()
    rank_copy.wait()
    for copy in deals:
        copy.wait()


def masked_shares(logits, hit, axis):
    peak = jnp.max(jnp.where(hit, logits, -1e30), axis=axis, keepdims=True)
    e = jnp.where(hit, jnp.exp(jnp.where(hit, logits - peak, 0.0)), 0.0)
    total = jnp.sum(e, axis=axis, keepdims=True)
    return e / jnp.where(total > 0.0, total, 1.0)


def split16(v):
    high = v.astype(bf16)
    return high, (v - high.astype(f32)).astype(bf16)


def neighbours():
    peers = plane_devices()
    return peers[4], peers[2], peers[1]


def greet(peers):
    barrier = pltpu.get_barrier_semaphore()
    for peer in peers:
        pl.semaphore_signal(barrier, inc=1, device_id=peer, device_id_type=pl.DeviceIdType.MESH)
    pl.semaphore_wait(barrier, len(peers))


def remote(source, target, send_sem, recv_sem, peer):
    return pltpu.make_async_remote_copy(
        src_ref=source, dst_ref=target, send_sem=send_sem, recv_sem=recv_sem,
        device_id=peer, device_id_type=pl.DeviceIdType.MESH,
    )


def live_rows(lengths, rows):
    first = lax.axis_index("tensor") * rows
    seq_len = 4 * rows // lengths.shape[0]
    position = lax.rem(first, seq_len) + lax.broadcasted_iota(jnp.int32, (rows, 1), 0)
    return (position < lengths[first // seq_len]).astype(f32)


def z_steps(step, up_from, down_from, up_to, down_to, sem):
    d, t = lax.axis_index("dp"), lax.axis_index("tensor")
    planes = lax.axis_size("dp") // 2
    z = d // 2
    above = {"dp": lax.rem(z + 1, planes) * 2 + d % 2, "tensor": t}
    below = {"dp": lax.rem(z + planes - 1, planes) * 2 + d % 2, "tensor": t}
    up = remote(up_from, up_to, sem.at[0], sem.at[1], above)
    down = remote(down_from, down_to, sem.at[2], sem.at[3], below)
    steps = (
        (up, (z >= step - 1) & (z < planes - 1), z >= step),
        (down, (z > 0) & (z <= planes - step), z < planes - step),
    )
    return steps, above, below


def start_steps(steps):
    for copy, sends, _ in steps:
        pl.when(sends)(copy.start)


def settle_steps(steps):
    for copy, sends, receives in steps:
        pl.when(sends)(copy.wait_send)
        pl.when(receives)(copy.wait_recv)


def block_ranks(ranks, j):
    return ranks[j // 4, lax.axis_index("tensor") ^ (j % 4)].astype(f32)


def own_group():
    return pl.multiple_of(own_place() * 8, 8)


def placing(ranks, cap):
    slot = lax.broadcasted_iota(jnp.int32, (cap, ranks.shape[1]), 0).astype(f32)
    return [(slot == ranks[e:e + 1]).astype(f32) for e in range(ranks.shape[0])]


def mix_kernel(
    local, cap, carry, lengths, tokens, keep, send, gain, out_own, out_y, out_x, ranks, router_t, *refs
):
    if carry:
        moving, refs = refs[0], refs[1:]
        (up_to, down_to), refs = refs[6:8], refs[:6] + refs[8:]
    (
        hidden_ref, normed_ref, inv_ref, gates_ref, x_hbm, g_hbm,
        normed_buf, out_buf, got_ref, stage_ref, ranks_ref, shares_ref,
        send_sem, recv_sem, core_sem, stage_sem, z_sem,
    ) = refs
    x_peer, y_peer, core_peer = neighbours()
    if carry:
        steps, above, below = z_steps(carry, moving, moving, up_to, down_to, z_sem)
        greet((x_peer, y_peer, core_peer, above, below))
    else:
        greet((x_peer, y_peer, core_peer))
    rows = tokens.shape[0]
    low, high = pl.ds(0, rows // 2), pl.ds(rows // 2, rows // 2)
    sent = []

    def push(kind, source, target, slot, peer):
        copy = remote(source, target, send_sem.at[kind, slot], recv_sem.at[kind, slot], peer)
        copy.start()
        sent.append(copy)

    def arrive(kind, target, slot):
        remote(target, target, send_sem.at[kind, slot], recv_sem.at[kind, slot], x_peer).wait_recv()

    core_copy = remote(send, got_ref, core_sem.at[0], core_sem.at[1], core_peer)
    core_copy.start()
    if carry:
        start_steps(steps)
    push(1, out_y.at[low], out_buf.at[6, low], 6, x_peer)
    push(1, out_x.at[high], out_buf.at[6, high], 8, y_peer)
    push(1, out_own, out_buf.at[1], 1, core_peer)
    push(1, out_y, out_buf.at[3], 3, core_peer)
    push(1, out_x, out_buf.at[5], 5, core_peer)
    core_copy.wait()
    branch = keep[...].astype(f32) + got_ref[...].astype(f32)
    hidden = tokens[...].astype(f32) + live_rows(lengths, rows) * branch
    inverse = lax.rsqrt(jnp.mean(hidden * hidden, axis=1, keepdims=True) + epsilon)
    hidden_ref[...] = hidden
    inv_ref[...] = inverse
    normed = (hidden * inverse * gain[...]).astype(bf16)
    normed_ref[...] = normed
    normed_buf[0] = normed
    own = normed_buf.at[0]
    push(0, own, normed_buf.at[2], 2, y_peer)
    push(0, own, normed_buf.at[4], 4, x_peer)
    push(0, own, normed_buf.at[1], 1, core_peer)

    staged = []

    def place(kind, j, source):
        n = len(staged)
        if n >= 2:
            staged[n - 2].wait()
        group = own_group()
        ranks_ref[...] = block_ranks(ranks, j)
        places = placing(ranks_ref[pl.ds(group, 8)][:local], cap)
        if kind == 0:
            logits = dot(router_t[...], source[...], 1, 1)
            shares_ref[...] = masked_shares(logits, ranks_ref[...] >= 0.0, 0)
            shares = shares_ref[pl.ds(group, 8)]
            for e in range(local):
                gates_ref[e, j] = jnp.sum(places[e] * shares[e:e + 1], axis=1, keepdims=True)
        matrix = jnp.concatenate([m.astype(bf16) for m in places], axis=0)
        placed = dot(matrix, source[...], 1, 0).astype(bf16)
        stage_ref[n % 2] = placed.reshape(local, cap, -1)
        copy = pltpu.make_async_copy(
            stage_ref.at[n % 2], (x_hbm if kind == 0 else g_hbm).at[:, j], stage_sem.at[n % 2]
        )
        copy.start()
        staged.append(copy)

    place(1, 0, out_own)
    place(1, 2, out_y)
    place(1, 4, out_x)
    place(0, 0, own)
    for j in (1, 3, 5):
        arrive(1, out_buf.at[j], j)
        place(1, j, out_buf.at[j])
    arrive(1, out_buf.at[6, low], 6)
    arrive(1, out_buf.at[6, high], 8)
    push(1, out_buf.at[6], out_buf.at[7], 7, core_peer)
    arrive(0, normed_buf.at[1], 1)
    place(0, 1, normed_buf.at[1])
    place(1, 6, out_buf.at[6])
    arrive(0, normed_buf.at[2], 2)
    push(0, normed_buf.at[2, low], normed_buf.at[6, low], 6, x_peer)
    push(0, normed_buf.at[2], normed_buf.at[3], 3, core_peer)
    arrive(0, normed_buf.at[4], 4)
    push(0, normed_buf.at[4, high], normed_buf.at[6, high], 8, y_peer)
    push(0, normed_buf.at[4], normed_buf.at[5], 5, core_peer)
    arrive(1, out_buf.at[7], 7)
    place(1, 7, out_buf.at[7])
    place(0, 2, normed_buf.at[2])
    place(0, 4, normed_buf.at[4])
    for j in (3, 5):
        arrive(0, normed_buf.at[j], j)
        place(0, j, normed_buf.at[j])
    arrive(0, normed_buf.at[6, low], 6)
    arrive(0, normed_buf.at[6, high], 8)
    push(0, normed_buf.at[6], normed_buf.at[7], 7, core_peer)
    place(0, 6, normed_buf.at[6])
    arrive(0, normed_buf.at[7], 7)
    place(0, 7, normed_buf.at[7])
    for copy in sent:
        copy.wait_send()
    for copy in staged[-2:]:
        copy.wait()
    if carry:
        settle_steps(steps)


def return_kernel(local, cap, *refs):
    dxs, ys, refs = refs[:local], refs[local:2 * local], refs[2 * local:]
    (
        lengths, ranks, normed, hidden_in, inv, out_grad, router, gain,
        grad_hidden_ref, branch_ref, router_grad_ref, gain_grad_ref, y_ref,
        load_ref, part_ref, core_ref, total_ref, diag_ref, last_ref, y_part, y_core, ranks_ref,
        load_sem, send_sem, recv_sem, y_send, y_recv, branch_sem,
    ) = refs
    x_peer, y_peer, core_peer = neighbours()
    core = lax.axis_index("tensor") % 2
    greet((x_peer, y_peer, core_peer))
    rows, width = normed.shape
    wide = part_ref.shape[-1]
    half = rows // 2
    low, high = pl.ds(0, half), pl.ds(half, half)
    order = [(0, j) for j in (7, 6, 5, 4, 3, 2, 1, 0)] + [(1, j) for j in (7, 5, 3, 1, 6, 4, 2, 0)]
    depth = load_ref.shape[0]
    sent = []

    def loads(n):
        kind, j = order[n]
        slot = n % depth
        cols = wide if kind == 0 else width
        return [
            pltpu.make_async_copy(
                (ys if kind else dxs)[e].at[j],
                load_ref.at[slot, pl.ds(e * cap, cap), pl.ds(0, cols)], load_sem.at[slot, e],
            )
            for e in range(local)
        ]

    def start(n):
        if n < len(order):
            for copy in loads(n):
                copy.start()

    for n in range(depth - 1):
        start(n)
    done = [0]

    def combined():
        n = done[0]
        done[0] += 1
        start(n + depth - 1)
        for copy in loads(n):
            copy.wait()
        kind, j = order[n]
        ranks_ref[...] = block_ranks(ranks, j)
        places = placing(ranks_ref[pl.ds(own_group(), 8)][:local], cap)
        matrix = jnp.concatenate([m.astype(bf16) for m in places], axis=0)
        values = load_ref[n % depth] if kind == 0 else load_ref[n % depth, :, :width]
        return dot(matrix, values, 0, 0)

    def push(source, target, n, peer):
        copy = remote(source, target, send_sem.at[n], recv_sem.at[n], peer)
        copy.start()
        sent.append(copy)

    def arrive(target, n):
        remote(target, target, send_sem.at[n], recv_sem.at[n], x_peer).wait_recv()

    def far_core(k):
        part_ref[k] = combined().astype(bf16)
        push(part_ref.at[k], core_ref.at[k], k, core_peer)

    def near_core(k):
        mine = combined()
        arrive(core_ref.at[k], k)
        return mine + core_ref[k].astype(f32)

    far_core(3)
    total_ref[2] = near_core(3).astype(bf16)
    push(total_ref.at[2, low], diag_ref.at[0], 4, x_peer)
    push(total_ref.at[2, high], diag_ref.at[1], 5, y_peer)
    far_core(2)
    total_ref[1] = near_core(2).astype(bf16)
    push(total_ref.at[1, low], last_ref.at[0, low], 6, x_peer)
    far_core(1)
    total_ref[0] = near_core(1).astype(bf16)
    push(total_ref.at[0, high], last_ref.at[1, high], 7, y_peer)
    far_core(0)
    part_own = near_core(0).astype(bf16)
    y_copies = []
    total_ref[3] = part_own

    def y_far(k):
        y_part[k] = combined().astype(bf16)
        copy = remote(y_part.at[k], y_core.at[k], y_send.at[k], y_recv.at[k], core_peer)
        copy.start()
        y_copies.append(copy)

    y_far(3)
    y_far(2)
    arrive(diag_ref.at[1], 5)
    total_ref[1, high] = (total_ref[1, high].astype(f32) + diag_ref[1].astype(f32)).astype(bf16)
    push(total_ref.at[1, high], last_ref.at[0, high], 8, x_peer)
    arrive(diag_ref.at[0], 4)
    total_ref[0, low] = (total_ref[0, low].astype(f32) + diag_ref[0].astype(f32)).astype(bf16)
    push(total_ref.at[0, low], last_ref.at[1, low], 9, y_peer)
    y_far(1)
    y_far(0)
    for k in (3, 2, 1, 0):
        mine = combined()
        y_copies[3 - k].wait()
        y_ref[k ^ (own_place() // 2)] = (mine + y_core[k].astype(f32)).astype(bf16)

    experts = router.shape[1]
    hit_rows = (block_ranks(ranks, 0) >= 0.0).astype(f32).astype(bf16)
    hit = dot(hit_rows, group_rows_of(experts), 0, 0) > 0.0
    shares = masked_shares(dot(normed[...], router[...], 1, 0), hit, 1)
    arrive(last_ref.at[0, low], 6)
    arrive(last_ref.at[1, high], 7)
    arrive(last_ref.at[0, high], 8)
    arrive(last_ref.at[1, low], 9)
    for copy in sent:
        copy.wait_send()

    def summed(lo, hi):
        cols = pl.ds(lo, hi - lo)
        return (
            total_ref[3, :, cols].astype(f32) + last_ref[0, :, cols].astype(f32) + last_ref[1, :, cols].astype(f32)
        )

    grad_shares = jnp.where(hit, summed(width, wide)[:, :experts], 0.0)
    grad_chosen = shares * (grad_shares - jnp.sum(shares * grad_shares, axis=1, keepdims=True))
    top, rest = split16(grad_chosen)
    hidden, inverse = hidden_in[...], inv[...]
    grad_mix = summed(0, width) + dot(top, router[...], 1, 1) + dot(rest, router[...], 1, 1)
    weighted = grad_mix * gain[...]
    centre = jnp.mean(hidden * weighted, axis=1, keepdims=True)
    grad_hidden = out_grad[...].astype(f32) + inverse * weighted - hidden * (inverse * inverse * inverse * centre)
    grad_hidden_ref[...] = grad_hidden
    at = pl.ds(pl.multiple_of(core * rows, rows), rows)
    branch_ref[at] = (live_rows(lengths, rows) * grad_hidden).astype(bf16)
    branch_copy = remote(branch_ref.at[at], branch_ref.at[at], branch_sem.at[0], branch_sem.at[1], core_peer)
    branch_copy.start()
    gain_grad_ref[...] = jnp.sum(grad_mix * hidden * inverse, axis=0, keepdims=True)
    router_grad_ref[...] = dot(top, normed[...], 0, 0) + dot(rest, normed[...], 0, 0)
    branch_copy.wait()


def expert_kernel(expert, local, steps, carry, chained, x_hbm, g_hbm, gates_hbm, *refs):
    sources, refs = refs[:steps], refs[steps:]
    if carry:
        (up_from, down_from), refs = refs[:2], refs[2:]
    if expert % 2:
        refs = refs[1:]
    if carry:
        (up_to, down_to), refs = refs[3:5], refs[:3] + refs[5:]
    y_hbm, dx_hbm, dw_hbm, x_ref, g_ref, gates_ref, w_buf, y_ref, dx_ref, dw_ref, in_sem, w_sem, out_sem, z_sem = refs
    d, t, p = lax.axis_index("dp"), lax.axis_index("tensor"), own_place()
    members, _, _, deep, quarter = w_buf.shape
    blocks = [(dp // 2, dp % 2 * 4) for dp in range(2 * members)]
    z = d // 2
    if carry:
        steps_out, above, below = z_steps(carry, up_from, down_from, up_to, down_to, z_sem)
        greet((above, below))
        start_steps(steps_out)

    def fetch(act):
        if not chained:
            source = sources[0] if expert in (0, local - 1) else sources[0].at[:, expert - 1]
            act(pltpu.make_async_copy(source, w_buf, w_sem.at[0]))
            return
        act(pltpu.make_async_copy(sources[0], w_buf.at[z], w_sem.at[0]))
        for n, source in enumerate(sources[1:]):
            origin = z - (n // 2 + 1) if n % 2 == 0 else z + n // 2 + 1

            @pl.when((origin >= 0) & (origin < members))
            def _():
                act(pltpu.make_async_copy(source, w_buf.at[origin], w_sem.at[n + 1]))

    x_copy = pltpu.make_async_copy(x_hbm.at[expert], x_ref, in_sem.at[0])
    g_copy = pltpu.make_async_copy(g_hbm.at[expert], g_ref, in_sem.at[1])
    gates_copy = pltpu.make_async_copy(gates_hbm.at[expert], gates_ref, in_sem.at[2])
    x_copy.start()
    fetch(lambda copy: copy.start())
    g_copy.start()
    gates_copy.start()
    slots, width = x_ref.shape[0] * x_ref.shape[1], x_ref.shape[2]

    def weight(which):
        rows = [
            jnp.concatenate([w_buf[at, (side + q) ^ p, which] for q in range(4)], axis=1) for at, side in blocks
        ]
        return jnp.concatenate(rows, axis=0)

    outs = []

    def send(source, target):
        copy = pltpu.make_async_copy(source, target, out_sem.at[len(outs)])
        copy.start()
        outs.append(copy)

    x_copy.wait()
    fetch(lambda copy: copy.wait())
    x = x_ref[...].reshape(slots, width)
    w_gate, w_up, w_down = weight(0), weight(1), weight(2)
    gate_lin = dot(x, w_gate, 1, 0)
    up_lin = dot(x, w_up, 1, 0)
    g_copy.wait()
    gates_copy.wait()
    g = g_ref[...].reshape(slots, width)
    gates = gates_ref[...].reshape(slots, 1)
    grad_scaled = dot(g, w_down, 1, 0)
    sigmoid = 1.0 / (1.0 + jnp.exp(-gate_lin))
    silu = gate_lin * sigmoid
    product = silu * up_lin
    grad_gates = jnp.sum(grad_scaled * product, axis=1, keepdims=True)
    scaled_hidden = (gates * product).astype(bf16)
    grad_act = gates * grad_scaled
    grad_gate_lin = (grad_act * up_lin * sigmoid * (1.0 + gate_lin * (1.0 - sigmoid))).astype(bf16)
    grad_up_lin = (grad_act * silu).astype(bf16)
    y_ref[...] = dot(scaled_hidden, w_down, 1, 1).astype(bf16).reshape(y_ref.shape)
    send(y_ref, y_hbm)
    dx = dot(grad_gate_lin, w_gate, 1, 1) + dot(grad_up_lin, w_up, 1, 1)
    dx_ref[:, :, :width] = dx.astype(bf16).reshape(y_ref.shape)
    lane = lax.broadcasted_iota(jnp.int32, (slots, LANES), 1)
    tail = jnp.where(lane == p * local + expert, grad_gates, 0.0).astype(bf16)
    dx_ref[:, :, width:] = tail.reshape(dx_ref.shape[:2] + (LANES,))
    send(dx_ref, dx_hbm)
    for which, (left, right) in enumerate(((x, grad_gate_lin), (x, grad_up_lin), (g, scaled_hidden))):
        grad = dot(left, right, 0, 0).astype(bf16)
        for dp, (at, side) in enumerate(blocks):
            for q in range(4):
                dw_ref[at, side + q, which] = grad[dp * deep:(dp + 1) * deep, q * quarter:(q + 1) * quarter]
        send(dw_ref.at[:, :, which], dw_hbm.at[:, expert % 2, :, which])
    for copy in outs:
        copy.wait()
    if carry:
        settle_steps(steps_out)


def all_peers(d, t, planes):
    peers = [{"dp": d, "tensor": t ^ 1}, {"dp": d, "tensor": t ^ 2}]
    bit = 1
    while bit < 2 * planes:
        peers.append({"dp": d ^ bit, "tensor": t})
        bit *= 2
    return peers


def push_back(p, plane_peers, sums, back_ref, send_sem, recv_sem):
    copies = []
    for e in range(2):
        for j in (6, 7, 2, 4, 3, 5, 1):
            copies.append(
                remote(sums.at[e, p ^ j], back_ref.at[e, p], send_sem.at[e, j], recv_sem.at[e, j], plane_peers[j])
            )
        copies.append(pltpu.make_async_copy(sums.at[e, p], back_ref.at[e, p], send_sem.at[e, 0]))
    for copy in copies:
        copy.start()
    return copies


def settle_back(p, plane_peers, copies, back_ref, send_sem, recv_sem):
    for e in range(2):
        for n, j in enumerate((6, 7, 2, 4, 3, 5, 1)):
            copies[8 * e + n].wait_send()
            slot = back_ref.at[e, p ^ j]
            remote(slot, slot, send_sem.at[e, j], recv_sem.at[e, j], plane_peers[1]).wait_recv()
        copies[8 * e + 7].wait()


def tail_kernel(
    tokens, keep, send, grad_hidden, gain, router_grad, gain_mix_grad, dw, sums,
    out_ref, router_ref, gains_ref, plane_ref, back_ref,
    got_ref, first_ref, second_ref, diag_ref, own_ref, small_ref, small_buf, part_ref, part_buf, parts_ref,
    core_sem, send_sem, recv_sem, small_send, small_recv, back_send, back_recv,
    part_send, part_recv, parts_send, parts_recv,
):
    d, t = lax.axis_index("dp"), lax.axis_index("tensor")
    planes = dw.shape[1] // 2
    half = planes // 2
    x = d % 2
    doubling = all_peers(d, t, planes)
    core_peer, y_peer, x_peer = doubling[:3]
    p, plane_peers = own_place(), plane_devices()
    greet((*plane_peers[1:], *doubling[3:]))
    experts = router_grad.shape[0]
    sent = []

    def push(source, target, kind, k, peer):
        copy = remote(source, target, send_sem.at[kind, k], recv_sem.at[kind, k], peer)
        copy.start()
        sent.append(copy)

    def arrive(target, kind, k):
        remote(target, target, send_sem.at[kind, k], recv_sem.at[kind, k], x_peer).wait_recv()

    core_copy = remote(send, got_ref, core_sem.at[0], core_sem.at[1], core_peer)
    core_copy.start()
    near = [k * 2 + x for k in range(planes)]
    over = [k * 2 + 1 - x for k in range(planes)]
    for k in range(half):
        push(dw.at[1, over[k]], diag_ref.at[k], 2, k, x_peer)
        push(dw.at[1, over[half + k]], diag_ref.at[half + k], 2, half + k, y_peer)
    for k in range(half):
        push(dw.at[0, over[k]], first_ref.at[k], 0, k, x_peer)
        push(dw.at[1, near[half + k]], second_ref.at[half + k], 1, half + k, y_peer)
    core_copy.wait()
    source = tokens[...].astype(f32)
    inverse = lax.rsqrt(jnp.mean(source * source, axis=1, keepdims=True) + epsilon)
    grad = keep[...].astype(f32) + got_ref[...].astype(f32)
    gain_grad = jnp.sum(grad * source * inverse, axis=0, keepdims=True)
    small_ref[:experts] = router_grad[...]
    row = lax.broadcasted_iota(jnp.int32, (8, small_ref.shape[1]), 0)
    small_ref[experts:] = jnp.where(row == 0, gain_mix_grad[...], jnp.where(row == 1, gain_grad, 0.0))

    def small_start(n):
        copy = remote(small_ref, small_buf.at[n], small_send.at[n], small_recv.at[n], doubling[n])
        copy.start()
        return copy

    def small_end(n, copy):
        copy.wait()
        small_ref[...] = small_ref[...] + small_buf[n]

    running = small_start(0)
    weighted = grad * gain[...]
    centre = jnp.mean(source * weighted, axis=1, keepdims=True)
    total = grad_hidden[...] + inverse * weighted - source * (inverse * inverse * inverse * centre)
    out_ref[...] = total.astype(bf16)
    small_end(0, running)
    running = small_start(1)
    for k in range(half):
        arrive(diag_ref.at[k], 2, k)
        own_ref[k] = (dw[1, near[k]].astype(f32) + diag_ref[k].astype(f32)).astype(bf16)
        push(own_ref.at[k], second_ref.at[k], 1, k, y_peer)
        arrive(diag_ref.at[half + k], 2, half + k)
        own_ref[half + k] = (dw[0, over[half + k]].astype(f32) + diag_ref[half + k].astype(f32)).astype(bf16)
        push(own_ref.at[half + k], first_ref.at[half + k], 0, half + k, x_peer)
    small_end(1, running)
    running = small_start(2)
    backs = push_back(p, plane_peers, sums, back_ref, back_send, back_recv)
    for copy in sent:
        copy.wait_send()
    for k in range(planes):
        arrive(first_ref.at[k], 0, k)
        arrive(second_ref.at[k], 1, k)
        plane_ref[k] = (
            dw[0, near[k]].astype(f32) + first_ref[k].astype(f32) + second_ref[k].astype(f32)
        ).astype(bf16)
    small_end(2, running)
    cols = small_ref.shape[1] // 8
    part_ref[...] = small_ref[:, pl.ds(pl.multiple_of(p * cols, cols), cols)]
    for n, peer in enumerate(doubling[3:]):
        copy = remote(part_ref, part_buf.at[n], part_send.at[n], part_recv.at[n], peer)
        copy.start()
        copy.wait()
        part_ref[...] = part_ref[...] + part_buf[n]
    spread = []
    for j in range(1, 8):
        copy = remote(part_ref, parts_ref.at[p], parts_send.at[j], parts_recv.at[j], plane_peers[j])
        copy.start()
        spread.append(copy)
    parts_ref[p] = part_ref[...]
    settle_back(p, plane_peers, backs, back_ref, back_send, back_recv)
    for j in range(1, 8):
        spread[j - 1].wait_send()
        slot = parts_ref.at[p ^ j]
        remote(slot, slot, parts_send.at[j], parts_recv.at[j], plane_peers[1]).wait_recv()
    for q in range(8):
        router_ref[q * cols:(q + 1) * cols] = parts_ref[q, :experts].T
        gains_ref[:, q * cols:(q + 1) * cols] = parts_ref[q, experts:]


def last_kernel(
    plane, back_first, sums, query_ref, keyval_ref, wo_ref, gate_ref, up_ref, down_ref,
    back_ref, far_ref, far_send, far_recv, back_send, back_recv,
):
    d, t = lax.axis_index("dp"), lax.axis_index("tensor")
    planes = plane.shape[0]
    z, x = d // 2, d % 2
    z_peers = [{"dp": lax.rem(z + k, planes) * 2 + x, "tensor": t} for k in range(1, planes)]
    p, plane_peers = own_place(), plane_devices()
    greet((*plane_peers[1:], *z_peers))
    far = []
    for k, peer in enumerate(z_peers):
        copy = remote(plane.at[lax.rem(z + k + 1, planes)], far_ref.at[k], far_send.at[k], far_recv.at[k], peer)
        copy.start()
        far.append(copy)
    backs = push_back(p, plane_peers, sums, back_ref, back_send, back_recv)
    outs = (gate_ref, up_ref, down_ref)
    deep = back_first.shape[3]
    experts = gate_ref.shape[0] // deep

    def assemble(source, first, e, q):
        rows = pl.ds(q * (experts // 8) + first + e, deep, stride=experts)
        for which, out in enumerate(outs):
            out[rows, :] = source[e, q, which].astype(f32)

    for q in range(8):
        for e in range(2):
            assemble(back_first, 0, e, q)
    for e in range(2):
        backs[8 * e + 7].wait()
        assemble(back_ref, 2, e, p)
    for j in (1, 2, 4, 3, 5, 6, 7):
        for e in range(2):
            slot = back_ref.at[e, p ^ j]
            remote(slot, slot, back_send.at[e, j], back_recv.at[e, j], plane_peers[1]).wait_recv()
            assemble(back_ref, 2, e, p ^ j)
    for e in range(2):
        for n in range(7):
            backs[8 * e + n].wait_send()
    mine = plane[z].astype(f32)
    for k, copy in enumerate(far):
        copy.wait()
        mine += far_ref[k].astype(f32)
    qw, kvw = query_ref.shape[1], keyval_ref.shape[2]
    query_ref[...] = mine[:, :qw]
    keyval_ref[:, 0] = mine[:, qw:qw + kvw]
    keyval_ref[:, 1] = mine[:, qw + kvw:qw + 2 * kvw]
    wo_ref[...] = mine[:, qw + 2 * kvw:]


def shards(
    tokens,
    lengths,
    routes,
    gain_attn,
    w_query,
    w_keyvalue,
    w_out,
    gain_mixer,
    w_router,
    w_gate,
    w_up,
    w_down,
    out_grad,
):
    nd, nt = lax.axis_size("dp"), lax.axis_size("tensor")
    dp_id, t_id = lax.axis_index("dp"), lax.axis_index("tensor")
    rows, width = tokens.shape
    group_rows, top_count = routes.shape
    seq_count = lengths.shape[0]
    seq_len = group_rows // seq_count
    experts = w_router.shape[1]
    local = experts // 8
    planes = nd // 2
    deep = width // nd
    hidden = w_gate.shape[2] * nt
    capacity = (rows * top_count * 17 + experts * 16 - 1) // (experts * 16)
    cap = -(-capacity // 16) * 16
    core = t_id % 2
    z_groups = [[x + 2 * z for z in range(planes)] for x in range(2)]
    members = nd // 2
    with_place = [[a * 2 + side for a in range(members)] for side in range(2)]
    plane_groups = [
        [with_place[side][a] * nt + t for side in range(2) for t in range(nt)] for a in range(members)
    ]

    quarter = hidden // nt

    def for_plane(w):
        return jnp.transpose(w.reshape(deep, 8, local, quarter), (1, 2, 0, 3))

    w_send = jnp.stack([for_plane(w_gate), for_plane(w_up), for_plane(w_down)], axis=2)
    q_cols, kv_cols = w_query.shape[1], w_keyvalue.shape[2]
    cut = q_cols + 2 * kv_cols
    w_mine = jnp.concatenate([w_query, w_keyvalue[:, 0], w_keyvalue[:, 1], w_out], axis=1)
    pushes = 3 * planes
    hbm = pl.BlockSpec(memory_space=pl.ANY)
    dealt_shape = sds((8, 3, deep, quarter), bf16)
    dma = pltpu.SemaphoreType.DMA
    line_shape = sds((planes, deep, cut + q_cols), bf16)
    dealt_first, line = pl.pallas_call(
        deal_kernel,
        out_shape=[dealt_shape, line_shape],
        in_specs=[hbm, VM], out_specs=[hbm, VM],
        scratch_shapes=[dma((1, 8)), dma((1, 8)), dma((planes,)), dma((planes,))],
        compiler_params=pltpu.CompilerParams(
            vmem_limit_bytes=VMEM_LIMIT, collective_id=1, has_side_effects=True
        ),
        cost_estimate=pl.CostEstimate(flops=10**6, bytes_accessed=20 * 2**20, transcendentals=0),
    )(w_send, w_mine)
    later = tuple(range(1, local))
    normed_rows, w_attn, ranks, router_t, dealt_pair, dealt_last = pl.pallas_call(
        functools.partial(gather_kernel, later),
        out_shape=[
            sds((2 * rows, width), bf16), sds((2, nd, deep, cut + q_cols), bf16), sds((2, nt, 64, rows), bf16),
            sds((64, width), bf16),
        ]
        + [sds((2,) + dealt_shape.shape, bf16), dealt_shape],
        in_specs=[SM] + [VM] * 5 + [hbm], out_specs=[VM] * 4 + [hbm] * 2,
        scratch_shapes=[
            pltpu.SemaphoreType.DMA((pushes,)), pltpu.SemaphoreType.DMA((2, nd)), pltpu.SemaphoreType.DMA((4,)),
            pltpu.SemaphoreType.DMA((len(later), 8)), pltpu.SemaphoreType.DMA((len(later), 8)),
        ],
        compiler_params=pltpu.CompilerParams(
            vmem_limit_bytes=VMEM_LIMIT, collective_id=0, has_side_effects=True
        ),
        cost_estimate=pl.CostEstimate(flops=10**7, bytes_accessed=100 * 2**20, transcendentals=0),
    )(lengths, tokens, gain_attn[None, :], routes.T, w_router, line, w_send)

    w_first = gather_weights(dealt_first, with_place)
    w_pair = gather_weights(dealt_pair, with_place)
    by_steps = members == local == 4
    w_last = dealt_last if by_steps else gather_weights(dealt_last, with_place)

    exponent = 2.0 * np.arange(HD // 2) / HD
    angles = np.arange(seq_len)[:, None] * np.exp(-math.log(rope_base) * exponent)[None, :]
    cosine, sine = np.cos(angles).astype(np.float32), np.sin(angles).astype(np.float32)
    cos_table = jnp.asarray(np.concatenate([cosine] * 4, axis=1))
    sin_table = jnp.asarray(np.concatenate([-sine, sine] * 2, axis=1))

    out_late = after(out_grad, w_attn)
    out_y, out_x = hop_y(out_late), hop_x(out_late)
    q_width, k_width = 2 * q_cols, 2 * kv_cols
    heads = q_width // HD
    q, k, v, ctx, lse, keep, send = call(
        attend_kernel,
        [
            sds((seq_len, q_width), bf16), sds((seq_len, k_width), bf16), sds((seq_len, k_width), bf16),
            sds((seq_len, q_width), bf16), sds((heads, seq_len), f32),
            sds((rows, width), bf16), sds((rows, width), bf16),
        ],
        12 * 10**9, 16 * 2**20,
        in_specs=[SM] + [VM] * 4, out_specs=[VM] * 7,
    )(lengths, normed_rows, w_attn, cos_table, sin_table)

    def remote_call(kernel, number, out_shape, flops, nbytes, **kw):
        return pl.pallas_call(
            kernel, out_shape=out_shape,
            compiler_params=pltpu.CompilerParams(
                vmem_limit_bytes=VMEM_LIMIT, collective_id=number, has_side_effects=True
            ),
            cost_estimate=pl.CostEstimate(flops=flops, bytes_accessed=nbytes, transcendentals=0),
            **kw,
        )

    slots_shape = (local, 8, cap, width)
    hidden_own, normed_mix, inverse_mix, gates_in, rows_in, grads_in, *moving = remote_call(
        functools.partial(mix_kernel, local, cap, int(by_steps)), 2,
        [
            sds((rows, width), f32), sds((rows, width), bf16), sds((rows, 1), f32),
            sds((local, 8, cap, 1), f32), sds(slots_shape, bf16), sds(slots_shape, bf16),
        ] + [dealt_shape] * (2 * by_steps),
        10**10, 100 * 2**20,
        in_specs=[SM] + [VM] * 9 + [hbm] * by_steps, out_specs=[VM] * 4 + [hbm] * (2 + 2 * by_steps),
        scratch_shapes=[
            pltpu.VMEM((8, rows, width), bf16), pltpu.VMEM((8, rows, width), bf16), pltpu.VMEM((rows, width), bf16),
            pltpu.VMEM((2, local, cap, width), bf16), pltpu.VMEM((64, rows), f32), pltpu.VMEM((64, rows), f32),
            dma((2, 9)), dma((2, 9)), dma((2,)), dma((2,)), dma((4,)),
        ],
    )(
        lengths, tokens, after(keep, w_first), send, gain_mixer[None, :], out_grad, out_y, out_x, ranks, router_t,
        *([dealt_last] if by_steps else []),
    )
    ys, dxs, dw_pairs = [], [], []
    arrived = (w_last, *moving)
    pair_shape = sds((members, 2, 8, 3, deep, quarter), bf16)
    before = []
    for e in range(local):
        step = e + 2 if by_steps and e + 2 < members else 0
        sources = ((w_first,), (w_pair,), (w_pair,), arrived)[e]
        inputs = [after(rows_in, *before), grads_in, gates_in, *sources, *(moving if step else ())]
        aliases = {}
        if e % 2:
            aliases = {len(inputs): 2}
            inputs.append(dw_pairs.pop())
        y, dx, dw, *moved = pl.pallas_call(
            functools.partial(expert_kernel, e, local, len(sources), step, len(sources) > 1),
            out_shape=[
                sds((8, cap, width), bf16), sds((8, cap, width + LANES), bf16), pair_shape,
            ] + [dealt_shape] * (2 if step else 0),
            in_specs=[hbm] * len(inputs),
            out_specs=[hbm] * (5 if step else 3),
            scratch_shapes=[
                pltpu.VMEM((8, cap, width), bf16), pltpu.VMEM((8, cap, width), bf16), pltpu.VMEM((8, cap, 1), f32),
                pltpu.VMEM((members, 8, 3, deep, quarter), bf16),
                pltpu.VMEM((8, cap, width), bf16), pltpu.VMEM((8, cap, width + LANES), bf16),
                pltpu.VMEM((members, 8, 3, deep, quarter), bf16),
                dma((3,)), dma((len(sources),)), dma((5,)), dma((4,)),
            ],
            input_output_aliases=aliases,
            compiler_params=pltpu.CompilerParams(
                vmem_limit_bytes=VMEM_LIMIT, **(dict(collective_id=3 + step, has_side_effects=True) if step else {})
            ),
            cost_estimate=pl.CostEstimate(flops=10**10, bytes_accessed=20 * 2**20, transcendentals=0),
        )(*inputs)
        if step:
            moving = tuple(moved)
            arrived += moving
        ys.append(y)
        dxs.append(dx)
        dw_pairs.append(dw)
        before = [y]

    wide = width + LANES
    grad_hidden, grad_branch, router_grad, gain_mix_grad, y_totals = remote_call(
        functools.partial(return_kernel, local, cap), 3,
        [
            sds((rows, width), f32), sds((2 * rows, width), bf16), sds((experts, width), f32), sds((1, width), f32),
            sds((4, rows, width), bf16),
        ],
        10**10, 100 * 2**20,
        in_specs=[hbm] * (2 * local) + [SM] + [VM] * 7, out_specs=[VM] * 5,
        scratch_shapes=[
            pltpu.VMEM((3, local * cap, wide), bf16),
            pltpu.VMEM((4, rows, wide), bf16), pltpu.VMEM((4, rows, wide), bf16), pltpu.VMEM((4, rows, wide), bf16),
            pltpu.VMEM((2, rows // 2, wide), bf16), pltpu.VMEM((2, rows, wide), bf16),
            pltpu.VMEM((4, rows, width), bf16), pltpu.VMEM((4, rows, width), bf16), pltpu.VMEM((64, rows), f32),
            dma((3, local)), dma((10,)), dma((10,)), dma((4,)), dma((4,)), dma((2,)),
        ],
    )(
        *dxs, *ys, lengths, ranks, normed_mix, hidden_own, inverse_mix, out_grad, w_router, gain_mixer[None, :],
    )
    chip_groups = [
        [with_place[side][a] * nt + y * 2 + c for side in range(2) for y in range(2)]
        for a in range(members) for c in range(2)
    ]
    y_terms = lax.all_to_all(y_totals, BOTH, 0, 0, tiled=True, axis_index_groups=chip_groups)
    mixed = (hidden_own + jnp.sum(y_terms.astype(f32), axis=0)).astype(bf16)

    dw_attn, keep_back, send_back = call(
        attend_back_kernel,
        [
            sds((2, nd, deep, cut + q_cols), bf16), sds((rows, width), bf16), sds((rows, width), bf16),
        ],
        25 * 10**9, 24 * 2**20,
        in_specs=[SM] + [VM] * 10, out_specs=[VM] * 3,
        scratch_shapes=[
            pltpu.VMEM((seq_len, q_width), bf16), pltpu.VMEM((seq_len, 2 * cut), bf16),
            pltpu.VMEM((seq_len, LANES), f32), pltpu.VMEM((seq_len, LANES), f32),
        ],
    )(
        lengths, normed_rows, grad_branch, w_attn, cos_table, sin_table,
        q, k, v, ctx, lse,
    )
    per_dp = (deep, cut + q_cols)
    sums = [
        lax.psum_scatter(dw, "dp", scatter_dimension=0, axis_index_groups=with_place) for dw in dw_pairs
    ]
    back_shape = sds((2, 8, 3, deep, quarter), bf16)
    doublings = (nd - 1).bit_length() - 1
    small_rows, part = experts + 8, width // 8
    grad_tokens, grad_router, gains, plane_grad, back_first = remote_call(
        tail_kernel, 8,
        [
            sds((rows, width), bf16), sds((width, experts), f32), sds((8, width), f32),
            sds((planes,) + per_dp, bf16), back_shape,
        ],
        10**8, 30 * 2**20,
        in_specs=[VM] * 8 + [hbm], out_specs=[VM] * 4 + [hbm],
        scratch_shapes=[pltpu.VMEM((rows, width), bf16)]
        + [pltpu.VMEM((planes,) + per_dp, bf16)] * 4
        + [
            pltpu.VMEM((small_rows, width), f32), pltpu.VMEM((3, small_rows, width), f32),
            pltpu.VMEM((small_rows, part), f32), pltpu.VMEM((doublings, small_rows, part), f32),
            pltpu.VMEM((8, small_rows, part), f32),
            dma((2,)), dma((3, planes)), dma((3, planes)), dma((3,)), dma((3,)), dma((2, 8)), dma((2, 8)),
            dma((doublings,)), dma((doublings,)), dma((8,)), dma((8,)),
        ],
    )(
        after(tokens, y_terms), keep_back, send_back, grad_hidden, gain_attn[None, :], router_grad, gain_mix_grad,
        dw_attn, sums[0],
    )
    expert_grad = sds((deep * experts, quarter), f32)
    grad_query, grad_keyval, grad_out, *expert_grads = remote_call(
        last_kernel, 9,
        [
            sds((deep, q_cols), f32), sds((deep, 2, kv_cols), f32), sds((deep, q_cols), f32),
            expert_grad, expert_grad, expert_grad,
        ],
        10**8, 30 * 2**20,
        in_specs=[VM] * 2 + [hbm], out_specs=[VM] * 6,
        scratch_shapes=[
            pltpu.VMEM((2, 8, 3, deep, quarter), bf16), pltpu.VMEM((planes - 1,) + per_dp, bf16),
            dma((planes - 1,)), dma((planes - 1,)), dma((2, 8)), dma((2, 8)),
        ],
    )(plane_grad, back_first, sums[1])
    grad_gate, grad_up, grad_down = (g.reshape(deep, experts, quarter) for g in expert_grads)

    return (
        mixed,
        grad_tokens,
        gains[1],
        grad_query,
        grad_keyval,
        grad_out,
        gains[0],
        grad_router,
        grad_gate,
        grad_up,
        grad_down,
    )


def solution(mesh):
    placed = (
        P(("dp", "tensor"), None),
        P("dp"),
        P("dp", None),
        P(),
        P("dp", "tensor"),
        P("dp", None, "tensor"),
        P("dp", "tensor"),
        P(),
        P(),
        P("dp", None, "tensor"),
        P("dp", None, "tensor"),
        P("dp", None, "tensor"),
        P(("dp", "tensor"), None),
    )
    return jax.shard_map(
        shards,
        mesh=mesh,
        in_specs=placed,
        out_specs=(
            P(("dp", "tensor"), None),
            P(("dp", "tensor"), None),
            P(),
            P("dp", "tensor"),
            P("dp", None, "tensor"),
            P("dp", "tensor"),
            P(),
            P(),
            P("dp", None, "tensor"),
            P("dp", None, "tensor"),
            P("dp", None, "tensor"),
        ),
        check_vma=False,
    )
```

```python
import functools
import math

import jax
import jax.numpy as jnp
import numpy as np
from jax import lax
from jax.experimental import pallas as pl
from jax.experimental.pallas import tpu as pltpu
from jax.sharding import PartitionSpec as P

HD = 64
LANES = 128
epsilon = 1e-06
rope_base = 10000.0
bf16 = jnp.bfloat16
f32 = jnp.float32
BOTH = ("dp", "tensor")
VMEM_LIMIT = 60 * 1024 * 1024
QBLK = 256


def dot(a, b, ca, cb):
    return lax.dot_general(a, b, (((ca,), (cb,)), ((), ())), preferred_element_type=f32)


def call(kernel, out_shape, flops, nbytes, **kw):
    return pl.pallas_call(
        kernel,
        out_shape=out_shape,
        compiler_params=pltpu.CompilerParams(vmem_limit_bytes=VMEM_LIMIT),
        cost_estimate=pl.CostEstimate(flops=flops, bytes_accessed=nbytes, transcendentals=0),
        **kw,
    )


def sds(shape, dtype):
    return jax.ShapeDtypeStruct(shape, dtype)


VM = pl.BlockSpec(memory_space=pltpu.VMEM)
SM = pl.BlockSpec(memory_space=pltpu.SMEM)


def hop(x, dp_bit, t_bits):
    nd, nt = lax.axis_size("dp"), lax.axis_size("tensor")
    pairs = [
        (d * nt + t, (d ^ dp_bit) * nt + (t ^ t_bits)) for d in range(nd) for t in range(nt)
    ]
    return lax.ppermute(x, BOTH, pairs)


def hop_c(x):
    return hop(x, 0, 1)


def hop_y(x):
    return hop(x, 0, 2)


def hop_x(x):
    return hop(x, 1, 0)


def after(x, *others):
    return lax.optimization_barrier((x, *others))[0]


def gather_weights(x, weight_groups):
    return lax.all_gather(x, "dp", axis_index_groups=weight_groups)


def swap_halves(v):
    lane = lax.broadcasted_iota(jnp.int32, v.shape, 1)
    left = pltpu.roll(v, LANES - HD // 2, 1)
    right = pltpu.roll(v, HD // 2, 1)
    return jnp.where(lane % HD < HD // 2, left, right)


def in_head(tile, h):
    lane = lax.broadcasted_iota(jnp.int32, tile.shape, 1)
    return (lane < HD) if h == 0 else (lane >= HD)


def only_head(tile, h):
    return jnp.where(in_head(tile, h), tile, jnp.zeros_like(tile))


def spread_head(tile, h):
    wide = tile.astype(f32)
    return jnp.where(in_head(wide, h), wide, pltpu.roll(wide, HD, 1)).astype(tile.dtype)


def stacked(tile):
    return jnp.concatenate([only_head(tile, 0), only_head(tile, 1)], axis=0)


def key_limit(start, rows, length):
    column = lax.broadcasted_iota(jnp.int32, (1, 2 * rows), 1)
    position = start + jnp.where(column >= rows, column - rows, column)
    return jnp.minimum(position, length - 1)


def scores_t(kd, qm, limit):
    raw = dot(kd, qm, 1, 1) * (1.0 / math.sqrt(HD))
    key = lax.broadcasted_iota(jnp.int32, raw.shape, 0)
    return jnp.where(key <= limit, raw, -1e30)


def attend_kernel(
    lengths, rows, w, cos, sin,
    q_ref, k_ref, v_ref, ctx_ref, lse_ref, keep_ref, send_ref,
):
    core = lax.axis_index("tensor") % 2
    length = lengths[lax.axis_index("tensor") // 2]
    seq, width = rows.shape
    half = seq // 2
    kw = k_ref.shape[1] // 2
    qw = 2 * kw
    cut = qw + 2 * kw
    for blk in range(seq // QBLK):
        sl = slice(blk * QBLK, (blk + 1) * QBLK)
        c, s = cos[sl], sin[sl]
        for y in range(2):
            pre = dot(rows[sl], w[y, :, :, :cut].reshape(width, cut), 1, 0)
            for tile in range((qw + kw) // LANES):
                col = pre[:, tile * LANES:(tile + 1) * LANES]
                turned = (col * c + swap_halves(col) * s).astype(bf16)
                if tile * LANES < qw:
                    q_ref[sl, y * qw + tile * LANES:y * qw + (tile + 1) * LANES] = turned
                else:
                    at = y * kw + tile * LANES - qw
                    k_ref[sl, at:at + LANES] = turned
            v_ref[sl, y * kw:(y + 1) * kw] = pre[:, qw + kw:].astype(bf16)
    for g in range(2 * qw // LANES):
        kv = slice(g // 2 * LANES, (g // 2 + 1) * LANES)
        cols = slice(g * LANES, (g + 1) * LANES)
        kd = spread_head(k_ref[:, kv], g % 2)
        vd_t = spread_head(v_ref[:, kv], g % 2).T
        for blk in range(seq // QBLK):
            top = (blk + 1) * QBLK
            sl = slice(blk * QBLK, top)
            s = scores_t(kd[:top], stacked(q_ref[sl, cols]), key_limit(blk * QBLK, QBLK, length))
            peak = jnp.max(s, axis=0, keepdims=True)
            e = jnp.exp(s - peak)
            total = jnp.sum(e, axis=0, keepdims=True)
            p = (e * (1.0 / total)).astype(bf16)
            ctx = dot(vd_t[:, :top], p, 1, 0).T
            tile = jnp.where(in_head(ctx[:QBLK], 0), ctx[:QBLK], ctx[QBLK:])
            ctx_ref[sl, cols] = tile.astype(bf16)
            lse = peak + jnp.log(total)
            lse_ref[2 * g:2 * g + 1, sl] = lse[:, :QBLK]
            lse_ref[2 * g + 1:2 * g + 2, sl] = lse[:, QBLK:]
    for out_ref, side in ((send_ref, 1 - core), (keep_ref, core)):
        at = pl.ds(pl.multiple_of(side * half, half), half)
        out = dot(ctx_ref[at, :qw], w[0, :, :, cut:].reshape(width, qw), 1, 1)
        out += dot(ctx_ref[at, qw:], w[1, :, :, cut:].reshape(width, qw), 1, 1)
        out_ref[...] = out.astype(bf16)


def attend_back_kernel(
    lengths, rows, gb_ref, w, cos, sin, q_ref, k_ref, v_ref, ctx_ref, lse_ref,
    dw_ref, keep_ref, send_ref,
    gc_ref, dqkv_ref, dk_ref, dv_ref,
):
    core = lax.axis_index("tensor") % 2
    length = lengths[lax.axis_index("tensor") // 2]
    seq, width = rows.shape
    half = seq // 2
    kw = k_ref.shape[1] // 2
    qw = 2 * kw
    cut = qw + 2 * kw
    per_dp = dw_ref.shape[1:3]
    at_own = pl.ds(pl.multiple_of(core * half, half), half)
    at_peer = pl.ds(pl.multiple_of((1 - core) * half, half), half)
    for y in range(2):
        part = slice(y * qw, (y + 1) * qw)
        gc_ref[:, part] = dot(gb_ref[...], w[y, :, :, cut:].reshape(width, qw), 1, 0).astype(bf16)
        dw_ref[y, :, :, cut:] = dot(gb_ref[...], ctx_ref[:, part], 0, 0).astype(bf16).reshape(per_dp + (qw,))
    scale = 1.0 / math.sqrt(HD)
    folded = None
    for g in range(2 * qw // LANES):
        y = g // 2
        kv = slice(y * LANES, (y + 1) * LANES)
        cols = slice(g * LANES, (g + 1) * LANES)
        kd = spread_head(k_ref[:, kv], g % 2)
        kd_t = kd.T
        vd = spread_head(v_ref[:, kv], g % 2)
        for blk in reversed(range(seq // QBLK)):
            top = (blk + 1) * QBLK
            sl = slice(blk * QBLK, top)
            qm = stacked(q_ref[sl, cols])
            gm = stacked(gc_ref[sl, cols])
            s = scores_t(kd[:top], qm, key_limit(blk * QBLK, QBLK, length))
            lse = jnp.concatenate([lse_ref[2 * g:2 * g + 1, sl], lse_ref[2 * g + 1:2 * g + 2, sl]], axis=1)
            p = jnp.exp(s - lse)
            gw = dot(vd[:top], gm, 1, 1)
            centre = jnp.sum(p * gw, axis=0, keepdims=True)
            ds = (p * (gw - centre) * scale).astype(bf16)
            dv = dot(p.astype(bf16), gm, 1, 0)
            dk = dot(ds, qm, 1, 0)
            dq = dot(kd_t[:, :top], ds, 1, 0).T
            if top == seq:
                dk_ref[...] = dk
                dv_ref[...] = dv
            else:
                dk_ref[:top] += dk
                dv_ref[:top] += dv
            tile = jnp.where(in_head(dq[:QBLK], 0), dq[:QBLK], dq[QBLK:])
            back = tile * cos[sl] - swap_halves(tile) * sin[sl]
            at = y * cut + g % 2 * LANES
            dqkv_ref[sl, at:at + LANES] = back.astype(bf16)
        dk_all = dk_ref[...] + pltpu.roll(dk_ref[...], HD, 1)
        dv_all = dv_ref[...] + pltpu.roll(dv_ref[...], HD, 1)
        if g % 2 == 0:
            folded = (dk_all, dv_all)
        else:
            dk_pair = jnp.where(in_head(dk_all, 0), folded[0], dk_all)
            dv_pair = jnp.where(in_head(dv_all, 0), folded[1], dv_all)
            at = y * cut + qw
            back = dk_pair * cos[...] - swap_halves(dk_pair) * sin[...]
            dqkv_ref[:, at:at + LANES] = back.astype(bf16)
            dqkv_ref[:, at + LANES:at + 2 * LANES] = dv_pair.astype(bf16)
            part = slice(y * cut, (y + 1) * cut)
            dw_ref[y, :, :, :cut] = dot(rows[...], dqkv_ref[:, part], 0, 0).astype(bf16).reshape(per_dp + (cut,))
    for out_ref, at in ((send_ref, at_peer), (keep_ref, at_own)):
        out = dot(dqkv_ref[at, :cut], w[0, :, :, :cut].reshape(width, cut), 1, 1)
        out += dot(dqkv_ref[at, cut:], w[1, :, :, :cut].reshape(width, cut), 1, 1)
        out_ref[...] = out.astype(bf16)


def own_place():
    return lax.axis_index("dp") % 2 * 4 + lax.axis_index("tensor")


def plane_devices():
    d, p = lax.axis_index("dp"), own_place()
    return [{"dp": d + ((p ^ j) // 4 - p // 4), "tensor": (p ^ j) % 4} for j in range(8)]


def deal_out(p, plane_peers, w_send, numbers, dealt, send_sem, recv_sem):
    copies = []
    for i, e in enumerate(numbers):
        for j in (6, 7, 2, 4, 3, 5, 1):
            copies.append(
                pltpu.make_async_remote_copy(
                    src_ref=w_send.at[p ^ j, e], dst_ref=dealt[i].at[j], send_sem=send_sem.at[i, j],
                    recv_sem=recv_sem.at[i, j], device_id=plane_peers[j], device_id_type=pl.DeviceIdType.MESH,
                )
            )
        copies.append(pltpu.make_async_copy(w_send.at[p, e], dealt[i].at[0], send_sem.at[i, 0]))
    for copy in copies:
        copy.start()
    return copies


def deal_kernel(w_send, w_mine, *refs):
    pair, line_ref, send_sem, recv_sem, line_send, line_recv = refs
    d, t = lax.axis_index("dp"), lax.axis_index("tensor")
    planes = line_ref.shape[0]
    z, x = d // 2, d % 2
    p = own_place()
    peers = plane_devices()
    z_peers = [{"dp": lax.rem(z + k, planes) * 2 + x, "tensor": t} for k in range(1, planes)]
    greet((*peers[1:], *z_peers))
    lines = []
    for k, peer in enumerate(z_peers):
        copy = remote(w_mine, line_ref.at[z], line_send.at[k], line_recv.at[z], peer)
        copy.start()
        lines.append(copy)
    copies = deal_out(p, peers, w_send, (0, 1), (pair.at[0], pair.at[1]), send_sem, recv_sem)
    line_ref[z] = w_mine[...]
    for copy in copies:
        copy.wait()
    for k in range(1, planes):
        lines[k - 1].wait_send()
        at = lax.rem(z + k, planes)
        remote(line_ref.at[at], line_ref.at[at], line_send.at[0], line_recv.at[at], peers[1]).wait_recv()


def group_rows_of(experts):
    local = experts // 8
    row = lax.broadcasted_iota(jnp.int32, (64, experts), 0)
    expert = lax.broadcasted_iota(jnp.int32, (64, experts), 1)
    return ((row % 8 < local) & (row // 8 * local + row % 8 == expert)).astype(f32).astype(bf16)


def rank_rows(lengths, routes_t, block, ranks_ref):
    blocks, wide = ranks_ref.shape[1:3]
    seq_len = block * blocks // lengths.shape[0]
    local = wide // 16
    row = lax.broadcasted_iota(jnp.int32, (wide, block), 0)
    number = jnp.where(row % 8 < local, row // 8 * local + row % 8, -1)
    low = lax.broadcasted_iota(jnp.int32, (block, block), 0)
    high = lax.broadcasted_iota(jnp.int32, (block, block), 1)
    before = (low < high).astype(f32).astype(bf16)
    for b in range(blocks):
        at = slice(b * block, (b + 1) * block)
        position = lax.broadcasted_iota(jnp.int32, (wide, block), 1) + b * block % seq_len
        hit = jnp.zeros((wide, block), jnp.bool_)
        for k in range(routes_t.shape[0]):
            hit = hit | (routes_t[k:k + 1, at] == number)
        hit = hit & (position < lengths[b * block // seq_len])
        earlier = dot(hit.astype(f32).astype(bf16), before, 1, 0)
        ranks_ref[0, b] = jnp.where(hit, earlier, -1.0).astype(bf16)


def gather_kernel(
    later, lengths, tokens, gain, routes_t, router, line, w_send, rows_ref, w_ref, ranks_ref, router_ref, *refs
):
    dealt, (send_sem, recv_sem, row_sem, deal_send, deal_recv) = refs[:-5], refs[-5:]
    planes = line.shape[0]
    half = tokens.shape[0]
    x, core = lax.axis_index("dp") % 2, lax.axis_index("tensor") % 2
    p, plane_peers = own_place(), plane_devices()
    x_peer, y_peer, core_peer = neighbours()
    greet(plane_peers[1:])
    copies = []

    def push(source, side, dp, peer):
        copy = remote(source, w_ref.at[side, dp], send_sem.at[len(copies)], recv_sem.at[side, dp], peer)
        copy.start()
        copies.append(copy)

    def arrive(side, dp):
        slot = w_ref.at[side, dp]
        remote(slot, slot, send_sem.at[0], recv_sem.at[side, dp], x_peer).wait_recv()

    near = [k * 2 + x for k in range(planes)]
    over = [k * 2 + 1 - x for k in range(planes)]
    for k in range(planes):
        push(line.at[k], 0, near[k], x_peer)
        push(line.at[k], 1, near[k], y_peer)
    deals = deal_out(p, plane_peers, w_send, later, dealt, deal_send, deal_recv)
    values = tokens[...].astype(f32)
    inverse = lax.rsqrt(jnp.mean(values * values, axis=1, keepdims=True) + epsilon)
    at = pl.ds(pl.multiple_of(core * half, half), half)
    rows_ref[at] = (values * inverse * gain[...]).astype(bf16)
    row_copy = remote(rows_ref.at[at], rows_ref.at[at], row_sem.at[0], row_sem.at[1], core_peer)
    row_copy.start()
    rank_rows(lengths, routes_t, half, ranks_ref)
    rank_copy = remote(ranks_ref.at[0], ranks_ref.at[1], row_sem.at[2], row_sem.at[3], x_peer)
    rank_copy.start()
    router_ref[...] = dot(group_rows_of(router.shape[1]), router[...], 1, 1).astype(bf16)
    for k in range(planes):
        w_ref[0, near[k]] = line[k]
    for k in range(planes):
        arrive(0, over[k])
        if k < planes // 2:
            push(w_ref.at[0, over[k]], 1, over[k], y_peer)
        arrive(1, near[k])
        if k >= planes // 2:
            push(w_ref.at[1, near[k]], 1, near[k], x_peer)
    for k in range(planes):
        arrive(1, over[k])
    for copy in copies:
        copy.wait_send()
    row_copy.wait()
    rank_copy.wait()
    for copy in deals:
        copy.wait()


def masked_shares(logits, hit, axis):
    peak = jnp.max(jnp.where(hit, logits, -1e30), axis=axis, keepdims=True)
    e = jnp.where(hit, jnp.exp(jnp.where(hit, logits - peak, 0.0)), 0.0)
    total = jnp.sum(e, axis=axis, keepdims=True)
    return e / jnp.where(total > 0.0, total, 1.0)


def split16(v):
    high = v.astype(bf16)
    return high, (v - high.astype(f32)).astype(bf16)


def neighbours():
    peers = plane_devices()
    return peers[4], peers[2], peers[1]


def greet(peers):
    barrier = pltpu.get_barrier_semaphore()
    for peer in peers:
        pl.semaphore_signal(barrier, inc=1, device_id=peer, device_id_type=pl.DeviceIdType.MESH)
    pl.semaphore_wait(barrier, len(peers))


def remote(source, target, send_sem, recv_sem, peer):
    return pltpu.make_async_remote_copy(
        src_ref=source, dst_ref=target, send_sem=send_sem, recv_sem=recv_sem,
        device_id=peer, device_id_type=pl.DeviceIdType.MESH,
    )


def live_rows(lengths, rows):
    first = lax.axis_index("tensor") * rows
    seq_len = 4 * rows // lengths.shape[0]
    position = lax.rem(first, seq_len) + lax.broadcasted_iota(jnp.int32, (rows, 1), 0)
    return (position < lengths[first // seq_len]).astype(f32)


def z_steps(step, up_from, down_from, up_to, down_to, sem):
    d, t = lax.axis_index("dp"), lax.axis_index("tensor")
    planes = lax.axis_size("dp") // 2
    z = d // 2
    above = {"dp": lax.rem(z + 1, planes) * 2 + d % 2, "tensor": t}
    below = {"dp": lax.rem(z + planes - 1, planes) * 2 + d % 2, "tensor": t}
    up = remote(up_from, up_to, sem.at[0], sem.at[1], above)
    down = remote(down_from, down_to, sem.at[2], sem.at[3], below)
    steps = (
        (up, (z >= step - 1) & (z < planes - 1), z >= step),
        (down, (z > 0) & (z <= planes - step), z < planes - step),
    )
    return steps, above, below


def start_steps(steps):
    for copy, sends, _ in steps:
        pl.when(sends)(copy.start)


def settle_steps(steps):
    for copy, sends, receives in steps:
        pl.when(sends)(copy.wait_send)
        pl.when(receives)(copy.wait_recv)


def block_ranks(ranks, j):
    return ranks[j // 4, lax.axis_index("tensor") ^ (j % 4)].astype(f32)


def own_group():
    return pl.multiple_of(own_place() * 8, 8)


def placing(ranks, cap):
    slot = lax.broadcasted_iota(jnp.int32, (cap, ranks.shape[1]), 0).astype(f32)
    return [(slot == ranks[e:e + 1]).astype(f32) for e in range(ranks.shape[0])]


def mix_kernel(
    local, cap, carry, lengths, tokens, keep, send, gain, out_own, out_y, out_x, ranks, router_t, *refs
):
    if carry:
        moving, refs = refs[0], refs[1:]
        (up_to, down_to), refs = refs[6:8], refs[:6] + refs[8:]
    (
        hidden_ref, normed_ref, inv_ref, gates_ref, x_hbm, g_hbm,
        normed_buf, out_buf, got_ref, stage_ref, ranks_ref, shares_ref,
        send_sem, recv_sem, core_sem, stage_sem, z_sem,
    ) = refs
    x_peer, y_peer, core_peer = neighbours()
    if carry:
        steps, above, below = z_steps(carry, moving, moving, up_to, down_to, z_sem)
        greet((x_peer, y_peer, core_peer, above, below))
    else:
        greet((x_peer, y_peer, core_peer))
    rows = tokens.shape[0]
    low, high = pl.ds(0, rows // 2), pl.ds(rows // 2, rows // 2)
    sent = []

    def push(kind, source, target, slot, peer):
        copy = remote(source, target, send_sem.at[kind, slot], recv_sem.at[kind, slot], peer)
        copy.start()
        sent.append(copy)

    def arrive(kind, target, slot):
        remote(target, target, send_sem.at[kind, slot], recv_sem.at[kind, slot], x_peer).wait_recv()

    core_copy = remote(send, got_ref, core_sem.at[0], core_sem.at[1], core_peer)
    core_copy.start()
    if carry:
        start_steps(steps)
    push(1, out_y.at[low], out_buf.at[6, low], 6, x_peer)
    push(1, out_x.at[high], out_buf.at[6, high], 8, y_peer)
    push(1, out_own, out_buf.at[1], 1, core_peer)
    push(1, out_y, out_buf.at[3], 3, core_peer)
    push(1, out_x, out_buf.at[5], 5, core_peer)
    core_copy.wait()
    branch = keep[...].astype(f32) + got_ref[...].astype(f32)
    hidden = tokens[...].astype(f32) + live_rows(lengths, rows) * branch
    inverse = lax.rsqrt(jnp.mean(hidden * hidden, axis=1, keepdims=True) + epsilon)
    hidden_ref[...] = hidden
    inv_ref[...] = inverse
    normed = (hidden * inverse * gain[...]).astype(bf16)
    normed_ref[...] = normed
    normed_buf[0] = normed
    own = normed_buf.at[0]
    push(0, own, normed_buf.at[2], 2, y_peer)
    push(0, own, normed_buf.at[4], 4, x_peer)
    push(0, own, normed_buf.at[1], 1, core_peer)

    staged = []

    def place(kind, j, source):
        n = len(staged)
        if n >= 2:
            staged[n - 2].wait()
        group = own_group()
        ranks_ref[...] = block_ranks(ranks, j)
        places = placing(ranks_ref[pl.ds(group, 8)][:local], cap)
        if kind == 0:
            logits = dot(router_t[...], source[...], 1, 1)
            shares_ref[...] = masked_shares(logits, ranks_ref[...] >= 0.0, 0)
            shares = shares_ref[pl.ds(group, 8)]
            for e in range(local):
                gates_ref[e, j] = jnp.sum(places[e] * shares[e:e + 1], axis=1, keepdims=True)
        matrix = jnp.concatenate([m.astype(bf16) for m in places], axis=0)
        placed = dot(matrix, source[...], 1, 0).astype(bf16)
        stage_ref[n % 2] = placed.reshape(local, cap, -1)
        copy = pltpu.make_async_copy(
            stage_ref.at[n % 2], (x_hbm if kind == 0 else g_hbm).at[:, j], stage_sem.at[n % 2]
        )
        copy.start()
        staged.append(copy)

    place(1, 0, out_own)
    place(1, 2, out_y)
    place(1, 4, out_x)
    place(0, 0, own)
    for j in (1, 3, 5):
        arrive(1, out_buf.at[j], j)
        place(1, j, out_buf.at[j])
    arrive(1, out_buf.at[6, low], 6)
    arrive(1, out_buf.at[6, high], 8)
    push(1, out_buf.at[6], out_buf.at[7], 7, core_peer)
    arrive(0, normed_buf.at[1], 1)
    place(0, 1, normed_buf.at[1])
    place(1, 6, out_buf.at[6])
    arrive(0, normed_buf.at[2], 2)
    push(0, normed_buf.at[2, low], normed_buf.at[6, low], 6, x_peer)
    push(0, normed_buf.at[2], normed_buf.at[3], 3, core_peer)
    arrive(0, normed_buf.at[4], 4)
    push(0, normed_buf.at[4, high], normed_buf.at[6, high], 8, y_peer)
    push(0, normed_buf.at[4], normed_buf.at[5], 5, core_peer)
    arrive(1, out_buf.at[7], 7)
    place(1, 7, out_buf.at[7])
    place(0, 2, normed_buf.at[2])
    place(0, 4, normed_buf.at[4])
    for j in (3, 5):
        arrive(0, normed_buf.at[j], j)
        place(0, j, normed_buf.at[j])
    arrive(0, normed_buf.at[6, low], 6)
    arrive(0, normed_buf.at[6, high], 8)
    push(0, normed_buf.at[6], normed_buf.at[7], 7, core_peer)
    place(0, 6, normed_buf.at[6])
    arrive(0, normed_buf.at[7], 7)
    place(0, 7, normed_buf.at[7])
    for copy in sent:
        copy.wait_send()
    for copy in staged[-2:]:
        copy.wait()
    if carry:
        settle_steps(steps)


def return_kernel(local, cap, *refs):
    dxs, ys, refs = refs[:local], refs[local:2 * local], refs[2 * local:]
    (
        lengths, ranks, normed, hidden_in, inv, out_grad, router, gain,
        grad_hidden_ref, branch_ref, router_grad_ref, gain_grad_ref, y_ref,
        load_ref, part_ref, core_ref, total_ref, diag_ref, last_ref, y_part, y_core, ranks_ref,
        load_sem, send_sem, recv_sem, y_send, y_recv, branch_sem,
    ) = refs
    x_peer, y_peer, core_peer = neighbours()
    core = lax.axis_index("tensor") % 2
    greet((x_peer, y_peer, core_peer))
    rows, width = normed.shape
    wide = part_ref.shape[-1]
    half = rows // 2
    low, high = pl.ds(0, half), pl.ds(half, half)
    order = [(0, j) for j in (7, 6, 5, 4, 3, 2, 1, 0)] + [(1, j) for j in (7, 5, 3, 1, 6, 4, 2, 0)]
    depth = load_ref.shape[0]
    sent = []

    def loads(n):
        kind, j = order[n]
        slot = n % depth
        cols = wide if kind == 0 else width
        return [
            pltpu.make_async_copy(
                (ys if kind else dxs)[e].at[j],
                load_ref.at[slot, pl.ds(e * cap, cap), pl.ds(0, cols)], load_sem.at[slot, e],
            )
            for e in range(local)
        ]

    def start(n):
        if n < len(order):
            for copy in loads(n):
                copy.start()

    for n in range(depth - 1):
        start(n)
    done = [0]

    def combined():
        n = done[0]
        done[0] += 1
        start(n + depth - 1)
        for copy in loads(n):
            copy.wait()
        kind, j = order[n]
        ranks_ref[...] = block_ranks(ranks, j)
        places = placing(ranks_ref[pl.ds(own_group(), 8)][:local], cap)
        matrix = jnp.concatenate([m.astype(bf16) for m in places], axis=0)
        values = load_ref[n % depth] if kind == 0 else load_ref[n % depth, :, :width]
        return dot(matrix, values, 0, 0)

    def push(source, target, n, peer):
        copy = remote(source, target, send_sem.at[n], recv_sem.at[n], peer)
        copy.start()
        sent.append(copy)

    def arrive(target, n):
        remote(target, target, send_sem.at[n], recv_sem.at[n], x_peer).wait_recv()

    def far_core(k):
        part_ref[k] = combined().astype(bf16)
        push(part_ref.at[k], core_ref.at[k], k, core_peer)

    def near_core(k):
        mine = combined()
        arrive(core_ref.at[k], k)
        return mine + core_ref[k].astype(f32)

    far_core(3)
    total_ref[2] = near_core(3).astype(bf16)
    push(total_ref.at[2, low], diag_ref.at[0], 4, x_peer)
    push(total_ref.at[2, high], diag_ref.at[1], 5, y_peer)
    far_core(2)
    total_ref[1] = near_core(2).astype(bf16)
    push(total_ref.at[1, low], last_ref.at[0, low], 6, x_peer)
    far_core(1)
    total_ref[0] = near_core(1).astype(bf16)
    push(total_ref.at[0, high], last_ref.at[1, high], 7, y_peer)
    far_core(0)
    part_own = near_core(0).astype(bf16)
    y_copies = []
    total_ref[3] = part_own

    def y_far(k):
        y_part[k] = combined().astype(bf16)
        copy = remote(y_part.at[k], y_core.at[k], y_send.at[k], y_recv.at[k], core_peer)
        copy.start()
        y_copies.append(copy)

    y_far(3)
    y_far(2)
    arrive(diag_ref.at[1], 5)
    total_ref[1, high] = (total_ref[1, high].astype(f32) + diag_ref[1].astype(f32)).astype(bf16)
    push(total_ref.at[1, high], last_ref.at[0, high], 8, x_peer)
    arrive(diag_ref.at[0], 4)
    total_ref[0, low] = (total_ref[0, low].astype(f32) + diag_ref[0].astype(f32)).astype(bf16)
    push(total_ref.at[0, low], last_ref.at[1, low], 9, y_peer)
    y_far(1)
    y_far(0)
    for k in (3, 2, 1, 0):
        mine = combined()
        y_copies[3 - k].wait()
        y_ref[k ^ (own_place() // 2)] = (mine + y_core[k].astype(f32)).astype(bf16)

    experts = router.shape[1]
    hit_rows = (block_ranks(ranks, 0) >= 0.0).astype(f32).astype(bf16)
    hit = dot(hit_rows, group_rows_of(experts), 0, 0) > 0.0
    shares = masked_shares(dot(normed[...], router[...], 1, 0), hit, 1)
    arrive(last_ref.at[0, low], 6)
    arrive(last_ref.at[1, high], 7)
    arrive(last_ref.at[0, high], 8)
    arrive(last_ref.at[1, low], 9)
    for copy in sent:
        copy.wait_send()

    def summed(lo, hi):
        cols = pl.ds(lo, hi - lo)
        return (
            total_ref[3, :, cols].astype(f32) + last_ref[0, :, cols].astype(f32) + last_ref[1, :, cols].astype(f32)
        )

    grad_shares = jnp.where(hit, summed(width, wide)[:, :experts], 0.0)
    grad_chosen = shares * (grad_shares - jnp.sum(shares * grad_shares, axis=1, keepdims=True))
    top, rest = split16(grad_chosen)
    hidden, inverse = hidden_in[...], inv[...]
    grad_mix = summed(0, width) + dot(top, router[...], 1, 1) + dot(rest, router[...], 1, 1)
    weighted = grad_mix * gain[...]
    centre = jnp.mean(hidden * weighted, axis=1, keepdims=True)
    grad_hidden = out_grad[...].astype(f32) + inverse * weighted - hidden * (inverse * inverse * inverse * centre)
    grad_hidden_ref[...] = grad_hidden
    at = pl.ds(pl.multiple_of(core * rows, rows), rows)
    branch_ref[at] = (live_rows(lengths, rows) * grad_hidden).astype(bf16)
    branch_copy = remote(branch_ref.at[at], branch_ref.at[at], branch_sem.at[0], branch_sem.at[1], core_peer)
    branch_copy.start()
    gain_grad_ref[...] = jnp.sum(grad_mix * hidden * inverse, axis=0, keepdims=True)
    router_grad_ref[...] = dot(top, normed[...], 0, 0) + dot(rest, normed[...], 0, 0)
    branch_copy.wait()


def expert_kernel(expert, local, steps, carry, chained, x_hbm, g_hbm, gates_hbm, *refs):
    sources, refs = refs[:steps], refs[steps:]
    if carry:
        (up_from, down_from), refs = refs[:2], refs[2:]
    if expert % 2:
        refs = refs[1:]
    if carry:
        (up_to, down_to), refs = refs[3:5], refs[:3] + refs[5:]
    y_hbm, dx_hbm, dw_hbm, x_ref, g_ref, gates_ref, w_buf, y_ref, dx_ref, dw_ref, in_sem, w_sem, out_sem, z_sem = refs
    d, t, p = lax.axis_index("dp"), lax.axis_index("tensor"), own_place()
    members, _, _, deep, quarter = w_buf.shape
    blocks = [(dp // 2, dp % 2 * 4) for dp in range(2 * members)]
    z = d // 2
    if carry:
        steps_out, above, below = z_steps(carry, up_from, down_from, up_to, down_to, z_sem)
        greet((above, below))
        start_steps(steps_out)

    def fetch(act):
        if not chained:
            source = sources[0].at[:, expert] if expert < 2 else sources[0]
            act(pltpu.make_async_copy(source, w_buf, w_sem.at[0]))
            return
        act(pltpu.make_async_copy(sources[0], w_buf.at[z], w_sem.at[0]))
        for n, source in enumerate(sources[1:]):
            origin = z - (n // 2 + 1) if n % 2 == 0 else z + n // 2 + 1

            @pl.when((origin >= 0) & (origin < members))
            def _():
                act(pltpu.make_async_copy(source, w_buf.at[origin], w_sem.at[n + 1]))

    x_copy = pltpu.make_async_copy(x_hbm.at[expert], x_ref, in_sem.at[0])
    g_copy = pltpu.make_async_copy(g_hbm.at[expert], g_ref, in_sem.at[1])
    gates_copy = pltpu.make_async_copy(gates_hbm.at[expert], gates_ref, in_sem.at[2])
    x_copy.start()
    fetch(lambda copy: copy.start())
    g_copy.start()
    gates_copy.start()
    slots, width = x_ref.shape[0] * x_ref.shape[1], x_ref.shape[2]

    def weight(which):
        rows = [
            jnp.concatenate([w_buf[at, (side + q) ^ p, which] for q in range(4)], axis=1) for at, side in blocks
        ]
        return jnp.concatenate(rows, axis=0)

    outs = []

    def send(source, target):
        copy = pltpu.make_async_copy(source, target, out_sem.at[len(outs)])
        copy.start()
        outs.append(copy)

    x_copy.wait()
    fetch(lambda copy: copy.wait())
    x = x_ref[...].reshape(slots, width)
    w_gate, w_up, w_down = weight(0), weight(1), weight(2)
    gate_lin = dot(x, w_gate, 1, 0)
    up_lin = dot(x, w_up, 1, 0)
    g_copy.wait()
    gates_copy.wait()
    g = g_ref[...].reshape(slots, width)
    gates = gates_ref[...].reshape(slots, 1)
    grad_scaled = dot(g, w_down, 1, 0)
    sigmoid = 1.0 / (1.0 + jnp.exp(-gate_lin))
    silu = gate_lin * sigmoid
    product = silu * up_lin
    grad_gates = jnp.sum(grad_scaled * product, axis=1, keepdims=True)
    scaled_hidden = (gates * product).astype(bf16)
    grad_act = gates * grad_scaled
    grad_gate_lin = (grad_act * up_lin * sigmoid * (1.0 + gate_lin * (1.0 - sigmoid))).astype(bf16)
    grad_up_lin = (grad_act * silu).astype(bf16)
    y_ref[...] = dot(scaled_hidden, w_down, 1, 1).astype(bf16).reshape(y_ref.shape)
    send(y_ref, y_hbm)
    dx = dot(grad_gate_lin, w_gate, 1, 1) + dot(grad_up_lin, w_up, 1, 1)
    dx_ref[:, :, :width] = dx.astype(bf16).reshape(y_ref.shape)
    lane = lax.broadcasted_iota(jnp.int32, (slots, LANES), 1)
    tail = jnp.where(lane == p * local + expert, grad_gates, 0.0).astype(bf16)
    dx_ref[:, :, width:] = tail.reshape(dx_ref.shape[:2] + (LANES,))
    send(dx_ref, dx_hbm)
    for which, (left, right) in enumerate(((x, grad_gate_lin), (x, grad_up_lin), (g, scaled_hidden))):
        grad = dot(left, right, 0, 0).astype(bf16)
        for dp, (at, side) in enumerate(blocks):
            for q in range(4):
                dw_ref[at, side + q, which] = grad[dp * deep:(dp + 1) * deep, q * quarter:(q + 1) * quarter]
        send(dw_ref.at[:, :, which], dw_hbm.at[:, expert % 2, :, which])
    for copy in outs:
        copy.wait()
    if carry:
        settle_steps(steps_out)


def all_peers(d, t, planes):
    peers = [{"dp": d, "tensor": t ^ 1}, {"dp": d, "tensor": t ^ 2}]
    bit = 1
    while bit < 2 * planes:
        peers.append({"dp": d ^ bit, "tensor": t})
        bit *= 2
    return peers


def push_back(p, plane_peers, sums, back_ref, send_sem, recv_sem):
    copies = []
    for e in range(2):
        for j in (6, 7, 2, 4, 3, 5, 1):
            copies.append(
                remote(sums.at[e, p ^ j], back_ref.at[e, p], send_sem.at[e, j], recv_sem.at[e, j], plane_peers[j])
            )
        copies.append(pltpu.make_async_copy(sums.at[e, p], back_ref.at[e, p], send_sem.at[e, 0]))
    for copy in copies:
        copy.start()
    return copies


def settle_back(p, plane_peers, copies, back_ref, send_sem, recv_sem):
    for e in range(2):
        for n, j in enumerate((6, 7, 2, 4, 3, 5, 1)):
            copies[8 * e + n].wait_send()
            slot = back_ref.at[e, p ^ j]
            remote(slot, slot, send_sem.at[e, j], recv_sem.at[e, j], plane_peers[1]).wait_recv()
        copies[8 * e + 7].wait()


def tail_kernel(
    tokens, keep, send, grad_hidden, gain, router_grad, gain_mix_grad, dw, sums,
    out_ref, router_ref, gains_ref, plane_ref, back_ref,
    got_ref, first_ref, second_ref, diag_ref, own_ref, small_ref, small_buf, part_ref, part_buf, parts_ref,
    core_sem, send_sem, recv_sem, small_send, small_recv, back_send, back_recv,
    part_send, part_recv, parts_send, parts_recv,
):
    d, t = lax.axis_index("dp"), lax.axis_index("tensor")
    planes = dw.shape[1] // 2
    half = planes // 2
    x = d % 2
    doubling = all_peers(d, t, planes)
    core_peer, y_peer, x_peer = doubling[:3]
    p, plane_peers = own_place(), plane_devices()
    greet((*plane_peers[1:], *doubling[3:]))
    experts = router_grad.shape[0]
    sent = []

    def push(source, target, kind, k, peer):
        copy = remote(source, target, send_sem.at[kind, k], recv_sem.at[kind, k], peer)
        copy.start()
        sent.append(copy)

    def arrive(target, kind, k):
        remote(target, target, send_sem.at[kind, k], recv_sem.at[kind, k], x_peer).wait_recv()

    core_copy = remote(send, got_ref, core_sem.at[0], core_sem.at[1], core_peer)
    core_copy.start()
    near = [k * 2 + x for k in range(planes)]
    over = [k * 2 + 1 - x for k in range(planes)]
    for k in range(half):
        push(dw.at[1, over[k]], diag_ref.at[k], 2, k, x_peer)
        push(dw.at[1, over[half + k]], diag_ref.at[half + k], 2, half + k, y_peer)
    for k in range(half):
        push(dw.at[0, over[k]], first_ref.at[k], 0, k, x_peer)
        push(dw.at[1, near[half + k]], second_ref.at[half + k], 1, half + k, y_peer)
    core_copy.wait()
    source = tokens[...].astype(f32)
    inverse = lax.rsqrt(jnp.mean(source * source, axis=1, keepdims=True) + epsilon)
    grad = keep[...].astype(f32) + got_ref[...].astype(f32)
    gain_grad = jnp.sum(grad * source * inverse, axis=0, keepdims=True)
    small_ref[:experts] = router_grad[...]
    row = lax.broadcasted_iota(jnp.int32, (8, small_ref.shape[1]), 0)
    small_ref[experts:] = jnp.where(row == 0, gain_mix_grad[...], jnp.where(row == 1, gain_grad, 0.0))

    def small_start(n):
        copy = remote(small_ref, small_buf.at[n], small_send.at[n], small_recv.at[n], doubling[n])
        copy.start()
        return copy

    def small_end(n, copy):
        copy.wait()
        small_ref[...] = small_ref[...] + small_buf[n]

    running = small_start(0)
    weighted = grad * gain[...]
    centre = jnp.mean(source * weighted, axis=1, keepdims=True)
    total = grad_hidden[...] + inverse * weighted - source * (inverse * inverse * inverse * centre)
    out_ref[...] = total.astype(bf16)
    small_end(0, running)
    running = small_start(1)
    for k in range(half):
        arrive(diag_ref.at[k], 2, k)
        own_ref[k] = (dw[1, near[k]].astype(f32) + diag_ref[k].astype(f32)).astype(bf16)
        push(own_ref.at[k], second_ref.at[k], 1, k, y_peer)
        arrive(diag_ref.at[half + k], 2, half + k)
        own_ref[half + k] = (dw[0, over[half + k]].astype(f32) + diag_ref[half + k].astype(f32)).astype(bf16)
        push(own_ref.at[half + k], first_ref.at[half + k], 0, half + k, x_peer)
    small_end(1, running)
    running = small_start(2)
    backs = push_back(p, plane_peers, sums, back_ref, back_send, back_recv)
    for copy in sent:
        copy.wait_send()
    for k in range(planes):
        arrive(first_ref.at[k], 0, k)
        arrive(second_ref.at[k], 1, k)
        plane_ref[k] = (
            dw[0, near[k]].astype(f32) + first_ref[k].astype(f32) + second_ref[k].astype(f32)
        ).astype(bf16)
    small_end(2, running)
    cols = small_ref.shape[1] // 8
    part_ref[...] = small_ref[:, pl.ds(pl.multiple_of(p * cols, cols), cols)]
    for n, peer in enumerate(doubling[3:]):
        copy = remote(part_ref, part_buf.at[n], part_send.at[n], part_recv.at[n], peer)
        copy.start()
        copy.wait()
        part_ref[...] = part_ref[...] + part_buf[n]
    spread = []
    for j in range(1, 8):
        copy = remote(part_ref, parts_ref.at[p], parts_send.at[j], parts_recv.at[j], plane_peers[j])
        copy.start()
        spread.append(copy)
    parts_ref[p] = part_ref[...]
    settle_back(p, plane_peers, backs, back_ref, back_send, back_recv)
    for j in range(1, 8):
        spread[j - 1].wait_send()
        slot = parts_ref.at[p ^ j]
        remote(slot, slot, parts_send.at[j], parts_recv.at[j], plane_peers[1]).wait_recv()
    for q in range(8):
        router_ref[q * cols:(q + 1) * cols] = parts_ref[q, :experts].T
        gains_ref[:, q * cols:(q + 1) * cols] = parts_ref[q, experts:]


def last_kernel(
    plane, back_first, sums, query_ref, keyval_ref, wo_ref, gate_ref, up_ref, down_ref,
    back_ref, far_ref, far_send, far_recv, back_send, back_recv,
):
    d, t = lax.axis_index("dp"), lax.axis_index("tensor")
    planes = plane.shape[0]
    z, x = d // 2, d % 2
    z_peers = [{"dp": lax.rem(z + k, planes) * 2 + x, "tensor": t} for k in range(1, planes)]
    p, plane_peers = own_place(), plane_devices()
    greet((*plane_peers[1:], *z_peers))
    far = []
    for k, peer in enumerate(z_peers):
        copy = remote(plane.at[lax.rem(z + k + 1, planes)], far_ref.at[k], far_send.at[k], far_recv.at[k], peer)
        copy.start()
        far.append(copy)
    backs = push_back(p, plane_peers, sums, back_ref, back_send, back_recv)
    outs = (gate_ref, up_ref, down_ref)
    deep = back_first.shape[3]
    experts = gate_ref.shape[0] // deep

    def assemble(source, first, e, q):
        rows = pl.ds(q * (experts // 8) + first + e, deep, stride=experts)
        for which, out in enumerate(outs):
            out[rows, :] = source[e, q, which].astype(f32)

    for q in range(8):
        for e in range(2):
            assemble(back_first, 0, e, q)
    for e in range(2):
        backs[8 * e + 7].wait()
        assemble(back_ref, 2, e, p)
    for j in (1, 2, 4, 3, 5, 6, 7):
        for e in range(2):
            slot = back_ref.at[e, p ^ j]
            remote(slot, slot, back_send.at[e, j], back_recv.at[e, j], plane_peers[1]).wait_recv()
            assemble(back_ref, 2, e, p ^ j)
    for e in range(2):
        for n in range(7):
            backs[8 * e + n].wait_send()
    mine = plane[z].astype(f32)
    for k, copy in enumerate(far):
        copy.wait()
        mine += far_ref[k].astype(f32)
    qw, kvw = query_ref.shape[1], keyval_ref.shape[2]
    query_ref[...] = mine[:, :qw]
    keyval_ref[:, 0] = mine[:, qw:qw + kvw]
    keyval_ref[:, 1] = mine[:, qw + kvw:qw + 2 * kvw]
    wo_ref[...] = mine[:, qw + 2 * kvw:]


def shards(
    tokens,
    lengths,
    routes,
    gain_attn,
    w_query,
    w_keyvalue,
    w_out,
    gain_mixer,
    w_router,
    w_gate,
    w_up,
    w_down,
    out_grad,
):
    nd, nt = lax.axis_size("dp"), lax.axis_size("tensor")
    dp_id, t_id = lax.axis_index("dp"), lax.axis_index("tensor")
    rows, width = tokens.shape
    group_rows, top_count = routes.shape
    seq_count = lengths.shape[0]
    seq_len = group_rows // seq_count
    experts = w_router.shape[1]
    local = experts // 8
    planes = nd // 2
    deep = width // nd
    hidden = w_gate.shape[2] * nt
    capacity = (rows * top_count * 17 + experts * 16 - 1) // (experts * 16)
    cap = -(-capacity // 16) * 16
    core = t_id % 2
    z_groups = [[x + 2 * z for z in range(planes)] for x in range(2)]
    members = nd // 2
    with_place = [[a * 2 + side for a in range(members)] for side in range(2)]
    plane_groups = [
        [with_place[side][a] * nt + t for side in range(2) for t in range(nt)] for a in range(members)
    ]

    quarter = hidden // nt

    def for_plane(w):
        return jnp.transpose(w.reshape(deep, 8, local, quarter), (1, 2, 0, 3))

    w_send = jnp.stack([for_plane(w_gate), for_plane(w_up), for_plane(w_down)], axis=2)
    q_cols, kv_cols = w_query.shape[1], w_keyvalue.shape[2]
    cut = q_cols + 2 * kv_cols
    w_mine = jnp.concatenate([w_query, w_keyvalue[:, 0], w_keyvalue[:, 1], w_out], axis=1)
    pushes = 3 * planes
    hbm = pl.BlockSpec(memory_space=pl.ANY)
    dealt_shape = sds((8, 3, deep, quarter), bf16)
    dma = pltpu.SemaphoreType.DMA
    line_shape = sds((planes, deep, cut + q_cols), bf16)
    dealt_pair, line = pl.pallas_call(
        deal_kernel,
        out_shape=[sds((2,) + dealt_shape.shape, bf16), line_shape],
        in_specs=[hbm, VM], out_specs=[hbm, VM],
        scratch_shapes=[dma((2, 8)), dma((2, 8)), dma((planes,)), dma((planes,))],
        compiler_params=pltpu.CompilerParams(
            vmem_limit_bytes=VMEM_LIMIT, collective_id=1, has_side_effects=True
        ),
        cost_estimate=pl.CostEstimate(flops=10**6, bytes_accessed=20 * 2**20, transcendentals=0),
    )(w_send, w_mine)
    later = tuple(range(2, local))
    normed_rows, w_attn, ranks, router_t, dealt_third, dealt_last = pl.pallas_call(
        functools.partial(gather_kernel, later),
        out_shape=[
            sds((2 * rows, width), bf16), sds((2, nd, deep, cut + q_cols), bf16), sds((2, nt, 64, rows), bf16),
            sds((64, width), bf16),
        ]
        + [dealt_shape] * 2,
        in_specs=[SM] + [VM] * 5 + [hbm], out_specs=[VM] * 4 + [hbm] * 2,
        scratch_shapes=[
            pltpu.SemaphoreType.DMA((pushes,)), pltpu.SemaphoreType.DMA((2, nd)), pltpu.SemaphoreType.DMA((4,)),
            pltpu.SemaphoreType.DMA((len(later), 8)), pltpu.SemaphoreType.DMA((len(later), 8)),
        ],
        compiler_params=pltpu.CompilerParams(
            vmem_limit_bytes=VMEM_LIMIT, collective_id=0, has_side_effects=True
        ),
        cost_estimate=pl.CostEstimate(flops=10**7, bytes_accessed=100 * 2**20, transcendentals=0),
    )(lengths, tokens, gain_attn[None, :], routes.T, w_router, line, w_send)

    w_pair = gather_weights(dealt_pair, with_place)
    w_third = gather_weights(dealt_third, with_place)
    by_steps = members == local == 4
    w_last = dealt_last if by_steps else gather_weights(dealt_last, with_place)

    exponent = 2.0 * np.arange(HD // 2) / HD
    angles = np.arange(seq_len)[:, None] * np.exp(-math.log(rope_base) * exponent)[None, :]
    cosine, sine = np.cos(angles).astype(np.float32), np.sin(angles).astype(np.float32)
    cos_table = jnp.asarray(np.concatenate([cosine] * 4, axis=1))
    sin_table = jnp.asarray(np.concatenate([-sine, sine] * 2, axis=1))

    out_late = after(out_grad, w_attn)
    out_y, out_x = hop_y(out_late), hop_x(out_late)
    q_width, k_width = 2 * q_cols, 2 * kv_cols
    heads = q_width // HD
    q, k, v, ctx, lse, keep, send = call(
        attend_kernel,
        [
            sds((seq_len, q_width), bf16), sds((seq_len, k_width), bf16), sds((seq_len, k_width), bf16),
            sds((seq_len, q_width), bf16), sds((heads, seq_len), f32),
            sds((rows, width), bf16), sds((rows, width), bf16),
        ],
        12 * 10**9, 16 * 2**20,
        in_specs=[SM] + [VM] * 4, out_specs=[VM] * 7,
    )(lengths, normed_rows, w_attn, cos_table, sin_table)

    def remote_call(kernel, number, out_shape, flops, nbytes, **kw):
        return pl.pallas_call(
            kernel, out_shape=out_shape,
            compiler_params=pltpu.CompilerParams(
                vmem_limit_bytes=VMEM_LIMIT, collective_id=number, has_side_effects=True
            ),
            cost_estimate=pl.CostEstimate(flops=flops, bytes_accessed=nbytes, transcendentals=0),
            **kw,
        )

    slots_shape = (local, 8, cap, width)
    hidden_own, normed_mix, inverse_mix, gates_in, rows_in, grads_in, *moving = remote_call(
        functools.partial(mix_kernel, local, cap, int(by_steps)), 2,
        [
            sds((rows, width), f32), sds((rows, width), bf16), sds((rows, 1), f32),
            sds((local, 8, cap, 1), f32), sds(slots_shape, bf16), sds(slots_shape, bf16),
        ] + [dealt_shape] * (2 * by_steps),
        10**10, 100 * 2**20,
        in_specs=[SM] + [VM] * 9 + [hbm] * by_steps, out_specs=[VM] * 4 + [hbm] * (2 + 2 * by_steps),
        scratch_shapes=[
            pltpu.VMEM((8, rows, width), bf16), pltpu.VMEM((8, rows, width), bf16), pltpu.VMEM((rows, width), bf16),
            pltpu.VMEM((2, local, cap, width), bf16), pltpu.VMEM((64, rows), f32), pltpu.VMEM((64, rows), f32),
            dma((2, 9)), dma((2, 9)), dma((2,)), dma((2,)), dma((4,)),
        ],
    )(
        lengths, tokens, keep, send, gain_mixer[None, :], out_grad, out_y, out_x, ranks, router_t,
        *([dealt_last] if by_steps else []),
    )
    ys, dxs, dw_pairs = [], [], []
    arrived = (w_last, *moving)
    pair_shape = sds((members, 2, 8, 3, deep, quarter), bf16)
    before = []
    for e in range(local):
        step = e + 2 if by_steps and e + 2 < members else 0
        sources = ((w_pair,), (w_pair,), (w_third,), arrived)[e]
        inputs = [after(rows_in, *before), grads_in, gates_in, *sources, *(moving if step else ())]
        aliases = {}
        if e % 2:
            aliases = {len(inputs): 2}
            inputs.append(dw_pairs.pop())
        y, dx, dw, *moved = pl.pallas_call(
            functools.partial(expert_kernel, e, local, len(sources), step, len(sources) > 1),
            out_shape=[
                sds((8, cap, width), bf16), sds((8, cap, width + LANES), bf16), pair_shape,
            ] + [dealt_shape] * (2 if step else 0),
            in_specs=[hbm] * len(inputs),
            out_specs=[hbm] * (5 if step else 3),
            scratch_shapes=[
                pltpu.VMEM((8, cap, width), bf16), pltpu.VMEM((8, cap, width), bf16), pltpu.VMEM((8, cap, 1), f32),
                pltpu.VMEM((members, 8, 3, deep, quarter), bf16),
                pltpu.VMEM((8, cap, width), bf16), pltpu.VMEM((8, cap, width + LANES), bf16),
                pltpu.VMEM((members, 8, 3, deep, quarter), bf16),
                dma((3,)), dma((len(sources),)), dma((5,)), dma((4,)),
            ],
            input_output_aliases=aliases,
            compiler_params=pltpu.CompilerParams(
                vmem_limit_bytes=VMEM_LIMIT, **(dict(collective_id=3 + step, has_side_effects=True) if step else {})
            ),
            cost_estimate=pl.CostEstimate(flops=10**10, bytes_accessed=20 * 2**20, transcendentals=0),
        )(*inputs)
        if step:
            moving = tuple(moved)
            arrived += moving
        ys.append(y)
        dxs.append(dx)
        dw_pairs.append(dw)
        before = [y]

    wide = width + LANES
    grad_hidden, grad_branch, router_grad, gain_mix_grad, y_totals = remote_call(
        functools.partial(return_kernel, local, cap), 3,
        [
            sds((rows, width), f32), sds((2 * rows, width), bf16), sds((experts, width), f32), sds((1, width), f32),
            sds((4, rows, width), bf16),
        ],
        10**10, 100 * 2**20,
        in_specs=[hbm] * (2 * local) + [SM] + [VM] * 7, out_specs=[VM] * 5,
        scratch_shapes=[
            pltpu.VMEM((3, local * cap, wide), bf16),
            pltpu.VMEM((4, rows, wide), bf16), pltpu.VMEM((4, rows, wide), bf16), pltpu.VMEM((4, rows, wide), bf16),
            pltpu.VMEM((2, rows // 2, wide), bf16), pltpu.VMEM((2, rows, wide), bf16),
            pltpu.VMEM((4, rows, width), bf16), pltpu.VMEM((4, rows, width), bf16), pltpu.VMEM((64, rows), f32),
            dma((3, local)), dma((10,)), dma((10,)), dma((4,)), dma((4,)), dma((2,)),
        ],
    )(
        *dxs, *ys, lengths, ranks, normed_mix, hidden_own, inverse_mix, out_grad, w_router, gain_mixer[None, :],
    )
    chip_groups = [
        [with_place[side][a] * nt + y * 2 + c for side in range(2) for y in range(2)]
        for a in range(members) for c in range(2)
    ]
    y_terms = lax.all_to_all(y_totals, BOTH, 0, 0, tiled=True, axis_index_groups=chip_groups)
    mixed = (hidden_own + jnp.sum(y_terms.astype(f32), axis=0)).astype(bf16)

    dw_attn, keep_back, send_back = call(
        attend_back_kernel,
        [
            sds((2, nd, deep, cut + q_cols), bf16), sds((rows, width), bf16), sds((rows, width), bf16),
        ],
        25 * 10**9, 24 * 2**20,
        in_specs=[SM] + [VM] * 10, out_specs=[VM] * 3,
        scratch_shapes=[
            pltpu.VMEM((seq_len, q_width), bf16), pltpu.VMEM((seq_len, 2 * cut), bf16),
            pltpu.VMEM((seq_len, LANES), f32), pltpu.VMEM((seq_len, LANES), f32),
        ],
    )(
        lengths, normed_rows, grad_branch, w_attn, cos_table, sin_table,
        q, k, v, ctx, lse,
    )
    per_dp = (deep, cut + q_cols)
    sums = [
        lax.psum_scatter(dw, "dp", scatter_dimension=0, axis_index_groups=with_place) for dw in dw_pairs
    ]
    back_shape = sds((2, 8, 3, deep, quarter), bf16)
    doublings = (nd - 1).bit_length() - 1
    small_rows, part = experts + 8, width // 8
    grad_tokens, grad_router, gains, plane_grad, back_first = remote_call(
        tail_kernel, 8,
        [
            sds((rows, width), bf16), sds((width, experts), f32), sds((8, width), f32),
            sds((planes,) + per_dp, bf16), back_shape,
        ],
        10**8, 30 * 2**20,
        in_specs=[VM] * 8 + [hbm], out_specs=[VM] * 4 + [hbm],
        scratch_shapes=[pltpu.VMEM((rows, width), bf16)]
        + [pltpu.VMEM((planes,) + per_dp, bf16)] * 4
        + [
            pltpu.VMEM((small_rows, width), f32), pltpu.VMEM((3, small_rows, width), f32),
            pltpu.VMEM((small_rows, part), f32), pltpu.VMEM((doublings, small_rows, part), f32),
            pltpu.VMEM((8, small_rows, part), f32),
            dma((2,)), dma((3, planes)), dma((3, planes)), dma((3,)), dma((3,)), dma((2, 8)), dma((2, 8)),
            dma((doublings,)), dma((doublings,)), dma((8,)), dma((8,)),
        ],
    )(
        after(tokens, y_terms), keep_back, send_back, grad_hidden, gain_attn[None, :], router_grad, gain_mix_grad,
        dw_attn, sums[0],
    )
    expert_grad = sds((deep * experts, quarter), f32)
    grad_query, grad_keyval, grad_out, *expert_grads = remote_call(
        last_kernel, 9,
        [
            sds((deep, q_cols), f32), sds((deep, 2, kv_cols), f32), sds((deep, q_cols), f32),
            expert_grad, expert_grad, expert_grad,
        ],
        10**8, 30 * 2**20,
        in_specs=[VM] * 2 + [hbm], out_specs=[VM] * 6,
        scratch_shapes=[
            pltpu.VMEM((2, 8, 3, deep, quarter), bf16), pltpu.VMEM((planes - 1,) + per_dp, bf16),
            dma((planes - 1,)), dma((planes - 1,)), dma((2, 8)), dma((2, 8)),
        ],
    )(plane_grad, back_first, sums[1])
    grad_gate, grad_up, grad_down = (g.reshape(deep, experts, quarter) for g in expert_grads)

    return (
        mixed,
        grad_tokens,
        gains[1],
        grad_query,
        grad_keyval,
        grad_out,
        gains[0],
        grad_router,
        grad_gate,
        grad_up,
        grad_down,
    )


def solution(mesh):
    placed = (
        P(("dp", "tensor"), None),
        P("dp"),
        P("dp", None),
        P(),
        P("dp", "tensor"),
        P("dp", None, "tensor"),
        P("dp", "tensor"),
        P(),
        P(),
        P("dp", None, "tensor"),
        P("dp", None, "tensor"),
        P("dp", None, "tensor"),
        P(("dp", "tensor"), None),
    )
    return jax.shard_map(
        shards,
        mesh=mesh,
        in_specs=placed,
        out_specs=(
            P(("dp", "tensor"), None),
            P(("dp", "tensor"), None),
            P(),
            P("dp", "tensor"),
            P("dp", None, "tensor"),
            P("dp", "tensor"),
            P(),
            P(),
            P("dp", None, "tensor"),
            P("dp", None, "tensor"),
            P("dp", None, "tensor"),
        ),
        check_vma=False,
    )
```

```python
import functools
import math

import jax
import jax.numpy as jnp
import numpy as np
from jax import lax
from jax.experimental import pallas as pl
from jax.experimental.pallas import tpu as pltpu
from jax.sharding import PartitionSpec as P

HD = 64
LANES = 128
epsilon = 1e-06
rope_base = 10000.0
bf16 = jnp.bfloat16
f32 = jnp.float32
BOTH = ("dp", "tensor")
VMEM_LIMIT = 60 * 1024 * 1024
QBLK = 256


def dot(a, b, ca, cb):
    return lax.dot_general(a, b, (((ca,), (cb,)), ((), ())), preferred_element_type=f32)


def call(kernel, out_shape, flops, nbytes, **kw):
    return pl.pallas_call(
        kernel,
        out_shape=out_shape,
        compiler_params=pltpu.CompilerParams(vmem_limit_bytes=VMEM_LIMIT),
        cost_estimate=pl.CostEstimate(flops=flops, bytes_accessed=nbytes, transcendentals=0),
        **kw,
    )


def sds(shape, dtype):
    return jax.ShapeDtypeStruct(shape, dtype)


VM = pl.BlockSpec(memory_space=pltpu.VMEM)
SM = pl.BlockSpec(memory_space=pltpu.SMEM)


def hop(x, dp_bit, t_bits):
    nd, nt = lax.axis_size("dp"), lax.axis_size("tensor")
    pairs = [
        (d * nt + t, (d ^ dp_bit) * nt + (t ^ t_bits)) for d in range(nd) for t in range(nt)
    ]
    return lax.ppermute(x, BOTH, pairs)


def hop_c(x):
    return hop(x, 0, 1)


def hop_y(x):
    return hop(x, 0, 2)


def hop_x(x):
    return hop(x, 1, 0)


def after(x, *others):
    return lax.optimization_barrier((x, *others))[0]


def gather_weights(x, weight_groups):
    return lax.all_gather(x, "dp", axis_index_groups=weight_groups)


def swap_halves(v):
    lane = lax.broadcasted_iota(jnp.int32, v.shape, 1)
    left = pltpu.roll(v, LANES - HD // 2, 1)
    right = pltpu.roll(v, HD // 2, 1)
    return jnp.where(lane % HD < HD // 2, left, right)


def in_head(tile, h):
    lane = lax.broadcasted_iota(jnp.int32, tile.shape, 1)
    return (lane < HD) if h == 0 else (lane >= HD)


def only_head(tile, h):
    return jnp.where(in_head(tile, h), tile, jnp.zeros_like(tile))


def spread_head(tile, h):
    wide = tile.astype(f32)
    return jnp.where(in_head(wide, h), wide, pltpu.roll(wide, HD, 1)).astype(tile.dtype)


def stacked(tile):
    return jnp.concatenate([only_head(tile, 0), only_head(tile, 1)], axis=0)


def key_limit(start, rows, length):
    column = lax.broadcasted_iota(jnp.int32, (1, 2 * rows), 1)
    position = start + jnp.where(column >= rows, column - rows, column)
    return jnp.minimum(position, length - 1)


def scores_t(kd, qm, limit):
    raw = dot(kd, qm, 1, 1) * (1.0 / math.sqrt(HD))
    key = lax.broadcasted_iota(jnp.int32, raw.shape, 0)
    return jnp.where(key <= limit, raw, -1e30)


def attend_kernel(
    lengths, rows, w, cos, sin,
    q_ref, k_ref, v_ref, ctx_ref, lse_ref, keep_ref, send_ref,
):
    core = lax.axis_index("tensor") % 2
    length = lengths[lax.axis_index("tensor") // 2]
    seq, width = rows.shape
    half = seq // 2
    kw = k_ref.shape[1] // 2
    qw = 2 * kw
    cut = qw + 2 * kw
    for blk in range(seq // QBLK):
        sl = slice(blk * QBLK, (blk + 1) * QBLK)
        c, s = cos[sl], sin[sl]
        for y in range(2):
            pre = dot(rows[sl], w[y, :, :, :cut].reshape(width, cut), 1, 0)
            for tile in range((qw + kw) // LANES):
                col = pre[:, tile * LANES:(tile + 1) * LANES]
                turned = (col * c + swap_halves(col) * s).astype(bf16)
                if tile * LANES < qw:
                    q_ref[sl, y * qw + tile * LANES:y * qw + (tile + 1) * LANES] = turned
                else:
                    at = y * kw + tile * LANES - qw
                    k_ref[sl, at:at + LANES] = turned
            v_ref[sl, y * kw:(y + 1) * kw] = pre[:, qw + kw:].astype(bf16)
    for g in range(2 * qw // LANES):
        kv = slice(g // 2 * LANES, (g // 2 + 1) * LANES)
        cols = slice(g * LANES, (g + 1) * LANES)
        kd = spread_head(k_ref[:, kv], g % 2)
        vd_t = spread_head(v_ref[:, kv], g % 2).T
        for blk in range(seq // QBLK):
            top = (blk + 1) * QBLK
            sl = slice(blk * QBLK, top)
            s = scores_t(kd[:top], stacked(q_ref[sl, cols]), key_limit(blk * QBLK, QBLK, length))
            peak = jnp.max(s, axis=0, keepdims=True)
            e = jnp.exp(s - peak)
            total = jnp.sum(e, axis=0, keepdims=True)
            p = (e * (1.0 / total)).astype(bf16)
            ctx = dot(vd_t[:, :top], p, 1, 0).T
            tile = jnp.where(in_head(ctx[:QBLK], 0), ctx[:QBLK], ctx[QBLK:])
            ctx_ref[sl, cols] = tile.astype(bf16)
            lse = peak + jnp.log(total)
            lse_ref[2 * g:2 * g + 1, sl] = lse[:, :QBLK]
            lse_ref[2 * g + 1:2 * g + 2, sl] = lse[:, QBLK:]
    for out_ref, side in ((send_ref, 1 - core), (keep_ref, core)):
        at = pl.ds(pl.multiple_of(side * half, half), half)
        out = dot(ctx_ref[at, :qw], w[0, :, :, cut:].reshape(width, qw), 1, 1)
        out += dot(ctx_ref[at, qw:], w[1, :, :, cut:].reshape(width, qw), 1, 1)
        out_ref[...] = out.astype(bf16)


def attend_back_kernel(
    lengths, rows, gb_ref, w, cos, sin, q_ref, k_ref, v_ref, ctx_ref, lse_ref,
    dw_ref, keep_ref, send_ref,
    gc_ref, dqkv_ref, dk_ref, dv_ref,
):
    core = lax.axis_index("tensor") % 2
    length = lengths[lax.axis_index("tensor") // 2]
    seq, width = rows.shape
    half = seq // 2
    kw = k_ref.shape[1] // 2
    qw = 2 * kw
    cut = qw + 2 * kw
    per_dp = dw_ref.shape[1:3]
    at_own = pl.ds(pl.multiple_of(core * half, half), half)
    at_peer = pl.ds(pl.multiple_of((1 - core) * half, half), half)
    for y in range(2):
        part = slice(y * qw, (y + 1) * qw)
        gc_ref[:, part] = dot(gb_ref[...], w[y, :, :, cut:].reshape(width, qw), 1, 0).astype(bf16)
        dw_ref[y, :, :, cut:] = dot(gb_ref[...], ctx_ref[:, part], 0, 0).astype(bf16).reshape(per_dp + (qw,))
    scale = 1.0 / math.sqrt(HD)
    folded = None
    for g in range(2 * qw // LANES):
        y = g // 2
        kv = slice(y * LANES, (y + 1) * LANES)
        cols = slice(g * LANES, (g + 1) * LANES)
        kd = spread_head(k_ref[:, kv], g % 2)
        kd_t = kd.T
        vd = spread_head(v_ref[:, kv], g % 2)
        for blk in reversed(range(seq // QBLK)):
            top = (blk + 1) * QBLK
            sl = slice(blk * QBLK, top)
            qm = stacked(q_ref[sl, cols])
            gm = stacked(gc_ref[sl, cols])
            s = scores_t(kd[:top], qm, key_limit(blk * QBLK, QBLK, length))
            lse = jnp.concatenate([lse_ref[2 * g:2 * g + 1, sl], lse_ref[2 * g + 1:2 * g + 2, sl]], axis=1)
            p = jnp.exp(s - lse)
            gw = dot(vd[:top], gm, 1, 1)
            centre = jnp.sum(p * gw, axis=0, keepdims=True)
            ds = (p * (gw - centre) * scale).astype(bf16)
            dv = dot(p.astype(bf16), gm, 1, 0)
            dk = dot(ds, qm, 1, 0)
            dq = dot(kd_t[:, :top], ds, 1, 0).T
            if top == seq:
                dk_ref[...] = dk
                dv_ref[...] = dv
            else:
                dk_ref[:top] += dk
                dv_ref[:top] += dv
            tile = jnp.where(in_head(dq[:QBLK], 0), dq[:QBLK], dq[QBLK:])
            back = tile * cos[sl] - swap_halves(tile) * sin[sl]
            at = y * cut + g % 2 * LANES
            dqkv_ref[sl, at:at + LANES] = back.astype(bf16)
        dk_all = dk_ref[...] + pltpu.roll(dk_ref[...], HD, 1)
        dv_all = dv_ref[...] + pltpu.roll(dv_ref[...], HD, 1)
        if g % 2 == 0:
            folded = (dk_all, dv_all)
        else:
            dk_pair = jnp.where(in_head(dk_all, 0), folded[0], dk_all)
            dv_pair = jnp.where(in_head(dv_all, 0), folded[1], dv_all)
            at = y * cut + qw
            back = dk_pair * cos[...] - swap_halves(dk_pair) * sin[...]
            dqkv_ref[:, at:at + LANES] = back.astype(bf16)
            dqkv_ref[:, at + LANES:at + 2 * LANES] = dv_pair.astype(bf16)
            part = slice(y * cut, (y + 1) * cut)
            dw_ref[y, :, :, :cut] = dot(rows[...], dqkv_ref[:, part], 0, 0).astype(bf16).reshape(per_dp + (cut,))
    for out_ref, at in ((send_ref, at_peer), (keep_ref, at_own)):
        out = dot(dqkv_ref[at, :cut], w[0, :, :, :cut].reshape(width, cut), 1, 1)
        out += dot(dqkv_ref[at, cut:], w[1, :, :, :cut].reshape(width, cut), 1, 1)
        out_ref[...] = out.astype(bf16)


def own_place():
    return lax.axis_index("dp") % 2 * 4 + lax.axis_index("tensor")


def plane_devices():
    d, p = lax.axis_index("dp"), own_place()
    return [{"dp": d + ((p ^ j) // 4 - p // 4), "tensor": (p ^ j) % 4} for j in range(8)]


def deal_out(p, plane_peers, w_send, numbers, dealt, send_sem, recv_sem):
    copies = []
    for i, e in enumerate(numbers):
        for j in (6, 7, 2, 4, 3, 5, 1):
            copies.append(
                pltpu.make_async_remote_copy(
                    src_ref=w_send.at[p ^ j, e], dst_ref=dealt[i].at[j], send_sem=send_sem.at[i, j],
                    recv_sem=recv_sem.at[i, j], device_id=plane_peers[j], device_id_type=pl.DeviceIdType.MESH,
                )
            )
        copies.append(pltpu.make_async_copy(w_send.at[p, e], dealt[i].at[0], send_sem.at[i, 0]))
    for copy in copies:
        copy.start()
    return copies


def deal_kernel(w_send, w_mine, *refs):
    pair, line_ref, send_sem, recv_sem, line_send, line_recv = refs
    d, t = lax.axis_index("dp"), lax.axis_index("tensor")
    planes = line_ref.shape[0]
    z, x = d // 2, d % 2
    p = own_place()
    peers = plane_devices()
    z_peers = [{"dp": lax.rem(z + k, planes) * 2 + x, "tensor": t} for k in range(1, planes)]
    greet((*peers[1:], *z_peers))
    lines = []
    for k, peer in enumerate(z_peers):
        copy = remote(w_mine, line_ref.at[z], line_send.at[k], line_recv.at[z], peer)
        copy.start()
        lines.append(copy)
    copies = deal_out(p, peers, w_send, (0, 1), (pair.at[0], pair.at[1]), send_sem, recv_sem)
    line_ref[z] = w_mine[...]
    for copy in copies:
        copy.wait()
    for k in range(1, planes):
        lines[k - 1].wait_send()
        at = lax.rem(z + k, planes)
        remote(line_ref.at[at], line_ref.at[at], line_send.at[0], line_recv.at[at], peers[1]).wait_recv()


def group_rows_of(experts):
    local = experts // 8
    row = lax.broadcasted_iota(jnp.int32, (64, experts), 0)
    expert = lax.broadcasted_iota(jnp.int32, (64, experts), 1)
    return ((row % 8 < local) & (row // 8 * local + row % 8 == expert)).astype(f32).astype(bf16)


def rank_rows(lengths, routes_t, block, ranks_ref):
    blocks, wide = ranks_ref.shape[1:3]
    seq_len = block * blocks // lengths.shape[0]
    local = wide // 16
    row = lax.broadcasted_iota(jnp.int32, (wide, block), 0)
    number = jnp.where(row % 8 < local, row // 8 * local + row % 8, -1)
    low = lax.broadcasted_iota(jnp.int32, (block, block), 0)
    high = lax.broadcasted_iota(jnp.int32, (block, block), 1)
    before = (low < high).astype(f32).astype(bf16)
    for b in range(blocks):
        at = slice(b * block, (b + 1) * block)
        position = lax.broadcasted_iota(jnp.int32, (wide, block), 1) + b * block % seq_len
        hit = jnp.zeros((wide, block), jnp.bool_)
        for k in range(routes_t.shape[0]):
            hit = hit | (routes_t[k:k + 1, at] == number)
        hit = hit & (position < lengths[b * block // seq_len])
        earlier = dot(hit.astype(f32).astype(bf16), before, 1, 0)
        ranks_ref[0, b] = jnp.where(hit, earlier, -1.0).astype(bf16)


def gather_kernel(
    later, lengths, tokens, gain, routes_t, router, line, w_send, rows_ref, w_ref, ranks_ref, router_ref, *refs
):
    dealt, (send_sem, recv_sem, row_sem, deal_send, deal_recv) = refs[:-5], refs[-5:]
    planes = line.shape[0]
    half = tokens.shape[0]
    x, core = lax.axis_index("dp") % 2, lax.axis_index("tensor") % 2
    p, plane_peers = own_place(), plane_devices()
    x_peer, y_peer, core_peer = neighbours()
    greet(plane_peers[1:])
    copies = []

    def push(source, side, dp, peer):
        copy = remote(source, w_ref.at[side, dp], send_sem.at[len(copies)], recv_sem.at[side, dp], peer)
        copy.start()
        copies.append(copy)

    def arrive(side, dp):
        slot = w_ref.at[side, dp]
        remote(slot, slot, send_sem.at[0], recv_sem.at[side, dp], x_peer).wait_recv()

    near = [k * 2 + x for k in range(planes)]
    over = [k * 2 + 1 - x for k in range(planes)]
    for k in range(planes):
        push(line.at[k], 0, near[k], x_peer)
        push(line.at[k], 1, near[k], y_peer)
    deals = deal_out(p, plane_peers, w_send, later, dealt, deal_send, deal_recv)
    values = tokens[...].astype(f32)
    inverse = lax.rsqrt(jnp.mean(values * values, axis=1, keepdims=True) + epsilon)
    at = pl.ds(pl.multiple_of(core * half, half), half)
    rows_ref[at] = (values * inverse * gain[...]).astype(bf16)
    row_copy = remote(rows_ref.at[at], rows_ref.at[at], row_sem.at[0], row_sem.at[1], core_peer)
    row_copy.start()
    rank_rows(lengths, routes_t, half, ranks_ref)
    rank_copy = remote(ranks_ref.at[0], ranks_ref.at[1], row_sem.at[2], row_sem.at[3], x_peer)
    rank_copy.start()
    router_ref[...] = dot(group_rows_of(router.shape[1]), router[...], 1, 1).astype(bf16)
    for k in range(planes):
        w_ref[0, near[k]] = line[k]
    for k in range(planes):
        arrive(0, over[k])
        if k < planes // 2:
            push(w_ref.at[0, over[k]], 1, over[k], y_peer)
        arrive(1, near[k])
        if k >= planes // 2:
            push(w_ref.at[1, near[k]], 1, near[k], x_peer)
    for k in range(planes):
        arrive(1, over[k])
    for copy in copies:
        copy.wait_send()
    row_copy.wait()
    rank_copy.wait()
    for copy in deals:
        copy.wait()


def masked_shares(logits, hit, axis):
    peak = jnp.max(jnp.where(hit, logits, -1e30), axis=axis, keepdims=True)
    e = jnp.where(hit, jnp.exp(jnp.where(hit, logits - peak, 0.0)), 0.0)
    total = jnp.sum(e, axis=axis, keepdims=True)
    return e / jnp.where(total > 0.0, total, 1.0)


def split16(v):
    high = v.astype(bf16)
    return high, (v - high.astype(f32)).astype(bf16)


def neighbours():
    peers = plane_devices()
    return peers[4], peers[2], peers[1]


def greet(peers):
    barrier = pltpu.get_barrier_semaphore()
    for peer in peers:
        pl.semaphore_signal(barrier, inc=1, device_id=peer, device_id_type=pl.DeviceIdType.MESH)
    pl.semaphore_wait(barrier, len(peers))


def remote(source, target, send_sem, recv_sem, peer):
    return pltpu.make_async_remote_copy(
        src_ref=source, dst_ref=target, send_sem=send_sem, recv_sem=recv_sem,
        device_id=peer, device_id_type=pl.DeviceIdType.MESH,
    )


def live_rows(lengths, rows):
    first = lax.axis_index("tensor") * rows
    seq_len = 4 * rows // lengths.shape[0]
    position = lax.rem(first, seq_len) + lax.broadcasted_iota(jnp.int32, (rows, 1), 0)
    return (position < lengths[first // seq_len]).astype(f32)


def z_steps(step, up_from, down_from, up_to, down_to, sem):
    d, t = lax.axis_index("dp"), lax.axis_index("tensor")
    planes = lax.axis_size("dp") // 2
    z = d // 2
    above = {"dp": lax.rem(z + 1, planes) * 2 + d % 2, "tensor": t}
    below = {"dp": lax.rem(z + planes - 1, planes) * 2 + d % 2, "tensor": t}
    up = remote(up_from, up_to, sem.at[0], sem.at[1], above)
    down = remote(down_from, down_to, sem.at[2], sem.at[3], below)
    steps = (
        (up, (z >= step - 1) & (z < planes - 1), z >= step),
        (down, (z > 0) & (z <= planes - step), z < planes - step),
    )
    return steps, above, below


def start_steps(steps):
    for copy, sends, _ in steps:
        pl.when(sends)(copy.start)


def settle_steps(steps):
    for copy, sends, receives in steps:
        pl.when(sends)(copy.wait_send)
        pl.when(receives)(copy.wait_recv)


def block_ranks(ranks, j):
    return ranks[j // 4, lax.axis_index("tensor") ^ (j % 4)].astype(f32)


def own_group():
    return pl.multiple_of(own_place() * 8, 8)


def placing(ranks, cap):
    slot = lax.broadcasted_iota(jnp.int32, (cap, ranks.shape[1]), 0).astype(f32)
    return [(slot == ranks[e:e + 1]).astype(f32) for e in range(ranks.shape[0])]


def mix_kernel(
    local, cap, carry, lengths, tokens, keep, send, gain, out_own, out_y, out_x, ranks, router_t, *refs
):
    if carry:
        moving, refs = refs[0], refs[1:]
        (up_to, down_to), refs = refs[6:8], refs[:6] + refs[8:]
    (
        hidden_ref, normed_ref, inv_ref, gates_ref, x_hbm, g_hbm,
        normed_buf, out_buf, got_ref, stage_ref, ranks_ref, shares_ref,
        send_sem, recv_sem, core_sem, stage_sem, z_sem,
    ) = refs
    x_peer, y_peer, core_peer = neighbours()
    if carry:
        steps, above, below = z_steps(carry, moving, moving, up_to, down_to, z_sem)
        greet((x_peer, y_peer, core_peer, above, below))
    else:
        greet((x_peer, y_peer, core_peer))
    rows = tokens.shape[0]
    low, high = pl.ds(0, rows // 2), pl.ds(rows // 2, rows // 2)
    sent = []

    def push(kind, source, target, slot, peer):
        copy = remote(source, target, send_sem.at[kind, slot], recv_sem.at[kind, slot], peer)
        copy.start()
        sent.append(copy)

    def arrive(kind, target, slot):
        remote(target, target, send_sem.at[kind, slot], recv_sem.at[kind, slot], x_peer).wait_recv()

    core_copy = remote(send, got_ref, core_sem.at[0], core_sem.at[1], core_peer)
    core_copy.start()
    if carry:
        start_steps(steps)
    push(1, out_y.at[low], out_buf.at[6, low], 6, x_peer)
    push(1, out_x.at[high], out_buf.at[6, high], 8, y_peer)
    push(1, out_own, out_buf.at[1], 1, core_peer)
    push(1, out_y, out_buf.at[3], 3, core_peer)
    push(1, out_x, out_buf.at[5], 5, core_peer)
    core_copy.wait()
    branch = keep[...].astype(f32) + got_ref[...].astype(f32)
    hidden = tokens[...].astype(f32) + live_rows(lengths, rows) * branch
    inverse = lax.rsqrt(jnp.mean(hidden * hidden, axis=1, keepdims=True) + epsilon)
    hidden_ref[...] = hidden
    inv_ref[...] = inverse
    normed = (hidden * inverse * gain[...]).astype(bf16)
    normed_ref[...] = normed
    normed_buf[0] = normed
    own = normed_buf.at[0]
    push(0, own, normed_buf.at[2], 2, y_peer)
    push(0, own, normed_buf.at[4], 4, x_peer)
    push(0, own, normed_buf.at[1], 1, core_peer)

    staged = []

    def place(kind, j, source):
        n = len(staged)
        if n >= 2:
            staged[n - 2].wait()
        group = own_group()
        ranks_ref[...] = block_ranks(ranks, j)
        places = placing(ranks_ref[pl.ds(group, 8)][:local], cap)
        if kind == 0:
            logits = dot(router_t[...], source[...], 1, 1)
            shares_ref[...] = masked_shares(logits, ranks_ref[...] >= 0.0, 0)
            shares = shares_ref[pl.ds(group, 8)]
            for e in range(local):
                gates_ref[e, j] = jnp.sum(places[e] * shares[e:e + 1], axis=1, keepdims=True)
        matrix = jnp.concatenate([m.astype(bf16) for m in places], axis=0)
        placed = dot(matrix, source[...], 1, 0).astype(bf16)
        stage_ref[n % 2] = placed.reshape(local, cap, -1)
        copy = pltpu.make_async_copy(
            stage_ref.at[n % 2], (x_hbm if kind == 0 else g_hbm).at[:, j], stage_sem.at[n % 2]
        )
        copy.start()
        staged.append(copy)

    place(1, 0, out_own)
    place(1, 2, out_y)
    place(1, 4, out_x)
    place(0, 0, own)
    for j in (1, 3, 5):
        arrive(1, out_buf.at[j], j)
        place(1, j, out_buf.at[j])
    arrive(1, out_buf.at[6, low], 6)
    arrive(1, out_buf.at[6, high], 8)
    push(1, out_buf.at[6], out_buf.at[7], 7, core_peer)
    arrive(0, normed_buf.at[1], 1)
    place(0, 1, normed_buf.at[1])
    place(1, 6, out_buf.at[6])
    arrive(0, normed_buf.at[2], 2)
    push(0, normed_buf.at[2, low], normed_buf.at[6, low], 6, x_peer)
    push(0, normed_buf.at[2], normed_buf.at[3], 3, core_peer)
    arrive(0, normed_buf.at[4], 4)
    push(0, normed_buf.at[4, high], normed_buf.at[6, high], 8, y_peer)
    push(0, normed_buf.at[4], normed_buf.at[5], 5, core_peer)
    arrive(1, out_buf.at[7], 7)
    place(1, 7, out_buf.at[7])
    place(0, 2, normed_buf.at[2])
    place(0, 4, normed_buf.at[4])
    for j in (3, 5):
        arrive(0, normed_buf.at[j], j)
        place(0, j, normed_buf.at[j])
    arrive(0, normed_buf.at[6, low], 6)
    arrive(0, normed_buf.at[6, high], 8)
    push(0, normed_buf.at[6], normed_buf.at[7], 7, core_peer)
    place(0, 6, normed_buf.at[6])
    arrive(0, normed_buf.at[7], 7)
    place(0, 7, normed_buf.at[7])
    for copy in sent:
        copy.wait_send()
    for copy in staged[-2:]:
        copy.wait()
    if carry:
        settle_steps(steps)


def return_kernel(local, cap, *refs):
    dxs, ys, refs = refs[:local], refs[local:2 * local], refs[2 * local:]
    (
        lengths, ranks, normed, hidden_in, inv, out_grad, router, gain,
        grad_hidden_ref, branch_ref, router_grad_ref, gain_grad_ref, y_ref,
        load_ref, part_ref, core_ref, total_ref, diag_ref, last_ref, y_part, y_core, ranks_ref,
        load_sem, send_sem, recv_sem, y_send, y_recv, branch_sem,
    ) = refs
    x_peer, y_peer, core_peer = neighbours()
    core = lax.axis_index("tensor") % 2
    greet((x_peer, y_peer, core_peer))
    rows, width = normed.shape
    wide = part_ref.shape[-1]
    half = rows // 2
    low, high = pl.ds(0, half), pl.ds(half, half)
    order = [(0, j) for j in (7, 6, 5, 4, 3, 2, 1, 0)] + [(1, j) for j in (7, 5, 3, 1, 6, 4, 2, 0)]
    depth = load_ref.shape[0]
    sent = []

    def loads(n):
        kind, j = order[n]
        slot = n % depth
        cols = wide if kind == 0 else width
        return [
            pltpu.make_async_copy(
                (ys if kind else dxs)[e].at[j],
                load_ref.at[slot, pl.ds(e * cap, cap), pl.ds(0, cols)], load_sem.at[slot, e],
            )
            for e in range(local)
        ]

    def start(n):
        if n < len(order):
            for copy in loads(n):
                copy.start()

    for n in range(depth - 1):
        start(n)
    done = [0]

    def combined():
        n = done[0]
        done[0] += 1
        start(n + depth - 1)
        for copy in loads(n):
            copy.wait()
        kind, j = order[n]
        ranks_ref[...] = block_ranks(ranks, j)
        places = placing(ranks_ref[pl.ds(own_group(), 8)][:local], cap)
        matrix = jnp.concatenate([m.astype(bf16) for m in places], axis=0)
        values = load_ref[n % depth] if kind == 0 else load_ref[n % depth, :, :width]
        return dot(matrix, values, 0, 0)

    def push(source, target, n, peer):
        copy = remote(source, target, send_sem.at[n], recv_sem.at[n], peer)
        copy.start()
        sent.append(copy)

    def arrive(target, n):
        remote(target, target, send_sem.at[n], recv_sem.at[n], x_peer).wait_recv()

    def far_core(k):
        part_ref[k] = combined().astype(bf16)
        push(part_ref.at[k], core_ref.at[k], k, core_peer)

    def near_core(k):
        mine = combined()
        arrive(core_ref.at[k], k)
        return mine + core_ref[k].astype(f32)

    far_core(3)
    total_ref[2] = near_core(3).astype(bf16)
    push(total_ref.at[2, low], diag_ref.at[0], 4, x_peer)
    push(total_ref.at[2, high], diag_ref.at[1], 5, y_peer)
    far_core(2)
    total_ref[1] = near_core(2).astype(bf16)
    push(total_ref.at[1, low], last_ref.at[0, low], 6, x_peer)
    far_core(1)
    total_ref[0] = near_core(1).astype(bf16)
    push(total_ref.at[0, high], last_ref.at[1, high], 7, y_peer)
    far_core(0)
    part_own = near_core(0).astype(bf16)
    y_copies = []
    total_ref[3] = part_own

    def y_far(k):
        y_part[k] = combined().astype(bf16)
        copy = remote(y_part.at[k], y_core.at[k], y_send.at[k], y_recv.at[k], core_peer)
        copy.start()
        y_copies.append(copy)

    y_far(3)
    y_far(2)
    arrive(diag_ref.at[1], 5)
    total_ref[1, high] = (total_ref[1, high].astype(f32) + diag_ref[1].astype(f32)).astype(bf16)
    push(total_ref.at[1, high], last_ref.at[0, high], 8, x_peer)
    arrive(diag_ref.at[0], 4)
    total_ref[0, low] = (total_ref[0, low].astype(f32) + diag_ref[0].astype(f32)).astype(bf16)
    push(total_ref.at[0, low], last_ref.at[1, low], 9, y_peer)
    y_far(1)
    y_far(0)
    for k in (3, 2, 1, 0):
        mine = combined()
        y_copies[3 - k].wait()
        y_ref[k ^ (own_place() // 2)] = (mine + y_core[k].astype(f32)).astype(bf16)

    experts = router.shape[1]
    hit_rows = (block_ranks(ranks, 0) >= 0.0).astype(f32).astype(bf16)
    hit = dot(hit_rows, group_rows_of(experts), 0, 0) > 0.0
    shares = masked_shares(dot(normed[...], router[...], 1, 0), hit, 1)
    arrive(last_ref.at[0, low], 6)
    arrive(last_ref.at[1, high], 7)
    arrive(last_ref.at[0, high], 8)
    arrive(last_ref.at[1, low], 9)
    for copy in sent:
        copy.wait_send()

    def summed(lo, hi):
        cols = pl.ds(lo, hi - lo)
        return (
            total_ref[3, :, cols].astype(f32) + last_ref[0, :, cols].astype(f32) + last_ref[1, :, cols].astype(f32)
        )

    grad_shares = jnp.where(hit, summed(width, wide)[:, :experts], 0.0)
    grad_chosen = shares * (grad_shares - jnp.sum(shares * grad_shares, axis=1, keepdims=True))
    top, rest = split16(grad_chosen)
    hidden, inverse = hidden_in[...], inv[...]
    grad_mix = summed(0, width) + dot(top, router[...], 1, 1) + dot(rest, router[...], 1, 1)
    weighted = grad_mix * gain[...]
    centre = jnp.mean(hidden * weighted, axis=1, keepdims=True)
    grad_hidden = out_grad[...].astype(f32) + inverse * weighted - hidden * (inverse * inverse * inverse * centre)
    grad_hidden_ref[...] = grad_hidden
    at = pl.ds(pl.multiple_of(core * rows, rows), rows)
    branch_ref[at] = (live_rows(lengths, rows) * grad_hidden).astype(bf16)
    branch_copy = remote(branch_ref.at[at], branch_ref.at[at], branch_sem.at[0], branch_sem.at[1], core_peer)
    branch_copy.start()
    gain_grad_ref[...] = jnp.sum(grad_mix * hidden * inverse, axis=0, keepdims=True)
    router_grad_ref[...] = dot(top, normed[...], 0, 0) + dot(rest, normed[...], 0, 0)
    branch_copy.wait()


def expert_kernel(expert, local, steps, carry, chained, x_hbm, g_hbm, gates_hbm, *refs):
    sources, refs = refs[:steps], refs[steps:]
    if carry:
        (up_from, down_from), refs = refs[:2], refs[2:]
    if expert % 2:
        refs = refs[1:]
    if carry:
        (up_to, down_to), refs = refs[3:5], refs[:3] + refs[5:]
    y_hbm, dx_hbm, dw_hbm, x_ref, g_ref, gates_ref, w_buf, y_ref, dx_ref, dw_ref, in_sem, w_sem, out_sem, z_sem = refs
    d, t, p = lax.axis_index("dp"), lax.axis_index("tensor"), own_place()
    members, _, _, deep, quarter = w_buf.shape
    blocks = [(dp // 2, dp % 2 * 4) for dp in range(2 * members)]
    z = d // 2
    if carry:
        steps_out, above, below = z_steps(carry, up_from, down_from, up_to, down_to, z_sem)
        greet((above, below))
        start_steps(steps_out)

    def fetch(act):
        if not chained:
            source = sources[0].at[:, expert] if expert < 2 else sources[0]
            act(pltpu.make_async_copy(source, w_buf, w_sem.at[0]))
            return
        act(pltpu.make_async_copy(sources[0], w_buf.at[z], w_sem.at[0]))
        for n, source in enumerate(sources[1:]):
            origin = z - (n // 2 + 1) if n % 2 == 0 else z + n // 2 + 1

            @pl.when((origin >= 0) & (origin < members))
            def _():
                act(pltpu.make_async_copy(source, w_buf.at[origin], w_sem.at[n + 1]))

    x_copy = pltpu.make_async_copy(x_hbm.at[expert], x_ref, in_sem.at[0])
    g_copy = pltpu.make_async_copy(g_hbm.at[expert], g_ref, in_sem.at[1])
    gates_copy = pltpu.make_async_copy(gates_hbm.at[expert], gates_ref, in_sem.at[2])
    x_copy.start()
    fetch(lambda copy: copy.start())
    g_copy.start()
    gates_copy.start()
    slots, width = x_ref.shape[0] * x_ref.shape[1], x_ref.shape[2]

    def weight(which):
        rows = [
            jnp.concatenate([w_buf[at, (side + q) ^ p, which] for q in range(4)], axis=1) for at, side in blocks
        ]
        return jnp.concatenate(rows, axis=0)

    outs = []

    def send(source, target):
        copy = pltpu.make_async_copy(source, target, out_sem.at[len(outs)])
        copy.start()
        outs.append(copy)

    x_copy.wait()
    fetch(lambda copy: copy.wait())
    x = x_ref[...].reshape(slots, width)
    w_gate, w_up, w_down = weight(0), weight(1), weight(2)
    gate_lin = dot(x, w_gate, 1, 0)
    up_lin = dot(x, w_up, 1, 0)
    g_copy.wait()
    gates_copy.wait()
    g = g_ref[...].reshape(slots, width)
    gates = gates_ref[...].reshape(slots, 1)
    grad_scaled = dot(g, w_down, 1, 0)
    sigmoid = 1.0 / (1.0 + jnp.exp(-gate_lin))
    silu = gate_lin * sigmoid
    product = silu * up_lin
    grad_gates = jnp.sum(grad_scaled * product, axis=1, keepdims=True)
    scaled_hidden = (gates * product).astype(bf16)
    grad_act = gates * grad_scaled
    grad_gate_lin = (grad_act * up_lin * sigmoid * (1.0 + gate_lin * (1.0 - sigmoid))).astype(bf16)
    grad_up_lin = (grad_act * silu).astype(bf16)
    y_ref[...] = dot(scaled_hidden, w_down, 1, 1).astype(bf16).reshape(y_ref.shape)
    send(y_ref, y_hbm)
    dx = dot(grad_gate_lin, w_gate, 1, 1) + dot(grad_up_lin, w_up, 1, 1)
    dx_ref[:, :, :width] = dx.astype(bf16).reshape(y_ref.shape)
    lane = lax.broadcasted_iota(jnp.int32, (slots, LANES), 1)
    tail = jnp.where(lane == p * local + expert, grad_gates, 0.0).astype(bf16)
    dx_ref[:, :, width:] = tail.reshape(dx_ref.shape[:2] + (LANES,))
    send(dx_ref, dx_hbm)
    for which, (left, right) in enumerate(((x, grad_gate_lin), (x, grad_up_lin), (g, scaled_hidden))):
        grad = dot(left, right, 0, 0).astype(bf16)
        for dp, (at, side) in enumerate(blocks):
            for q in range(4):
                dw_ref[at, side + q, which] = grad[dp * deep:(dp + 1) * deep, q * quarter:(q + 1) * quarter]
        send(dw_ref.at[:, :, which], dw_hbm.at[:, expert % 2, :, which])
    for copy in outs:
        copy.wait()
    if carry:
        settle_steps(steps_out)


def all_peers(d, t, planes):
    peers = [{"dp": d, "tensor": t ^ 1}, {"dp": d, "tensor": t ^ 2}]
    bit = 1
    while bit < 2 * planes:
        peers.append({"dp": d ^ bit, "tensor": t})
        bit *= 2
    return peers


def push_back(p, plane_peers, sums, back_ref, send_sem, recv_sem):
    copies = []
    for e in range(2):
        for j in (6, 7, 2, 4, 3, 5, 1):
            copies.append(
                remote(sums.at[e, p ^ j], back_ref.at[e, p], send_sem.at[e, j], recv_sem.at[e, j], plane_peers[j])
            )
        copies.append(pltpu.make_async_copy(sums.at[e, p], back_ref.at[e, p], send_sem.at[e, 0]))
    for copy in copies:
        copy.start()
    return copies


def settle_back(p, plane_peers, copies, back_ref, send_sem, recv_sem):
    for e in range(2):
        for n, j in enumerate((6, 7, 2, 4, 3, 5, 1)):
            copies[8 * e + n].wait_send()
            slot = back_ref.at[e, p ^ j]
            remote(slot, slot, send_sem.at[e, j], recv_sem.at[e, j], plane_peers[1]).wait_recv()
        copies[8 * e + 7].wait()


def tail_kernel(
    tokens, keep, send, grad_hidden, gain, router_grad, gain_mix_grad, dw, sums,
    out_ref, router_ref, gains_ref, plane_ref, back_ref,
    got_ref, first_ref, second_ref, diag_ref, own_ref, small_ref, small_buf, part_ref, part_buf, parts_ref,
    core_sem, send_sem, recv_sem, small_send, small_recv, back_send, back_recv,
    part_send, part_recv, parts_send, parts_recv,
):
    d, t = lax.axis_index("dp"), lax.axis_index("tensor")
    planes = dw.shape[1] // 2
    half = planes // 2
    x = d % 2
    doubling = all_peers(d, t, planes)
    core_peer, y_peer, x_peer = doubling[:3]
    p, plane_peers = own_place(), plane_devices()
    greet((*plane_peers[1:], *doubling[3:]))
    experts = router_grad.shape[0]
    sent = []

    def push(source, target, kind, k, peer):
        copy = remote(source, target, send_sem.at[kind, k], recv_sem.at[kind, k], peer)
        copy.start()
        sent.append(copy)

    def arrive(target, kind, k):
        remote(target, target, send_sem.at[kind, k], recv_sem.at[kind, k], x_peer).wait_recv()

    core_copy = remote(send, got_ref, core_sem.at[0], core_sem.at[1], core_peer)
    core_copy.start()
    near = [k * 2 + x for k in range(planes)]
    over = [k * 2 + 1 - x for k in range(planes)]
    for k in range(half):
        push(dw.at[1, over[k]], diag_ref.at[k], 2, k, x_peer)
        push(dw.at[1, over[half + k]], diag_ref.at[half + k], 2, half + k, y_peer)
    for k in range(half):
        push(dw.at[0, over[k]], first_ref.at[k], 0, k, x_peer)
        push(dw.at[1, near[half + k]], second_ref.at[half + k], 1, half + k, y_peer)
    core_copy.wait()
    source = tokens[...].astype(f32)
    inverse = lax.rsqrt(jnp.mean(source * source, axis=1, keepdims=True) + epsilon)
    grad = keep[...].astype(f32) + got_ref[...].astype(f32)
    gain_grad = jnp.sum(grad * source * inverse, axis=0, keepdims=True)
    small_ref[:experts] = router_grad[...]
    row = lax.broadcasted_iota(jnp.int32, (8, small_ref.shape[1]), 0)
    small_ref[experts:] = jnp.where(row == 0, gain_mix_grad[...], jnp.where(row == 1, gain_grad, 0.0))

    def small_start(n):
        copy = remote(small_ref, small_buf.at[n], small_send.at[n], small_recv.at[n], doubling[n])
        copy.start()
        return copy

    def small_end(n, copy):
        copy.wait()
        small_ref[...] = small_ref[...] + small_buf[n]

    running = small_start(0)
    weighted = grad * gain[...]
    centre = jnp.mean(source * weighted, axis=1, keepdims=True)
    total = grad_hidden[...] + inverse * weighted - source * (inverse * inverse * inverse * centre)
    out_ref[...] = total.astype(bf16)
    small_end(0, running)
    running = small_start(1)
    for k in range(half):
        arrive(diag_ref.at[k], 2, k)
        own_ref[k] = (dw[1, near[k]].astype(f32) + diag_ref[k].astype(f32)).astype(bf16)
        push(own_ref.at[k], second_ref.at[k], 1, k, y_peer)
        arrive(diag_ref.at[half + k], 2, half + k)
        own_ref[half + k] = (dw[0, over[half + k]].astype(f32) + diag_ref[half + k].astype(f32)).astype(bf16)
        push(own_ref.at[half + k], first_ref.at[half + k], 0, half + k, x_peer)
    small_end(1, running)
    running = small_start(2)
    backs = push_back(p, plane_peers, sums, back_ref, back_send, back_recv)
    for copy in sent:
        copy.wait_send()
    for k in range(planes):
        arrive(first_ref.at[k], 0, k)
        arrive(second_ref.at[k], 1, k)
        plane_ref[k] = (
            dw[0, near[k]].astype(f32) + first_ref[k].astype(f32) + second_ref[k].astype(f32)
        ).astype(bf16)
    small_end(2, running)
    cols = small_ref.shape[1] // 8
    part_ref[...] = small_ref[:, pl.ds(pl.multiple_of(p * cols, cols), cols)]
    for n, peer in enumerate(doubling[3:]):
        copy = remote(part_ref, part_buf.at[n], part_send.at[n], part_recv.at[n], peer)
        copy.start()
        copy.wait()
        part_ref[...] = part_ref[...] + part_buf[n]
    spread = []
    for j in range(1, 8):
        copy = remote(part_ref, parts_ref.at[p], parts_send.at[j], parts_recv.at[j], plane_peers[j])
        copy.start()
        spread.append(copy)
    parts_ref[p] = part_ref[...]
    settle_back(p, plane_peers, backs, back_ref, back_send, back_recv)
    for j in range(1, 8):
        spread[j - 1].wait_send()
        slot = parts_ref.at[p ^ j]
        remote(slot, slot, parts_send.at[j], parts_recv.at[j], plane_peers[1]).wait_recv()
    for q in range(8):
        router_ref[q * cols:(q + 1) * cols] = parts_ref[q, :experts].T
        gains_ref[:, q * cols:(q + 1) * cols] = parts_ref[q, experts:]


def last_kernel(
    plane, back_first, sums, query_ref, keyval_ref, wo_ref, gate_ref, up_ref, down_ref,
    back_ref, far_ref, far_send, far_recv, back_send, back_recv,
):
    d, t = lax.axis_index("dp"), lax.axis_index("tensor")
    planes = plane.shape[0]
    z, x = d // 2, d % 2
    z_peers = [{"dp": lax.rem(z + k, planes) * 2 + x, "tensor": t} for k in range(1, planes)]
    p, plane_peers = own_place(), plane_devices()
    greet((*plane_peers[1:], *z_peers))
    far = []
    for k, peer in enumerate(z_peers):
        copy = remote(plane.at[lax.rem(z + k + 1, planes)], far_ref.at[k], far_send.at[k], far_recv.at[k], peer)
        copy.start()
        far.append(copy)
    backs = push_back(p, plane_peers, sums, back_ref, back_send, back_recv)
    outs = (gate_ref, up_ref, down_ref)
    deep = back_first.shape[3]
    experts = gate_ref.shape[0] // deep

    def assemble(source, first, e, q):
        rows = pl.ds(q * (experts // 8) + first + e, deep, stride=experts)
        for which, out in enumerate(outs):
            out[rows, :] = source[e, q, which].astype(f32)

    for q in range(8):
        for e in range(2):
            assemble(back_first, 0, e, q)
    for e in range(2):
        backs[8 * e + 7].wait()
        assemble(back_ref, 2, e, p)
    for j in (1, 2, 4, 3, 5, 6, 7):
        for e in range(2):
            slot = back_ref.at[e, p ^ j]
            remote(slot, slot, back_send.at[e, j], back_recv.at[e, j], plane_peers[1]).wait_recv()
            assemble(back_ref, 2, e, p ^ j)
    for e in range(2):
        for n in range(7):
            backs[8 * e + n].wait_send()
    mine = plane[z].astype(f32)
    for k, copy in enumerate(far):
        copy.wait()
        mine += far_ref[k].astype(f32)
    qw, kvw = query_ref.shape[1], keyval_ref.shape[2]
    query_ref[...] = mine[:, :qw]
    keyval_ref[:, 0] = mine[:, qw:qw + kvw]
    keyval_ref[:, 1] = mine[:, qw + kvw:qw + 2 * kvw]
    wo_ref[...] = mine[:, qw + 2 * kvw:]


def shards(
    tokens,
    lengths,
    routes,
    gain_attn,
    w_query,
    w_keyvalue,
    w_out,
    gain_mixer,
    w_router,
    w_gate,
    w_up,
    w_down,
    out_grad,
):
    nd, nt = lax.axis_size("dp"), lax.axis_size("tensor")
    dp_id, t_id = lax.axis_index("dp"), lax.axis_index("tensor")
    rows, width = tokens.shape
    group_rows, top_count = routes.shape
    seq_count = lengths.shape[0]
    seq_len = group_rows // seq_count
    experts = w_router.shape[1]
    local = experts // 8
    planes = nd // 2
    deep = width // nd
    hidden = w_gate.shape[2] * nt
    capacity = (rows * top_count * 17 + experts * 16 - 1) // (experts * 16)
    cap = -(-capacity // 16) * 16
    core = t_id % 2
    z_groups = [[x + 2 * z for z in range(planes)] for x in range(2)]
    members = nd // 2
    with_place = [[a * 2 + side for a in range(members)] for side in range(2)]
    plane_groups = [
        [with_place[side][a] * nt + t for side in range(2) for t in range(nt)] for a in range(members)
    ]

    quarter = hidden // nt

    def for_plane(weights, first):
        parts = [
            jnp.transpose(w.reshape(deep, 8, local, quarter)[:, :, first:first + 2], (1, 2, 0, 3)) for w in weights
        ]
        return jnp.stack(parts, axis=2)

    w_send = for_plane((w_gate, w_up, w_down), 0)
    q_cols, kv_cols = w_query.shape[1], w_keyvalue.shape[2]
    cut = q_cols + 2 * kv_cols
    w_mine = jnp.concatenate([w_query, w_keyvalue[:, 0], w_keyvalue[:, 1], w_out], axis=1)
    pushes = 3 * planes
    hbm = pl.BlockSpec(memory_space=pl.ANY)
    dealt_shape = sds((8, 3, deep, quarter), bf16)
    dma = pltpu.SemaphoreType.DMA
    line_shape = sds((planes, deep, cut + q_cols), bf16)
    dealt_pair, line = pl.pallas_call(
        deal_kernel,
        out_shape=[sds((2,) + dealt_shape.shape, bf16), line_shape],
        in_specs=[hbm, VM], out_specs=[hbm, VM],
        scratch_shapes=[dma((2, 8)), dma((2, 8)), dma((planes,)), dma((planes,))],
        compiler_params=pltpu.CompilerParams(
            vmem_limit_bytes=VMEM_LIMIT, collective_id=1, has_side_effects=True
        ),
        cost_estimate=pl.CostEstimate(flops=10**6, bytes_accessed=20 * 2**20, transcendentals=0),
    )(w_send, w_mine)
    later = (0, 1)
    w_late = for_plane([after(w, line) for w in (w_gate, w_up, w_down)], 2)
    normed_rows, w_attn, ranks, router_t, dealt_third, dealt_last = pl.pallas_call(
        functools.partial(gather_kernel, later),
        out_shape=[
            sds((2 * rows, width), bf16), sds((2, nd, deep, cut + q_cols), bf16), sds((2, nt, 64, rows), bf16),
            sds((64, width), bf16),
        ]
        + [dealt_shape] * 2,
        in_specs=[SM] + [VM] * 5 + [hbm], out_specs=[VM] * 4 + [hbm] * 2,
        scratch_shapes=[
            pltpu.SemaphoreType.DMA((pushes,)), pltpu.SemaphoreType.DMA((2, nd)), pltpu.SemaphoreType.DMA((4,)),
            pltpu.SemaphoreType.DMA((len(later), 8)), pltpu.SemaphoreType.DMA((len(later), 8)),
        ],
        compiler_params=pltpu.CompilerParams(
            vmem_limit_bytes=VMEM_LIMIT, collective_id=0, has_side_effects=True
        ),
        cost_estimate=pl.CostEstimate(flops=10**7, bytes_accessed=100 * 2**20, transcendentals=0),
    )(lengths, tokens, gain_attn[None, :], routes.T, w_router, line, w_late)

    w_pair = gather_weights(dealt_pair, with_place)
    w_third = gather_weights(dealt_third, with_place)
    by_steps = members == local == 4
    w_last = dealt_last if by_steps else gather_weights(dealt_last, with_place)

    exponent = 2.0 * np.arange(HD // 2) / HD
    angles = np.arange(seq_len)[:, None] * np.exp(-math.log(rope_base) * exponent)[None, :]
    cosine, sine = np.cos(angles).astype(np.float32), np.sin(angles).astype(np.float32)
    cos_table = jnp.asarray(np.concatenate([cosine] * 4, axis=1))
    sin_table = jnp.asarray(np.concatenate([-sine, sine] * 2, axis=1))

    out_late = after(out_grad, w_attn)
    out_y, out_x = hop_y(out_late), hop_x(out_late)
    q_width, k_width = 2 * q_cols, 2 * kv_cols
    heads = q_width // HD
    q, k, v, ctx, lse, keep, send = call(
        attend_kernel,
        [
            sds((seq_len, q_width), bf16), sds((seq_len, k_width), bf16), sds((seq_len, k_width), bf16),
            sds((seq_len, q_width), bf16), sds((heads, seq_len), f32),
            sds((rows, width), bf16), sds((rows, width), bf16),
        ],
        12 * 10**9, 16 * 2**20,
        in_specs=[SM] + [VM] * 4, out_specs=[VM] * 7,
    )(lengths, normed_rows, w_attn, cos_table, sin_table)

    def remote_call(kernel, number, out_shape, flops, nbytes, **kw):
        return pl.pallas_call(
            kernel, out_shape=out_shape,
            compiler_params=pltpu.CompilerParams(
                vmem_limit_bytes=VMEM_LIMIT, collective_id=number, has_side_effects=True
            ),
            cost_estimate=pl.CostEstimate(flops=flops, bytes_accessed=nbytes, transcendentals=0),
            **kw,
        )

    slots_shape = (local, 8, cap, width)
    hidden_own, normed_mix, inverse_mix, gates_in, rows_in, grads_in, *moving = remote_call(
        functools.partial(mix_kernel, local, cap, int(by_steps)), 2,
        [
            sds((rows, width), f32), sds((rows, width), bf16), sds((rows, 1), f32),
            sds((local, 8, cap, 1), f32), sds(slots_shape, bf16), sds(slots_shape, bf16),
        ] + [dealt_shape] * (2 * by_steps),
        10**10, 100 * 2**20,
        in_specs=[SM] + [VM] * 9 + [hbm] * by_steps, out_specs=[VM] * 4 + [hbm] * (2 + 2 * by_steps),
        scratch_shapes=[
            pltpu.VMEM((8, rows, width), bf16), pltpu.VMEM((8, rows, width), bf16), pltpu.VMEM((rows, width), bf16),
            pltpu.VMEM((2, local, cap, width), bf16), pltpu.VMEM((64, rows), f32), pltpu.VMEM((64, rows), f32),
            dma((2, 9)), dma((2, 9)), dma((2,)), dma((2,)), dma((4,)),
        ],
    )(
        lengths, tokens, keep, send, gain_mixer[None, :], out_grad, out_y, out_x, ranks, router_t,
        *([dealt_last] if by_steps else []),
    )
    ys, dxs, dw_pairs = [], [], []
    arrived = (w_last, *moving)
    pair_shape = sds((members, 2, 8, 3, deep, quarter), bf16)
    before = []
    for e in range(local):
        step = e + 2 if by_steps and e + 2 < members else 0
        sources = ((w_pair,), (w_pair,), (w_third,), arrived)[e]
        inputs = [after(rows_in, *before), grads_in, gates_in, *sources, *(moving if step else ())]
        aliases = {}
        if e % 2:
            aliases = {len(inputs): 2}
            inputs.append(dw_pairs.pop())
        y, dx, dw, *moved = pl.pallas_call(
            functools.partial(expert_kernel, e, local, len(sources), step, len(sources) > 1),
            out_shape=[
                sds((8, cap, width), bf16), sds((8, cap, width + LANES), bf16), pair_shape,
            ] + [dealt_shape] * (2 if step else 0),
            in_specs=[hbm] * len(inputs),
            out_specs=[hbm] * (5 if step else 3),
            scratch_shapes=[
                pltpu.VMEM((8, cap, width), bf16), pltpu.VMEM((8, cap, width), bf16), pltpu.VMEM((8, cap, 1), f32),
                pltpu.VMEM((members, 8, 3, deep, quarter), bf16),
                pltpu.VMEM((8, cap, width), bf16), pltpu.VMEM((8, cap, width + LANES), bf16),
                pltpu.VMEM((members, 8, 3, deep, quarter), bf16),
                dma((3,)), dma((len(sources),)), dma((5,)), dma((4,)),
            ],
            input_output_aliases=aliases,
            compiler_params=pltpu.CompilerParams(
                vmem_limit_bytes=VMEM_LIMIT, **(dict(collective_id=3 + step, has_side_effects=True) if step else {})
            ),
            cost_estimate=pl.CostEstimate(flops=10**10, bytes_accessed=20 * 2**20, transcendentals=0),
        )(*inputs)
        if step:
            moving = tuple(moved)
            arrived += moving
        ys.append(y)
        dxs.append(dx)
        dw_pairs.append(dw)
        before = [y]

    wide = width + LANES
    grad_hidden, grad_branch, router_grad, gain_mix_grad, y_totals = remote_call(
        functools.partial(return_kernel, local, cap), 3,
        [
            sds((rows, width), f32), sds((2 * rows, width), bf16), sds((experts, width), f32), sds((1, width), f32),
            sds((4, rows, width), bf16),
        ],
        10**10, 100 * 2**20,
        in_specs=[hbm] * (2 * local) + [SM] + [VM] * 7, out_specs=[VM] * 5,
        scratch_shapes=[
            pltpu.VMEM((3, local * cap, wide), bf16),
            pltpu.VMEM((4, rows, wide), bf16), pltpu.VMEM((4, rows, wide), bf16), pltpu.VMEM((4, rows, wide), bf16),
            pltpu.VMEM((2, rows // 2, wide), bf16), pltpu.VMEM((2, rows, wide), bf16),
            pltpu.VMEM((4, rows, width), bf16), pltpu.VMEM((4, rows, width), bf16), pltpu.VMEM((64, rows), f32),
            dma((3, local)), dma((10,)), dma((10,)), dma((4,)), dma((4,)), dma((2,)),
        ],
    )(
        *dxs, *ys, lengths, ranks, normed_mix, hidden_own, inverse_mix, out_grad, w_router, gain_mixer[None, :],
    )
    chip_groups = [
        [with_place[side][a] * nt + y * 2 + c for side in range(2) for y in range(2)]
        for a in range(members) for c in range(2)
    ]
    y_terms = lax.all_to_all(y_totals, BOTH, 0, 0, tiled=True, axis_index_groups=chip_groups)
    mixed = (hidden_own + jnp.sum(y_terms.astype(f32), axis=0)).astype(bf16)

    dw_attn, keep_back, send_back = call(
        attend_back_kernel,
        [
            sds((2, nd, deep, cut + q_cols), bf16), sds((rows, width), bf16), sds((rows, width), bf16),
        ],
        25 * 10**9, 24 * 2**20,
        in_specs=[SM] + [VM] * 10, out_specs=[VM] * 3,
        scratch_shapes=[
            pltpu.VMEM((seq_len, q_width), bf16), pltpu.VMEM((seq_len, 2 * cut), bf16),
            pltpu.VMEM((seq_len, LANES), f32), pltpu.VMEM((seq_len, LANES), f32),
        ],
    )(
        lengths, normed_rows, grad_branch, w_attn, cos_table, sin_table,
        q, k, v, ctx, lse,
    )
    per_dp = (deep, cut + q_cols)
    sums = [
        lax.psum_scatter(dw, "dp", scatter_dimension=0, axis_index_groups=with_place) for dw in dw_pairs
    ]
    back_shape = sds((2, 8, 3, deep, quarter), bf16)
    doublings = (nd - 1).bit_length() - 1
    small_rows, part = experts + 8, width // 8
    grad_tokens, grad_router, gains, plane_grad, back_first = remote_call(
        tail_kernel, 8,
        [
            sds((rows, width), bf16), sds((width, experts), f32), sds((8, width), f32),
            sds((planes,) + per_dp, bf16), back_shape,
        ],
        10**8, 30 * 2**20,
        in_specs=[VM] * 8 + [hbm], out_specs=[VM] * 4 + [hbm],
        scratch_shapes=[pltpu.VMEM((rows, width), bf16)]
        + [pltpu.VMEM((planes,) + per_dp, bf16)] * 4
        + [
            pltpu.VMEM((small_rows, width), f32), pltpu.VMEM((3, small_rows, width), f32),
            pltpu.VMEM((small_rows, part), f32), pltpu.VMEM((doublings, small_rows, part), f32),
            pltpu.VMEM((8, small_rows, part), f32),
            dma((2,)), dma((3, planes)), dma((3, planes)), dma((3,)), dma((3,)), dma((2, 8)), dma((2, 8)),
            dma((doublings,)), dma((doublings,)), dma((8,)), dma((8,)),
        ],
    )(
        after(tokens, y_terms), keep_back, send_back, grad_hidden, gain_attn[None, :], router_grad, gain_mix_grad,
        dw_attn, sums[0],
    )
    expert_grad = sds((deep * experts, quarter), f32)
    grad_query, grad_keyval, grad_out, *expert_grads = remote_call(
        last_kernel, 9,
        [
            sds((deep, q_cols), f32), sds((deep, 2, kv_cols), f32), sds((deep, q_cols), f32),
            expert_grad, expert_grad, expert_grad,
        ],
        10**8, 30 * 2**20,
        in_specs=[VM] * 2 + [hbm], out_specs=[VM] * 6,
        scratch_shapes=[
            pltpu.VMEM((2, 8, 3, deep, quarter), bf16), pltpu.VMEM((planes - 1,) + per_dp, bf16),
            dma((planes - 1,)), dma((planes - 1,)), dma((2, 8)), dma((2, 8)),
        ],
    )(plane_grad, back_first, sums[1])
    grad_gate, grad_up, grad_down = (g.reshape(deep, experts, quarter) for g in expert_grads)

    return (
        mixed,
        grad_tokens,
        gains[1],
        grad_query,
        grad_keyval,
        grad_out,
        gains[0],
        grad_router,
        grad_gate,
        grad_up,
        grad_down,
    )


def solution(mesh):
    placed = (
        P(("dp", "tensor"), None),
        P("dp"),
        P("dp", None),
        P(),
        P("dp", "tensor"),
        P("dp", None, "tensor"),
        P("dp", "tensor"),
        P(),
        P(),
        P("dp", None, "tensor"),
        P("dp", None, "tensor"),
        P("dp", None, "tensor"),
        P(("dp", "tensor"), None),
    )
    return jax.shard_map(
        shards,
        mesh=mesh,
        in_specs=placed,
        out_specs=(
            P(("dp", "tensor"), None),
            P(("dp", "tensor"), None),
            P(),
            P("dp", "tensor"),
            P("dp", None, "tensor"),
            P("dp", "tensor"),
            P(),
            P(),
            P("dp", None, "tensor"),
            P("dp", None, "tensor"),
            P("dp", None, "tensor"),
        ),
        check_vma=False,
    )
```
